32 devices in a mesh: tp: 2 (over core), grp: 8 (over z, y), rep: 2 (over x).
Axes of the slice: x: 2, y: 2, z: 4, core: 2. Of those that a mesh axis runs over, the one named last changes fastest.
Arguments:
- tokens: bfloat16 [2048, 4096], P(('rep', 'tp', 'grp')), parts along dimension 0, may hold values from -6 to 6
- qkv_weight: bfloat16 [4096, 5120], P(None, ('tp', 'grp')), may hold values from -0.09375 to 0.09375
- qkv_bias: bfloat16 [5120], replicated, may hold values from -3 to 3
- cache: bfloat16 [128, 1024, 1024], P(('rep', 'tp', 'grp')), parts along dimension 0, may hold values from -80 to 80
- lengths: int32 [128], P('rep'), parts along dimension 0, may hold values from 128 to 1024, as said below
- slot_stream: int32 [128], P('rep'), parts along dimension 0, may hold values from 0 to 63, each once
Outputs:
- attended: bfloat16 [2048, 4096], P(('rep', 'tp', 'grp')), parts along dimension 0
The draws below stay inside these ranges and needn't reach their ends.
There are 2 independent parts, one for each index of `rep`. The reference program is written for one: setup_inputs(seed, part) draws one part's arguments, and reference() takes and returns one part's arrays. A program takes and returns all parts, laid end to end along the dimension named above; an argument that names none is the same for every part. Nothing has to cross between parts.
Inputs may be any that keep to these rules, and one draw needn't show every extreme that they name: `lengths`: cache length of each stream; some stream has exactly 1024 and some exactly 128. `slot_stream`: each stream appears in exactly one slot.
All inputs are finite; a program needn't handle non-finite values.
Results may differ from the reference program's by a relative error of at most 0.004.
The reference program's roundings to bfloat16 on the way count: a program that leaves them out, or rounds other values in their place, can miss the bound.
Values may be sent and summed in bfloat16 or wider, within the bound.
A program may use at most 128 MiB of HBM per device.

```python
import jax
import jax.numpy as jnp
from jax import lax

D = 4096
HD = 128
HQ = 32
KVH = 4
STRETCH = 16
CAP = 1024
GROUP = 8
STREAMS = 64
ROWS = 1024
QKV_COLS = 5120


def draw_cache(key, part):
    key_base = jax.random.fold_in(key, 11)
    column = jnp.arange(2 * KVH * HD, dtype=jnp.int32)
    base_draw = jax.random.normal(key_base, (STREAMS, CAP, 2 * KVH * HD), jnp.float32)
    boost_factor = jnp.ones((STREAMS, CAP, 1), jnp.float32)
    column_scale = jnp.where(column[None, None, :] < KVH * HD, 3.0 * boost_factor, 1.0)
    return (base_draw * column_scale).astype(jnp.bfloat16)


def draw_lengths(key, part):
    key_values = jax.random.fold_in(key, 21)
    key_longest = jax.random.fold_in(key, 22)
    values = jax.random.randint(key_values, (STREAMS,), CAP // 8, CAP + 1)
    longest = jax.random.randint(key_longest, (), 0, STREAMS)
    shortest = (longest + 1) % STREAMS
    values = values.at[longest].set(CAP)
    values = values.at[shortest].set(CAP // 8)
    return values.astype(jnp.int32)


def block_levels(own_key, dims, pieces, smallest, high):
    level = 1.0
    for axis_at, parts in pieces:
        heights = jax.random.uniform(jax.random.fold_in(jax.random.fold_in(own_key, 6), axis_at), (parts,), jnp.float32, smallest / len(pieces), high / len(pieces))
        level = level * jnp.repeat(jnp.exp(heights), dims[axis_at] // parts).reshape((-1,) + (1,) * (len(dims) - 1 - axis_at))
    return level


def bell_draw(rng, dims, scale, reach, split=(), held_as=jnp.bfloat16):
    gain = block_levels(rng, dims, split, -0.22, 0.18) if split else 1.0
    drawn = jax.random.normal(rng, dims, jnp.float32) * scale * gain
    return jnp.minimum(jnp.maximum(drawn, -reach), reach).astype(held_as)


def setup_inputs(seed: int = 0, part: int = 0) -> dict:
    key_of = jax.random.split(jax.random.key(seed), 7)
    own_keys = jax.random.split(jax.random.fold_in(key_of[6], part), 7)
    return {
        "tokens": bell_draw(own_keys[0], (ROWS, D), 1.0, 6.0, ((0, 16),)),
        "qkv_weight": bell_draw(key_of[1], (D, QKV_COLS), D ** -0.5, 0.09375, ((1, 16),)),
        "qkv_bias": bell_draw(key_of[2], (QKV_COLS,), 0.5, 3.0),
        "cache": draw_cache(jax.random.fold_in(jax.random.fold_in(key_of[6], part), 71), part),
        "lengths": draw_lengths(jax.random.fold_in(jax.random.fold_in(key_of[6], part), 71), part),
        "slot_stream": jax.random.permutation(own_keys[5], STREAMS).astype(jnp.int32),
    }


ROPE_THETA = 1000000.0


def rotate(vectors, positions):
    half_width = vectors.shape[-1] // 2
    frequency = ROPE_THETA ** (-(jnp.arange(half_width, dtype=jnp.float32) * 2.0) / vectors.shape[-1])
    angles = positions.astype(jnp.float32)[:, None] * frequency[None, :]
    cosine = jnp.cos(angles)[:, None, :]
    sine_part = jnp.sin(angles)[:, None, :]
    front_half = vectors[..., :half_width]
    back_half = vectors[..., half_width:]
    return jnp.concatenate([front_half * cosine - back_half * sine_part, back_half * cosine + front_half * sine_part], axis=-1)


def rounded(values):
    return lax.optimization_barrier(values.astype(jnp.bfloat16)).astype(jnp.float32)


def reference(tokens, qkv_weight, qkv_bias, cache, lengths, slot_stream):
    query_width = HQ * HD
    kv_width = KVH * HD
    projected_qkv = (jnp.dot(tokens, qkv_weight, preferred_element_type=jnp.float32) + qkv_bias.astype(jnp.float32)[None, :]).astype(jnp.bfloat16)
    projected_qkv = projected_qkv.reshape(STREAMS, STRETCH, QKV_COLS)
    token_index = jnp.arange(STRETCH, dtype=jnp.int32)
    key_index = jnp.arange(CAP + STRETCH, dtype=jnp.int32)
    score_scale = HD ** -0.5

    def one_slot(inputs):
        slot_cache, token_slab, stream = inputs
        length = lax.dynamic_index_in_dim(lengths, stream, 0, keepdims=False)
        token_block = token_slab.astype(jnp.float32)
        positions = length + token_index
        queries = rounded(rotate(token_block[:, :query_width].reshape(STRETCH, HQ, HD), positions)).reshape(STRETCH, KVH, GROUP, HD)
        new_keys = rounded(rotate(token_block[:, query_width:query_width + kv_width].reshape(STRETCH, KVH, HD), positions))
        new_values = token_block[:, query_width + kv_width:].reshape(STRETCH, KVH, HD)
        cache_float = slot_cache.astype(jnp.float32)
        key_all = jnp.concatenate([cache_float[:, :kv_width].reshape(CAP, KVH, HD), new_keys], axis=0)
        value_all = jnp.concatenate([cache_float[:, kv_width:].reshape(CAP, KVH, HD), new_values], axis=0)
        scores = jnp.einsum("ckgd,jkd->ckgj", queries, key_all, precision=lax.Precision.HIGHEST) * score_scale
        allowed = jnp.where(key_index[None, :] < CAP, key_index[None, :] < length, key_index[None, :] - CAP <= token_index[:, None])
        scores = jnp.where(allowed[:, None, None, :], scores, -jnp.inf)
        row_max = jnp.max(scores, axis=-1, keepdims=True)
        exponent = jnp.exp(scores - row_max)
        row_total = jnp.sum(exponent, axis=-1, keepdims=True)
        result = jnp.einsum("ckgj,jkd->ckgd", rounded(exponent), value_all, precision=lax.Precision.HIGHEST) / row_total
        return result.reshape(STRETCH, HQ * HD).astype(jnp.bfloat16)

    attended = lax.map(one_slot, (cache, projected_qkv, slot_stream))
    return attended.reshape(ROWS, HQ * HD)
```

```python
import functools

import jax
import jax.numpy as jnp
from jax import lax
from jax.experimental import pallas as pl
from jax.experimental.pallas import tpu as pltpu
from jax.sharding import PartitionSpec as P

HD = 128
HQ = 32
KVH = 4
STRETCH = 16
CAP = 1024
GROUP = 8


ROPE_THETA = 1000000.0


def rotate(vectors, positions):
    half_width = vectors.shape[-1] // 2
    frequency = ROPE_THETA ** (
        -(jnp.arange(half_width, dtype=jnp.float32) * 2.0) / vectors.shape[-1]
    )
    angles = positions.astype(jnp.float32)[:, None] * frequency[None, :]
    cosine = jnp.cos(angles)[:, None, :]
    sine_part = jnp.sin(angles)[:, None, :]
    front_half = vectors[..., :half_width]
    back_half = vectors[..., half_width:]
    return jnp.concatenate(
        [front_half * cosine - back_half * sine_part, back_half * cosine + front_half * sine_part],
        axis=-1,
    )


def attend(token_block, slot_cache, length):
    query_width = HQ * HD
    kv_width = KVH * HD
    positions = length + jnp.arange(STRETCH, dtype=jnp.int32)
    queries = rotate(
        token_block[:, :query_width].astype(jnp.float32).reshape(STRETCH, HQ, HD), positions
    ).astype(jnp.bfloat16)
    new_keys = rotate(
        token_block[:, query_width : query_width + kv_width]
        .astype(jnp.float32)
        .reshape(STRETCH, KVH, HD),
        positions,
    ).astype(jnp.bfloat16)
    new_values = token_block[:, query_width + kv_width :].reshape(STRETCH, KVH, HD)
    grouped = (
        queries.reshape(STRETCH, KVH, GROUP, HD)
        .transpose(1, 0, 2, 3)
        .reshape(KVH, STRETCH * GROUP, HD)
    )
    score_scale = HD ** (-0.5)
    query_token = jnp.arange(STRETCH * GROUP, dtype=jnp.int32) // GROUP
    scores = (
        jnp.einsum("krd,jkd->krj", grouped, new_keys, preferred_element_type=jnp.float32)
        * score_scale
    )
    causal = jnp.arange(STRETCH, dtype=jnp.int32)[None, :] <= query_token[:, None]
    scores = jnp.where(causal[None], scores, -jnp.inf)
    row_max = jnp.max(scores, axis=-1)
    exponent = jnp.exp(scores - row_max[..., None])
    row_total = jnp.sum(exponent, axis=-1)
    running = jnp.einsum(
        "krj,jkd->krd",
        exponent.astype(jnp.bfloat16),
        new_values,
        preferred_element_type=jnp.float32,
    )
    key_span = min(CAP, 256)
    key_part = slot_cache[:, :kv_width]
    value_part = slot_cache[:, kv_width:]

    def visit(block_index, running_state):
        old_max, old_total, old_sum = running_state
        offset = block_index * key_span
        key_block = lax.dynamic_slice_in_dim(key_part, offset, key_span, 0).reshape(
            key_span, KVH, HD
        )
        value_block = lax.dynamic_slice_in_dim(value_part, offset, key_span, 0).reshape(
            key_span, KVH, HD
        )
        block_scores = (
            jnp.einsum("krd,jkd->krj", grouped, key_block, preferred_element_type=jnp.float32)
            * score_scale
        )
        in_cache = offset + jnp.arange(key_span, dtype=jnp.int32) < length
        block_scores = jnp.where(in_cache[None, None, :], block_scores, -jnp.inf)
        new_max = jnp.maximum(old_max, jnp.max(block_scores, axis=-1))
        rescale = jnp.exp(old_max - new_max)
        block_exp = jnp.exp(block_scores - new_max[..., None])
        new_total = old_total * rescale + jnp.sum(block_exp, axis=-1)
        new_sum = old_sum * rescale[..., None] + jnp.einsum(
            "krj,jkd->krd",
            block_exp.astype(jnp.bfloat16),
            value_block,
            preferred_element_type=jnp.float32,
        )
        return (new_max, new_total, new_sum)

    block_count = CAP // key_span
    row_max, row_total, running = lax.fori_loop(
        0, block_count, visit, (row_max, row_total, running)
    )
    result = running / row_total[..., None]
    return (
        result.reshape(KVH, STRETCH, GROUP, HD)
        .transpose(1, 0, 2, 3)
        .reshape(STRETCH, HQ * HD)
        .astype(jnp.bfloat16)
    )


def on_device(tokens, qkv_weight, qkv_bias, cache, lengths, slot_stream):
    my_index = lax.axis_index(("tp", "grp"))
    grp_index = lax.axis_index("grp")
    tp_count = lax.axis_size("tp")
    grp_count = lax.axis_size("grp")
    per_device = cache.shape[0]
    local_rows = per_device * STRETCH
    shard_cols = qkv_weight.shape[1]
    weight_cols = lax.all_gather(qkv_weight, "tp", axis=1, tiled=True)
    bias_table = qkv_bias.reshape(tp_count, grp_count, shard_cols)
    bias_cols = (
        lax.dynamic_index_in_dim(bias_table, grp_index, 1, keepdims=False)
        .reshape(-1)
        .astype(jnp.float32)
    )
    partial_cols = jnp.dot(
        lax.all_gather(tokens, "grp", axis=0, tiled=True),
        weight_cols,
        preferred_element_type=jnp.float32,
    )
    rounded_cols = (partial_cols + bias_cols[None, :]).astype(jnp.bfloat16)
    received = lax.all_to_all(rounded_cols, "grp", split_axis=0, concat_axis=1, tiled=True)
    projected_qkv = (
        received.reshape(local_rows, grp_count, tp_count, shard_cols)
        .transpose(0, 2, 1, 3)
        .reshape(local_rows, -1)
    )
    my_slots = my_index * per_device + jnp.arange(per_device, dtype=jnp.int32)
    my_lengths = jnp.take(lengths, jnp.take(slot_stream, my_slots))
    attended = jnp.concatenate(
        [
            attend(
                projected_qkv[slot_index * STRETCH : (slot_index + 1) * STRETCH],
                cache[slot_index],
                my_lengths[slot_index],
            )
            for slot_index in range(per_device)
        ],
        axis=0,
    )
    return attended


MESH = pl.DeviceIdType.MESH
LOG2E = 1.4426950408889634


def fused_kernel(
    n,
    groups,
    cols,
    tokens_ref,
    weight_ref,
    bias_ref,
    cache_ref,
    lengths_ref,
    streams_ref,
    freq_ref,
    out_ref,
    tok,
    weights,
    slots,
    acc,
    outgoing,
    incoming,
    cos_table,
    sin_table,
    tok_local,
    tok_send,
    tok_recv,
    part_send,
    part_recv,
    weight_sems,
    cache_sems,
):
    tp = lax.axis_index("tp")
    me = lax.axis_index("grp")
    chain = groups // 2
    depth = me // 2
    side = me % 2
    across = depth * 2 + 1 - side
    wide = acc.shape[1]
    first_slot = (tp * groups + me) * n

    def local_tokens(c):
        return pltpu.make_async_copy(
            tokens_ref.at[pl.ds(pl.multiple_of(c * STRETCH, STRETCH), STRETCH)],
            tok.at[c, me],
            tok_local.at[c],
        )

    def cache_copy(c):
        return pltpu.make_async_copy(cache_ref.at[c], slots.at[c], cache_sems.at[c])

    def tok_copy(c, block, direction, target):
        return pltpu.make_async_remote_copy(
            src_ref=tok.at[c, block],
            dst_ref=tok.at[c, block],
            send_sem=tok_send.at[c, block, direction],
            recv_sem=tok_recv.at[c, block],
            device_id={"grp": target},
            device_id_type=MESH,
        )

    def part_copy(c, peer):
        return pltpu.make_async_remote_copy(
            src_ref=outgoing.at[c, peer],
            dst_ref=incoming.at[c, me],
            send_sem=part_send.at[c, peer],
            recv_sem=part_recv.at[c, me],
            device_id={"grp": peer},
            device_id_type=MESH,
        )

    def part_arrival(c, peer):
        return pltpu.make_async_remote_copy(
            src_ref=outgoing.at[c, peer],
            dst_ref=incoming.at[c, peer],
            send_sem=part_send.at[c, peer],
            recv_sem=part_recv.at[c, peer],
            device_id={"grp": peer},
            device_id_type=MESH,
        )

    weight_own = pltpu.make_async_copy(weight_ref, weights.at[tp], weight_sems.at[0])
    weight_swap = pltpu.make_async_remote_copy(
        src_ref=weight_ref,
        dst_ref=weights.at[tp],
        send_sem=weight_sems.at[1],
        recv_sem=weight_sems.at[2],
        device_id={"tp": 1 - tp},
        device_id_type=MESH,
    )

    for c in range(n):
        local_tokens(c).start()

    barrier = pltpu.get_barrier_semaphore()
    pl.semaphore_signal(barrier, inc=1, device_id={"tp": 1 - tp}, device_id_type=MESH)
    for d in range(1, groups):
        pl.semaphore_signal(
            barrier, inc=1, device_id={"grp": lax.rem(me + d, groups)}, device_id_type=MESH
        )
    pl.semaphore_wait(barrier, groups)

    def send_own(c):
        local_tokens(c).wait()
        tok_copy(c, me, 2, across).start()

        @pl.when(depth + 1 < chain)
        def _():
            tok_copy(c, me, 0, me + 2).start()

        @pl.when(depth >= 1)
        def _():
            tok_copy(c, me, 1, me - 2).start()

    def forward(c, s):
        @pl.when(depth >= s)
        def _():
            block = me - 2 * s
            tok_copy(c, block, 2, across).wait_recv()
            tok_copy(c, block, 2, across).start()

            @pl.when(depth + 1 < chain)
            def _():
                tok_copy(c, block, 0, me + 2).start()

        @pl.when(depth + s < chain)
        def _():
            block = me + 2 * s
            tok_copy(c, block, 2, across).wait_recv()
            tok_copy(c, block, 2, across).start()

            @pl.when(depth >= 1)
            def _():
                tok_copy(c, block, 1, me - 2).start()

    def finish_sends(c):
        for level in range(chain):
            block = level * 2 + side
            tok_copy(c, block, 2, across).wait_send()

            @pl.when((level <= depth) & (depth + 1 < chain))
            def _():
                tok_copy(c, block, 0, me + 2).wait_send()

            @pl.when((level >= depth) & (depth >= 1))
            def _():
                tok_copy(c, block, 1, me - 2).wait_send()

        for d in range(1, groups):
            part_copy(c, lax.rem(me + d, groups)).wait_send()

    def project(c):
        for level in range(chain):
            tok_copy(c, level * 2 + 1 - side, 2, across).wait_recv()
        rows = tok[c].reshape(groups * STRETCH, tok.shape[3])
        for t in range(2):
            acc[:, :cols] = (
                jnp.dot(rows, weights[t], preferred_element_type=jnp.float32)
                + bias_ref[t * groups + me]
            )
            moved = pltpu.roll(acc[...], (wide - cols) * side, 1)
            outgoing[c, :, t] = moved.astype(jnp.bfloat16).reshape(groups, STRETCH, wide)
        for d in range(1, groups):
            part_copy(c, lax.rem(me + d, groups)).start()
        incoming[c, me] = outgoing[c, me]

    lane = lax.broadcasted_iota(jnp.int32, (STRETCH, HD), 1)
    rows_all = STRETCH * GROUP
    pair_heads = 2 * cols // HD
    half = groups // 2 * pair_heads

    def attention(c):
        for d in range(1, groups):
            part_arrival(c, lax.rem(me + d, groups)).wait_recv()
        cache_copy(c).wait()
        length = lengths_ref[streams_ref[first_slot + c]]
        cosine = cos_table[c]
        sine = sin_table[c]
        key_index = lax.broadcasted_iota(jnp.int32, (1, CAP), 1)
        in_cache = key_index < length
        new_index = lax.broadcasted_iota(jnp.int32, (rows_all, STRETCH), 1)
        new_token = lax.broadcasted_iota(jnp.int32, (rows_all, STRETCH), 0) % STRETCH
        causal = new_index <= new_token
        factor = HD ** (-0.5) * LOG2E
        middle = pair_heads // 2

        def head(i):
            t, rest = divmod(i, half)
            pair, k = divmod(rest, pair_heads)
            if k < middle:
                return incoming[c, 2 * pair, t, :, k * HD : (k + 1) * HD]
            right = incoming[c, 2 * pair + 1, t, :, (k - middle) * HD : (k - middle + 1) * HD]
            if k > middle:
                return right
            left = incoming[c, 2 * pair, t, :, k * HD : (k + 1) * HD]
            return jnp.where(
                lane < HD // 2, left.astype(jnp.float32), right.astype(jnp.float32)
            ).astype(jnp.bfloat16)

        def rotated(i):
            u = head(i).astype(jnp.float32)
            return (u * cosine + pltpu.roll(u, HD // 2, 1) * sine).astype(jnp.bfloat16)

        nt = (((1,), (1,)), ((), ()))
        for k in range(KVH):
            queries = jnp.concatenate([rotated(k * GROUP + g) for g in range(GROUP)], axis=0)
            new_keys = rotated(HQ + k)
            new_values = head(HQ + KVH + k)
            keys = slots[c, :, k * HD : (k + 1) * HD]
            values = slots[c, :, (KVH + k) * HD : (KVH + k + 1) * HD]
            scores = lax.dot_general(queries, keys, nt, preferred_element_type=jnp.float32)
            scores = jnp.where(in_cache, scores, -jnp.inf)
            new_scores = lax.dot_general(queries, new_keys, nt, preferred_element_type=jnp.float32)
            new_scores = jnp.where(causal, new_scores, -jnp.inf)
            top = jnp.maximum(
                jnp.max(scores, axis=-1, keepdims=True), jnp.max(new_scores, axis=-1, keepdims=True)
            )
            probs = jnp.exp2((scores - top) * factor)
            new_probs = jnp.exp2((new_scores - top) * factor)
            total = jnp.sum(probs, axis=-1, keepdims=True) + jnp.sum(
                new_probs, axis=-1, keepdims=True
            )
            summed = jnp.dot(
                probs.astype(jnp.bfloat16), values, preferred_element_type=jnp.float32
            ) + jnp.dot(
                new_probs.astype(jnp.bfloat16), new_values, preferred_element_type=jnp.float32
            )
            result = (summed / total).astype(jnp.bfloat16)
            for g in range(GROUP):
                h = k * GROUP + g
                out_ref[
                    pl.ds(pl.multiple_of(c * STRETCH, STRETCH), STRETCH), h * HD : (h + 1) * HD
                ] = result[g * STRETCH : (g + 1) * STRETCH]

    for c in range(min(2, n)):
        send_own(c)
    weight_own.start()
    weight_swap.start()
    for c in range(n):
        cache_copy(c).start()

    acc[...] = jnp.zeros_like(acc)
    sign = jnp.where(lane < HD // 2, -1.0, 1.0)
    token = lax.broadcasted_iota(jnp.int32, (STRETCH, HD), 0)
    for c in range(n):
        length = lengths_ref[streams_ref[first_slot + c]]
        angles = (length + token).astype(jnp.float32) * freq_ref[...]
        cos_table[c] = jnp.cos(angles)
        sin_table[c] = jnp.sin(angles) * sign

    @pl.loop(0, n + 2)
    def _(i):
        @pl.when(i < n)
        def _():
            forward(i, 1)

        @pl.when(i == 1)
        def _():
            weight_own.wait()
            weight_swap.wait()

        @pl.when((i >= 1) & (i < n + 1))
        def _():
            project(i - 1)

        @pl.when(i < n)
        def _():
            for s in range(2, chain):
                forward(i, s)

        @pl.when(i + 2 < n)
        def _():
            send_own(i + 2)

        @pl.when(i >= 2)
        def _():
            attention(i - 2)

    @pl.loop(0, n)
    def _(c):
        finish_sends(c)


def fused(tokens, qkv_weight, qkv_bias, cache, lengths, slot_stream):
    groups = lax.axis_size("grp")
    n = cache.shape[0]
    width, cols = qkv_weight.shape
    wide = cols + HD // 2
    bias = qkv_bias.astype(jnp.float32).reshape(2 * groups, 1, cols)
    frequency = ROPE_THETA ** (-(jnp.arange(HD // 2, dtype=jnp.float32) * 2.0) / HD)
    frequency = jnp.concatenate([frequency, frequency])[None, :]
    anywhere = pl.BlockSpec(memory_space=pl.ANY)
    vmem = pl.BlockSpec(memory_space=pltpu.VMEM)
    smem = pl.BlockSpec(memory_space=pltpu.SMEM)
    dma = pltpu.SemaphoreType.DMA
    rows = groups * STRETCH
    attention_ops = 4 * n * KVH * STRETCH * GROUP * CAP * HD
    return pl.pallas_call(
        functools.partial(fused_kernel, n, groups, cols),
        out_shape=jax.ShapeDtypeStruct((n * STRETCH, HQ * HD), jnp.bfloat16),
        in_specs=[anywhere, anywhere, vmem, anywhere, smem, smem, vmem],
        out_specs=vmem,
        scratch_shapes=[
            pltpu.VMEM((n, groups, STRETCH, width), jnp.bfloat16),
            pltpu.VMEM((2, width, cols), jnp.bfloat16),
            pltpu.VMEM(cache.shape, jnp.bfloat16),
            pltpu.VMEM((rows, wide), jnp.float32),
            pltpu.VMEM((n, groups, 2, STRETCH, wide), jnp.bfloat16),
            pltpu.VMEM((n, groups, 2, STRETCH, wide), jnp.bfloat16),
            pltpu.VMEM((n, STRETCH, HD), jnp.float32),
            pltpu.VMEM((n, STRETCH, HD), jnp.float32),
            dma((n,)),
            dma((n, groups, 3)),
            dma((n, groups)),
            dma((n, groups)),
            dma((n, groups)),
            dma((3,)),
            dma((n,)),
        ],
        compiler_params=pltpu.CompilerParams(
            collective_id=0, has_side_effects=True, vmem_limit_bytes=56 * 2**20
        ),
        cost_estimate=pl.CostEstimate(
            flops=4 * n * rows * width * cols + attention_ops,
            bytes_accessed=2 * (cache.size + 2 * qkv_weight.size),
            transcendentals=n * KVH * STRETCH * GROUP * CAP,
        ),
    )(tokens, qkv_weight, bias, cache, lengths, slot_stream, frequency)


def solution(mesh):
    def program(tokens, qkv_weight, qkv_bias, cache, lengths, slot_stream):
        cols = qkv_weight.shape[1]
        groups = lax.axis_size("grp")
        fits = lax.axis_size("tp") == 2 and groups % 2 == 0 and cols % HD == HD // 2
        body = fused if fits else on_device
        return body(tokens, qkv_weight, qkv_bias, cache, lengths, slot_stream)

    in_specs = (
        P(("rep", "tp", "grp"), None),
        P(None, ("tp", "grp")),
        P(),
        P(("rep", "tp", "grp"), None, None),
        P("rep"),
        P("rep"),
    )
    out_specs = P(("rep", "tp", "grp"), None)
    return jax.shard_map(
        program, mesh=mesh, in_specs=in_specs, out_specs=out_specs, check_vma=False
    )
```

```python
import functools

import jax
import jax.numpy as jnp
import numpy as np
from jax import lax
from jax.experimental import pallas as pl
from jax.experimental.pallas import tpu as pltpu
from jax.sharding import PartitionSpec as P

HD = 128
HQ = 32
KVH = 4
STRETCH = 16
CAP = 1024
GROUP = 8


ROPE_THETA = 1000000.0


def rotate(vectors, positions):
    half_width = vectors.shape[-1] // 2
    frequency = ROPE_THETA ** (
        -(jnp.arange(half_width, dtype=jnp.float32) * 2.0) / vectors.shape[-1]
    )
    angles = positions.astype(jnp.float32)[:, None] * frequency[None, :]
    cosine = jnp.cos(angles)[:, None, :]
    sine_part = jnp.sin(angles)[:, None, :]
    front_half = vectors[..., :half_width]
    back_half = vectors[..., half_width:]
    return jnp.concatenate(
        [front_half * cosine - back_half * sine_part, back_half * cosine + front_half * sine_part],
        axis=-1,
    )


def attend(token_block, slot_cache, length):
    query_width = HQ * HD
    kv_width = KVH * HD
    positions = length + jnp.arange(STRETCH, dtype=jnp.int32)
    queries = rotate(
        token_block[:, :query_width].astype(jnp.float32).reshape(STRETCH, HQ, HD), positions
    ).astype(jnp.bfloat16)
    new_keys = rotate(
        token_block[:, query_width : query_width + kv_width]
        .astype(jnp.float32)
        .reshape(STRETCH, KVH, HD),
        positions,
    ).astype(jnp.bfloat16)
    new_values = token_block[:, query_width + kv_width :].reshape(STRETCH, KVH, HD)
    grouped = (
        queries.reshape(STRETCH, KVH, GROUP, HD)
        .transpose(1, 0, 2, 3)
        .reshape(KVH, STRETCH * GROUP, HD)
    )
    score_scale = HD ** (-0.5)
    query_token = jnp.arange(STRETCH * GROUP, dtype=jnp.int32) // GROUP
    scores = (
        jnp.einsum("krd,jkd->krj", grouped, new_keys, preferred_element_type=jnp.float32)
        * score_scale
    )
    causal = jnp.arange(STRETCH, dtype=jnp.int32)[None, :] <= query_token[:, None]
    scores = jnp.where(causal[None], scores, -jnp.inf)
    row_max = jnp.max(scores, axis=-1)
    exponent = jnp.exp(scores - row_max[..., None])
    row_total = jnp.sum(exponent, axis=-1)
    running = jnp.einsum(
        "krj,jkd->krd",
        exponent.astype(jnp.bfloat16),
        new_values,
        preferred_element_type=jnp.float32,
    )
    key_span = min(CAP, 256)
    key_part = slot_cache[:, :kv_width]
    value_part = slot_cache[:, kv_width:]

    def visit(block_index, running_state):
        old_max, old_total, old_sum = running_state
        offset = block_index * key_span
        key_block = lax.dynamic_slice_in_dim(key_part, offset, key_span, 0).reshape(
            key_span, KVH, HD
        )
        value_block = lax.dynamic_slice_in_dim(value_part, offset, key_span, 0).reshape(
            key_span, KVH, HD
        )
        block_scores = (
            jnp.einsum("krd,jkd->krj", grouped, key_block, preferred_element_type=jnp.float32)
            * score_scale
        )
        in_cache = offset + jnp.arange(key_span, dtype=jnp.int32) < length
        block_scores = jnp.where(in_cache[None, None, :], block_scores, -jnp.inf)
        new_max = jnp.maximum(old_max, jnp.max(block_scores, axis=-1))
        rescale = jnp.exp(old_max - new_max)
        block_exp = jnp.exp(block_scores - new_max[..., None])
        new_total = old_total * rescale + jnp.sum(block_exp, axis=-1)
        new_sum = old_sum * rescale[..., None] + jnp.einsum(
            "krj,jkd->krd",
            block_exp.astype(jnp.bfloat16),
            value_block,
            preferred_element_type=jnp.float32,
        )
        return (new_max, new_total, new_sum)

    block_count = CAP // key_span
    row_max, row_total, running = lax.fori_loop(
        0, block_count, visit, (row_max, row_total, running)
    )
    result = running / row_total[..., None]
    return (
        result.reshape(KVH, STRETCH, GROUP, HD)
        .transpose(1, 0, 2, 3)
        .reshape(STRETCH, HQ * HD)
        .astype(jnp.bfloat16)
    )


def on_device(tokens, qkv_weight, qkv_bias, cache, lengths, slot_stream):
    my_index = lax.axis_index(("tp", "grp"))
    grp_index = lax.axis_index("grp")
    tp_count = lax.axis_size("tp")
    grp_count = lax.axis_size("grp")
    per_device = cache.shape[0]
    local_rows = per_device * STRETCH
    shard_cols = qkv_weight.shape[1]
    weight_cols = lax.all_gather(qkv_weight, "tp", axis=1, tiled=True)
    bias_table = qkv_bias.reshape(tp_count, grp_count, shard_cols)
    bias_cols = (
        lax.dynamic_index_in_dim(bias_table, grp_index, 1, keepdims=False)
        .reshape(-1)
        .astype(jnp.float32)
    )
    partial_cols = jnp.dot(
        lax.all_gather(tokens, "grp", axis=0, tiled=True),
        weight_cols,
        preferred_element_type=jnp.float32,
    )
    rounded_cols = (partial_cols + bias_cols[None, :]).astype(jnp.bfloat16)
    received = lax.all_to_all(rounded_cols, "grp", split_axis=0, concat_axis=1, tiled=True)
    projected_qkv = (
        received.reshape(local_rows, grp_count, tp_count, shard_cols)
        .transpose(0, 2, 1, 3)
        .reshape(local_rows, -1)
    )
    my_slots = my_index * per_device + jnp.arange(per_device, dtype=jnp.int32)
    my_lengths = jnp.take(lengths, jnp.take(slot_stream, my_slots))
    attended = jnp.concatenate(
        [
            attend(
                projected_qkv[slot_index * STRETCH : (slot_index + 1) * STRETCH],
                cache[slot_index],
                my_lengths[slot_index],
            )
            for slot_index in range(per_device)
        ],
        axis=0,
    )
    return attended


MESH = pl.DeviceIdType.MESH
LOG2E = 1.4426950408889634


def fused_kernel(
    n,
    groups,
    cols,
    tokens_ref,
    weight_ref,
    bias_ref,
    cache_ref,
    lengths_ref,
    streams_ref,
    freq_ref,
    out_ref,
    tok,
    weights,
    slots,
    bias,
    outgoing,
    incoming,
    cos_table,
    sin_table,
    tok_local,
    tok_send,
    tok_recv,
    part_send,
    part_recv,
    weight_sems,
    cache_sems,
):
    tp = lax.axis_index("tp")
    me = lax.axis_index("grp")
    chain = groups // 2
    depth = me // 2
    side = me % 2
    across = depth * 2 + 1 - side
    main = cols - HD // 2
    first_slot = (tp * groups + me) * n

    def local_tokens(c):
        return pltpu.make_async_copy(
            tokens_ref.at[pl.ds(pl.multiple_of(c * STRETCH, STRETCH), STRETCH)],
            tok.at[c, me],
            tok_local.at[c],
        )

    def cache_copy(c):
        return pltpu.make_async_copy(cache_ref.at[c], slots.at[c], cache_sems.at[c])

    def tok_copy(c, block, direction, target):
        return pltpu.make_async_remote_copy(
            src_ref=tok.at[c, block],
            dst_ref=tok.at[c, block],
            send_sem=tok_send.at[c, block, direction],
            recv_sem=tok_recv.at[c, block],
            device_id={"grp": target},
            device_id_type=MESH,
        )

    def part_copy(c, peer):
        return pltpu.make_async_remote_copy(
            src_ref=outgoing.at[c, peer],
            dst_ref=incoming.at[c, me],
            send_sem=part_send.at[c, peer],
            recv_sem=part_recv.at[c, me],
            device_id={"grp": peer},
            device_id_type=MESH,
        )

    def part_arrival(c, peer):
        return pltpu.make_async_remote_copy(
            src_ref=outgoing.at[c, peer],
            dst_ref=incoming.at[c, peer],
            send_sem=part_send.at[c, peer],
            recv_sem=part_recv.at[c, peer],
            device_id={"grp": peer},
            device_id_type=MESH,
        )

    pieces = (
        (HD // 2 * side, main, (main + HD) * tp),
        (main * (1 - side), HD // 2, main + HD // 2 * ((tp + side) % 2)),
    )

    def weight_own(p):
        start, size, at = pieces[p]
        return pltpu.make_async_copy(
            weight_ref.at[pl.ds(pl.multiple_of(start, HD // 2), size)],
            weights.at[pl.ds(pl.multiple_of(at, HD // 2), size)],
            weight_sems.at[p, 0],
        )

    def weight_swap(p):
        start, size, at = pieces[p]
        return pltpu.make_async_remote_copy(
            src_ref=weight_ref.at[pl.ds(pl.multiple_of(start, HD // 2), size)],
            dst_ref=weights.at[pl.ds(pl.multiple_of(at, HD // 2), size)],
            send_sem=weight_sems.at[p, 1],
            recv_sem=weight_sems.at[p, 2],
            device_id={"tp": 1 - tp},
            device_id_type=MESH,
        )

    for c in range(n):
        local_tokens(c).start()

    barrier = pltpu.get_barrier_semaphore()
    pl.semaphore_signal(barrier, inc=1, device_id={"tp": 1 - tp}, device_id_type=MESH)
    for d in range(1, groups):
        pl.semaphore_signal(
            barrier, inc=1, device_id={"grp": lax.rem(me + d, groups)}, device_id_type=MESH
        )
    pl.semaphore_wait(barrier, groups)

    def send_own(c):
        local_tokens(c).wait()
        tok_copy(c, me, 2, across).start()

        @pl.when(depth + 1 < chain)
        def _():
            tok_copy(c, me, 0, me + 2).start()

        @pl.when(depth >= 1)
        def _():
            tok_copy(c, me, 1, me - 2).start()

    def forward(c, s):
        @pl.when(depth >= s)
        def _():
            block = me - 2 * s
            tok_copy(c, block, 2, across).wait_recv()
            tok_copy(c, block, 2, across).start()

            @pl.when(depth + 1 < chain)
            def _():
                tok_copy(c, block, 0, me + 2).start()

        @pl.when(depth + s < chain)
        def _():
            block = me + 2 * s
            tok_copy(c, block, 2, across).wait_recv()
            tok_copy(c, block, 2, across).start()

            @pl.when(depth >= 1)
            def _():
                tok_copy(c, block, 1, me - 2).start()

    nt = (((1,), (1,)), ((), ()))

    def finish_sends(c):
        for level in range(chain):
            block = level * 2 + side
            tok_copy(c, block, 2, across).wait_send()

            @pl.when((level <= depth) & (depth + 1 < chain))
            def _():
                tok_copy(c, block, 0, me + 2).wait_send()

            @pl.when((level >= depth) & (depth >= 1))
            def _():
                tok_copy(c, block, 1, me - 2).wait_send()

        for d in range(1, groups):
            part_copy(c, lax.rem(me + d, groups)).wait_send()

    def project(c):
        for level in range(chain):
            tok_copy(c, level * 2 + 1 - side, 2, across).wait_recv()
        rows = tok[c].reshape(groups * STRETCH, tok.shape[3])
        product = lax.dot_general(rows, weights[...], nt, preferred_element_type=jnp.float32)
        product = (product + bias[...]).astype(jnp.bfloat16)
        outgoing[c] = product.reshape(groups, STRETCH, 2 * cols)
        for d in range(1, groups):
            part_copy(c, lax.rem(me + d, groups)).start()
        incoming[c, me] = outgoing[c, me]

    lane = lax.broadcasted_iota(jnp.int32, (STRETCH, HD), 1)
    rows_all = STRETCH * GROUP
    pair_heads = 2 * cols // HD
    half = groups // 2 * pair_heads
    middle = pair_heads // 2

    def attention(c):
        for d in range(1, groups):
            part_arrival(c, lax.rem(me + d, groups)).wait_recv()
        cache_copy(c).wait()
        length = lengths_ref[streams_ref[first_slot + c]]
        cosine = cos_table[c]
        sine = sin_table[c]
        key_index = lax.broadcasted_iota(jnp.int32, (1, CAP), 1)
        in_cache = key_index < length
        new_index = lax.broadcasted_iota(jnp.int32, (rows_all, STRETCH), 1)
        new_token = lax.broadcasted_iota(jnp.int32, (rows_all, STRETCH), 0) % STRETCH
        causal = new_index <= new_token
        factor = HD ** (-0.5) * LOG2E

        def head(i):
            t, rest = divmod(i, half)
            pair, k = divmod(rest, pair_heads)
            if k != middle:
                block, at = (2 * pair, k) if k < middle else (2 * pair + 1, k - middle - 1)
                at = at * HD + t * (main + HD)
                return incoming[c, block, :, at : at + HD]
            left = incoming[c, 2 * pair, :, main : main + HD].astype(jnp.float32)
            right = incoming[c, 2 * pair + 1, :, main : main + HD].astype(jnp.float32)
            if t == 0:
                joined = jnp.where(lane < HD // 2, left, right)
            else:
                joined = pltpu.roll(jnp.where(lane < HD // 2, right, left), HD // 2, 1)
            return joined.astype(jnp.bfloat16)

        def rotated(i):
            u = head(i).astype(jnp.float32)
            return (u * cosine + pltpu.roll(u, HD // 2, 1) * sine).astype(jnp.bfloat16)

        for k in range(KVH):
            queries = jnp.concatenate([rotated(k * GROUP + g) for g in range(GROUP)], axis=0)
            new_keys = rotated(HQ + k)
            new_values = head(HQ + KVH + k)
            keys = slots[c, :, k * HD : (k + 1) * HD]
            values = slots[c, :, (KVH + k) * HD : (KVH + k + 1) * HD]
            scores = lax.dot_general(queries, keys, nt, preferred_element_type=jnp.float32)
            scores = jnp.where(in_cache, scores, -jnp.inf)
            new_scores = lax.dot_general(queries, new_keys, nt, preferred_element_type=jnp.float32)
            new_scores = jnp.where(causal, new_scores, -jnp.inf)
            top = jnp.maximum(
                jnp.max(scores, axis=-1, keepdims=True), jnp.max(new_scores, axis=-1, keepdims=True)
            )
            probs = jnp.exp2((scores - top) * factor)
            new_probs = jnp.exp2((new_scores - top) * factor)
            total = jnp.sum(probs, axis=-1, keepdims=True) + jnp.sum(
                new_probs, axis=-1, keepdims=True
            )
            summed = jnp.dot(
                probs.astype(jnp.bfloat16), values, preferred_element_type=jnp.float32
            ) + jnp.dot(
                new_probs.astype(jnp.bfloat16), new_values, preferred_element_type=jnp.float32
            )
            result = (summed / total).astype(jnp.bfloat16)
            for g in range(GROUP):
                h = k * GROUP + g
                out_ref[
                    pl.ds(pl.multiple_of(c * STRETCH, STRETCH), STRETCH), h * HD : (h + 1) * HD
                ] = result[g * STRETCH : (g + 1) * STRETCH]

    for c in range(min(2, n)):
        send_own(c)
    for p in range(2):
        weight_own(p).start()
        weight_swap(p).start()
    for c in range(n):
        cache_copy(c).start()

    first_head = depth * pair_heads

    def bias_heads(start, count):
        at = pl.multiple_of(start * HD, HD)
        return bias_ref[:, pl.ds(at, count * HD)].astype(jnp.float32)

    for t in range(2):
        whole = bias_heads(t * half + first_head + (middle + 1) * side, middle)
        bias[:, t * (main + HD) : t * (main + HD) + main] = whole
    joint = [bias_heads(t * half + first_head + middle, 1) for t in range(2)]
    front = lax.broadcasted_iota(jnp.int32, (1, HD), 1) // (HD // 2) == side
    bias[:, main : main + HD] = jnp.where(front, joint[0], pltpu.roll(joint[1], HD // 2, 1))

    sign = jnp.where(lane < HD // 2, -1.0, 1.0)
    token = lax.broadcasted_iota(jnp.int32, (STRETCH, HD), 0)
    for c in range(n):
        length = lengths_ref[streams_ref[first_slot + c]]
        angles = (length + token).astype(jnp.float32) * freq_ref[...]
        cos_table[c] = jnp.cos(angles)
        sin_table[c] = jnp.sin(angles) * sign

    @pl.loop(0, n + 2)
    def _(i):
        @pl.when(i < n)
        def _():
            forward(i, 1)

        @pl.when(i == 1)
        def _():
            for p in range(2):
                weight_own(p).wait()
                weight_swap(p).wait()

        @pl.when((i >= 1) & (i < n + 1))
        def _():
            project(i - 1)

        @pl.when(i < n)
        def _():
            for s in range(2, chain):
                forward(i, s)

        @pl.when(i + 2 < n)
        def _():
            send_own(i + 2)

        @pl.when(i >= 2)
        def _():
            attention(i - 2)

    @pl.loop(0, n)
    def _(c):
        finish_sends(c)


def fused(tokens, qkv_weight, qkv_bias, cache, lengths, slot_stream):
    groups = lax.axis_size("grp")
    n = cache.shape[0]
    width, cols = qkv_weight.shape
    frequency = ROPE_THETA ** (-(np.arange(HD // 2) * 2.0) / HD)
    frequency = np.concatenate([frequency, frequency])[None, :].astype(np.float32)
    anywhere = pl.BlockSpec(memory_space=pl.ANY)
    vmem = pl.BlockSpec(memory_space=pltpu.VMEM)
    smem = pl.BlockSpec(memory_space=pltpu.SMEM)
    dma = pltpu.SemaphoreType.DMA
    rows = groups * STRETCH
    attention_ops = 4 * n * KVH * STRETCH * GROUP * CAP * HD
    return pl.pallas_call(
        functools.partial(fused_kernel, n, groups, cols),
        out_shape=jax.ShapeDtypeStruct((n * STRETCH, HQ * HD), jnp.bfloat16),
        in_specs=[anywhere, anywhere, vmem, anywhere, smem, smem, vmem],
        out_specs=vmem,
        scratch_shapes=[
            pltpu.VMEM((n, groups, STRETCH, width), jnp.bfloat16),
            pltpu.VMEM((2 * cols, width), jnp.bfloat16),
            pltpu.VMEM(cache.shape, jnp.bfloat16),
            pltpu.VMEM((1, 2 * cols), jnp.float32),
            pltpu.VMEM((n, groups, STRETCH, 2 * cols), jnp.bfloat16),
            pltpu.VMEM((n, groups, STRETCH, 2 * cols), jnp.bfloat16),
            pltpu.VMEM((n, STRETCH, HD), jnp.float32),
            pltpu.VMEM((n, STRETCH, HD), jnp.float32),
            dma((n,)),
            dma((n, groups, 3)),
            dma((n, groups)),
            dma((n, groups)),
            dma((n, groups)),
            dma((2, 3)),
            dma((n,)),
        ],
        compiler_params=pltpu.CompilerParams(
            collective_id=0, has_side_effects=True, vmem_limit_bytes=56 * 2**20
        ),
        cost_estimate=pl.CostEstimate(
            flops=4 * n * rows * width * cols + attention_ops,
            bytes_accessed=2 * (cache.size + 2 * qkv_weight.size),
            transcendentals=n * KVH * STRETCH * GROUP * CAP,
        ),
    )(tokens, qkv_weight.T, qkv_bias[None, :], cache, lengths, slot_stream, jnp.asarray(frequency))


def solution(mesh):
    def program(tokens, qkv_weight, qkv_bias, cache, lengths, slot_stream):
        cols = qkv_weight.shape[1]
        groups = lax.axis_size("grp")
        fits = lax.axis_size("tp") == 2 and groups % 2 == 0 and cols % HD == HD // 2
        body = fused if fits else on_device
        return body(tokens, qkv_weight, qkv_bias, cache, lengths, slot_stream)

    in_specs = (
        P(("rep", "tp", "grp"), None),
        P(None, ("tp", "grp")),
        P(),
        P(("rep", "tp", "grp"), None, None),
        P("rep"),
        P("rep"),
    )
    out_specs = P(("rep", "tp", "grp"), None)
    return jax.shard_map(
        program, mesh=mesh, in_specs=in_specs, out_specs=out_specs, check_vma=False
    )
```

```python
import functools

import jax
import jax.numpy as jnp
import numpy as np
from jax import lax
from jax.experimental import pallas as pl
from jax.experimental.pallas import tpu as pltpu
from jax.sharding import PartitionSpec as P

HD = 128
HQ = 32
KVH = 4
STRETCH = 16
CAP = 1024
GROUP = 8


ROPE_THETA = 1000000.0


def rotate(vectors, positions):
    half_width = vectors.shape[-1] // 2
    frequency = ROPE_THETA ** (
        -(jnp.arange(half_width, dtype=jnp.float32) * 2.0) / vectors.shape[-1]
    )
    angles = positions.astype(jnp.float32)[:, None] * frequency[None, :]
    cosine = jnp.cos(angles)[:, None, :]
    sine_part = jnp.sin(angles)[:, None, :]
    front_half = vectors[..., :half_width]
    back_half = vectors[..., half_width:]
    return jnp.concatenate(
        [front_half * cosine - back_half * sine_part, back_half * cosine + front_half * sine_part],
        axis=-1,
    )


def attend(token_block, slot_cache, length):
    query_width = HQ * HD
    kv_width = KVH * HD
    positions = length + jnp.arange(STRETCH, dtype=jnp.int32)
    queries = rotate(
        token_block[:, :query_width].astype(jnp.float32).reshape(STRETCH, HQ, HD), positions
    ).astype(jnp.bfloat16)
    new_keys = rotate(
        token_block[:, query_width : query_width + kv_width]
        .astype(jnp.float32)
        .reshape(STRETCH, KVH, HD),
        positions,
    ).astype(jnp.bfloat16)
    new_values = token_block[:, query_width + kv_width :].reshape(STRETCH, KVH, HD)
    grouped = (
        queries.reshape(STRETCH, KVH, GROUP, HD)
        .transpose(1, 0, 2, 3)
        .reshape(KVH, STRETCH * GROUP, HD)
    )
    score_scale = HD ** (-0.5)
    query_token = jnp.arange(STRETCH * GROUP, dtype=jnp.int32) // GROUP
    scores = (
        jnp.einsum("krd,jkd->krj", grouped, new_keys, preferred_element_type=jnp.float32)
        * score_scale
    )
    causal = jnp.arange(STRETCH, dtype=jnp.int32)[None, :] <= query_token[:, None]
    scores = jnp.where(causal[None], scores, -jnp.inf)
    row_max = jnp.max(scores, axis=-1)
    exponent = jnp.exp(scores - row_max[..., None])
    row_total = jnp.sum(exponent, axis=-1)
    running = jnp.einsum(
        "krj,jkd->krd",
        exponent.astype(jnp.bfloat16),
        new_values,
        preferred_element_type=jnp.float32,
    )
    key_span = min(CAP, 256)
    key_part = slot_cache[:, :kv_width]
    value_part = slot_cache[:, kv_width:]

    def visit(block_index, running_state):
        old_max, old_total, old_sum = running_state
        offset = block_index * key_span
        key_block = lax.dynamic_slice_in_dim(key_part, offset, key_span, 0).reshape(
            key_span, KVH, HD
        )
        value_block = lax.dynamic_slice_in_dim(value_part, offset, key_span, 0).reshape(
            key_span, KVH, HD
        )
        block_scores = (
            jnp.einsum("krd,jkd->krj", grouped, key_block, preferred_element_type=jnp.float32)
            * score_scale
        )
        in_cache = offset + jnp.arange(key_span, dtype=jnp.int32) < length
        block_scores = jnp.where(in_cache[None, None, :], block_scores, -jnp.inf)
        new_max = jnp.maximum(old_max, jnp.max(block_scores, axis=-1))
        rescale = jnp.exp(old_max - new_max)
        block_exp = jnp.exp(block_scores - new_max[..., None])
        new_total = old_total * rescale + jnp.sum(block_exp, axis=-1)
        new_sum = old_sum * rescale[..., None] + jnp.einsum(
            "krj,jkd->krd",
            block_exp.astype(jnp.bfloat16),
            value_block,
            preferred_element_type=jnp.float32,
        )
        return (new_max, new_total, new_sum)

    block_count = CAP // key_span
    row_max, row_total, running = lax.fori_loop(
        0, block_count, visit, (row_max, row_total, running)
    )
    result = running / row_total[..., None]
    return (
        result.reshape(KVH, STRETCH, GROUP, HD)
        .transpose(1, 0, 2, 3)
        .reshape(STRETCH, HQ * HD)
        .astype(jnp.bfloat16)
    )


def on_device(tokens, qkv_weight, qkv_bias, cache, lengths, slot_stream):
    my_index = lax.axis_index(("tp", "grp"))
    grp_index = lax.axis_index("grp")
    tp_count = lax.axis_size("tp")
    grp_count = lax.axis_size("grp")
    per_device = cache.shape[0]
    local_rows = per_device * STRETCH
    shard_cols = qkv_weight.shape[1]
    weight_cols = lax.all_gather(qkv_weight, "tp", axis=1, tiled=True)
    bias_table = qkv_bias.reshape(tp_count, grp_count, shard_cols)
    bias_cols = (
        lax.dynamic_index_in_dim(bias_table, grp_index, 1, keepdims=False)
        .reshape(-1)
        .astype(jnp.float32)
    )
    partial_cols = jnp.dot(
        lax.all_gather(tokens, "grp", axis=0, tiled=True),
        weight_cols,
        preferred_element_type=jnp.float32,
    )
    rounded_cols = (partial_cols + bias_cols[None, :]).astype(jnp.bfloat16)
    received = lax.all_to_all(rounded_cols, "grp", split_axis=0, concat_axis=1, tiled=True)
    projected_qkv = (
        received.reshape(local_rows, grp_count, tp_count, shard_cols)
        .transpose(0, 2, 1, 3)
        .reshape(local_rows, -1)
    )
    my_slots = my_index * per_device + jnp.arange(per_device, dtype=jnp.int32)
    my_lengths = jnp.take(lengths, jnp.take(slot_stream, my_slots))
    attended = jnp.concatenate(
        [
            attend(
                projected_qkv[slot_index * STRETCH : (slot_index + 1) * STRETCH],
                cache[slot_index],
                my_lengths[slot_index],
            )
            for slot_index in range(per_device)
        ],
        axis=0,
    )
    return attended


MESH = pl.DeviceIdType.MESH
LOG2E = 1.4426950408889634


def fused_kernel(
    n,
    groups,
    cols,
    tokens_ref,
    weight_ref,
    bias_ref,
    cache_ref,
    lengths_ref,
    streams_ref,
    freq_ref,
    out_ref,
    tok,
    weights,
    slots,
    bias,
    outgoing,
    incoming,
    cos_table,
    sin_table,
    tok_local,
    tok_send,
    tok_recv,
    part_send,
    part_recv,
    weight_sems,
    cache_sems,
    relay_sems,
):
    tp = lax.axis_index("tp")
    me = lax.axis_index("grp")
    chain = groups // 2
    depth = me // 2
    side = me % 2
    across = depth * 2 + 1 - side
    paired = depth + 1 - 2 * (depth % 2)
    width = tok.shape[3]
    split = width * 11 // 32 // HD * HD
    main = cols - HD // 2
    first_slot = (tp * groups + me) * n

    def local_tokens(c):
        return pltpu.make_async_copy(
            tokens_ref.at[pl.ds(pl.multiple_of(c * STRETCH, STRETCH), STRETCH)],
            tok.at[c, me],
            tok_local.at[c],
        )

    def cache_copy(c):
        return pltpu.make_async_copy(cache_ref.at[c], slots.at[c], cache_sems.at[c])

    def tok_copy(c, block, direction, target):
        return pltpu.make_async_remote_copy(
            src_ref=tok.at[c, block],
            dst_ref=tok.at[c, block],
            send_sem=tok_send.at[c, block, direction],
            recv_sem=tok_recv.at[c, block],
            device_id={"grp": target},
            device_id_type=MESH,
        )

    def rest_copy(c, block):
        part = tok.at[c, block, :, pl.ds(split, width - split)]
        return pltpu.make_async_remote_copy(
            src_ref=part,
            dst_ref=part,
            send_sem=tok_send.at[c, block, 2],
            recv_sem=tok_recv.at[c, block],
            device_id={"grp": across},
            device_id_type=MESH,
        )

    def relay_copy(c, level):
        part = tok.at[c, level * 2 + 1 - side, :, pl.ds(0, split)]
        return pltpu.make_async_remote_copy(
            src_ref=part,
            dst_ref=part,
            send_sem=relay_sems.at[c, 0],
            recv_sem=relay_sems.at[c, 1],
            device_id={"grp": paired * 2 + side},
            device_id_type=MESH,
        )

    def part_copy(c, peer):
        return pltpu.make_async_remote_copy(
            src_ref=outgoing.at[c, peer],
            dst_ref=incoming.at[c, me],
            send_sem=part_send.at[c, peer],
            recv_sem=part_recv.at[c, me],
            device_id={"grp": peer},
            device_id_type=MESH,
        )

    def part_arrival(c, peer):
        return pltpu.make_async_remote_copy(
            src_ref=outgoing.at[c, peer],
            dst_ref=incoming.at[c, peer],
            send_sem=part_send.at[c, peer],
            recv_sem=part_recv.at[c, peer],
            device_id={"grp": peer},
            device_id_type=MESH,
        )

    pieces = (
        (HD // 2 * side, main, (main + HD) * tp),
        (main * (1 - side), HD // 2, main + HD // 2 * ((tp + side) % 2)),
    )

    def weight_own(p):
        start, size, at = pieces[p]
        return pltpu.make_async_copy(
            weight_ref.at[pl.ds(pl.multiple_of(start, HD // 2), size)],
            weights.at[pl.ds(pl.multiple_of(at, HD // 2), size)],
            weight_sems.at[p, 0],
        )

    def weight_swap(p):
        start, size, at = pieces[p]
        return pltpu.make_async_remote_copy(
            src_ref=weight_ref.at[pl.ds(pl.multiple_of(start, HD // 2), size)],
            dst_ref=weights.at[pl.ds(pl.multiple_of(at, HD // 2), size)],
            send_sem=weight_sems.at[p, 1],
            recv_sem=weight_sems.at[p, 2],
            device_id={"tp": 1 - tp},
            device_id_type=MESH,
        )

    for c in range(n):
        local_tokens(c).start()

    barrier = pltpu.get_barrier_semaphore()
    pl.semaphore_signal(barrier, inc=1, device_id={"tp": 1 - tp}, device_id_type=MESH)
    for d in range(1, groups):
        pl.semaphore_signal(
            barrier, inc=1, device_id={"grp": lax.rem(me + d, groups)}, device_id_type=MESH
        )
    pl.semaphore_wait(barrier, groups)

    def send_own(c):
        local_tokens(c).wait()
        tok_copy(c, me, 2, across).start()

        @pl.when(depth + 1 < chain)
        def _():
            tok_copy(c, me, 0, me + 2).start()

        @pl.when(depth >= 1)
        def _():
            tok_copy(c, me, 1, me - 2).start()

    def send_across(c, block, shared):
        @pl.when(shared)
        def _():
            rest_copy(c, block).start()

        @pl.when(jnp.logical_not(shared))
        def _():
            tok_copy(c, block, 2, across).start()

    def relay(c):
        tok_copy(c, across, 2, across).wait_recv()
        relay_copy(c, depth).start()

    def forward(c, s):
        @pl.when(depth >= s)
        def _():
            block = me - 2 * s
            tok_copy(c, block, 2, across).wait_recv()
            send_across(c, block, (s == 1) & (depth % 2 == 1))

            @pl.when(depth + 1 < chain)
            def _():
                tok_copy(c, block, 0, me + 2).start()

        @pl.when(depth + s < chain)
        def _():
            block = me + 2 * s
            tok_copy(c, block, 2, across).wait_recv()
            send_across(c, block, (s == 1) & (depth % 2 == 0))

            @pl.when(depth >= 1)
            def _():
                tok_copy(c, block, 1, me - 2).start()

    nt = (((1,), (1,)), ((), ()))

    def finish_sends(c):
        for level in range(chain):
            block = level * 2 + side

            @pl.when(level == paired)
            def _():
                rest_copy(c, block).wait_send()

            @pl.when(level != paired)
            def _():
                tok_copy(c, block, 2, across).wait_send()

            @pl.when((level <= depth) & (depth + 1 < chain))
            def _():
                tok_copy(c, block, 0, me + 2).wait_send()

            @pl.when((level >= depth) & (depth >= 1))
            def _():
                tok_copy(c, block, 1, me - 2).wait_send()

        relay_copy(c, depth).wait_send()
        for d in range(1, groups):
            part_copy(c, lax.rem(me + d, groups)).wait_send()

    def project(c):
        for level in range(chain):
            block = level * 2 + 1 - side

            @pl.when((level != paired) & (level != depth))
            def _():
                tok_copy(c, block, 2, across).wait_recv()

            @pl.when(level == paired)
            def _():
                rest_copy(c, block).wait_recv()
                relay_copy(c, level).wait_recv()

        rows = tok[c].reshape(groups * STRETCH, tok.shape[3])
        product = lax.dot_general(rows, weights[...], nt, preferred_element_type=jnp.float32)
        product = (product + bias[...]).astype(jnp.bfloat16)
        outgoing[c] = product.reshape(groups, STRETCH, 2 * cols)
        for d in range(1, groups):
            part_copy(c, lax.rem(me + d, groups)).start()
        incoming[c, me] = outgoing[c, me]

    lane = lax.broadcasted_iota(jnp.int32, (STRETCH, HD), 1)
    rows_all = STRETCH * GROUP
    pair_heads = 2 * cols // HD
    half = groups // 2 * pair_heads
    middle = pair_heads // 2

    def attention(c):
        for d in range(1, groups):
            part_arrival(c, lax.rem(me + d, groups)).wait_recv()
        cache_copy(c).wait()
        length = lengths_ref[streams_ref[first_slot + c]]
        cosine = cos_table[c]
        sine = sin_table[c]
        key_index = lax.broadcasted_iota(jnp.int32, (1, CAP), 1)
        in_cache = key_index < length
        new_index = lax.broadcasted_iota(jnp.int32, (rows_all, STRETCH), 1)
        new_token = lax.broadcasted_iota(jnp.int32, (rows_all, STRETCH), 0) % STRETCH
        causal = new_index <= new_token
        factor = HD ** (-0.5) * LOG2E

        def head(i):
            t, rest = divmod(i, half)
            pair, k = divmod(rest, pair_heads)
            if k != middle:
                block, at = (2 * pair, k) if k < middle else (2 * pair + 1, k - middle - 1)
                at = at * HD + t * (main + HD)
                return incoming[c, block, :, at : at + HD]
            left = incoming[c, 2 * pair, :, main : main + HD].astype(jnp.float32)
            right = incoming[c, 2 * pair + 1, :, main : main + HD].astype(jnp.float32)
            if t == 0:
                joined = jnp.where(lane < HD // 2, left, right)
            else:
                joined = pltpu.roll(jnp.where(lane < HD // 2, right, left), HD // 2, 1)
            return joined.astype(jnp.bfloat16)

        def rotated(i):
            u = head(i).astype(jnp.float32)
            return (u * cosine + pltpu.roll(u, HD // 2, 1) * sine).astype(jnp.bfloat16)

        for k in range(KVH):
            queries = jnp.concatenate([rotated(k * GROUP + g) for g in range(GROUP)], axis=0)
            new_keys = rotated(HQ + k)
            new_values = head(HQ + KVH + k)
            keys = slots[c, :, k * HD : (k + 1) * HD]
            values = slots[c, :, (KVH + k) * HD : (KVH + k + 1) * HD]
            scores = lax.dot_general(queries, keys, nt, preferred_element_type=jnp.float32)
            scores = jnp.where(in_cache, scores, -jnp.inf)
            new_scores = lax.dot_general(queries, new_keys, nt, preferred_element_type=jnp.float32)
            new_scores = jnp.where(causal, new_scores, -jnp.inf)
            top = jnp.maximum(
                jnp.max(scores, axis=-1, keepdims=True), jnp.max(new_scores, axis=-1, keepdims=True)
            )
            probs = jnp.exp2((scores - top) * factor)
            new_probs = jnp.exp2((new_scores - top) * factor)
            total = jnp.sum(probs, axis=-1, keepdims=True) + jnp.sum(
                new_probs, axis=-1, keepdims=True
            )
            summed = jnp.dot(
                probs.astype(jnp.bfloat16), values, preferred_element_type=jnp.float32
            ) + jnp.dot(
                new_probs.astype(jnp.bfloat16), new_values, preferred_element_type=jnp.float32
            )
            result = (summed / total).astype(jnp.bfloat16)
            for g in range(GROUP):
                h = k * GROUP + g
                out_ref[
                    pl.ds(pl.multiple_of(c * STRETCH, STRETCH), STRETCH), h * HD : (h + 1) * HD
                ] = result[g * STRETCH : (g + 1) * STRETCH]

    for c in range(min(2, n)):
        send_own(c)
    for p in range(2):
        weight_own(p).start()
        weight_swap(p).start()
    for c in range(n):
        cache_copy(c).start()

    first_head = depth * pair_heads

    def bias_heads(start, count):
        at = pl.multiple_of(start * HD, HD)
        return bias_ref[:, pl.ds(at, count * HD)].astype(jnp.float32)

    for t in range(2):
        whole = bias_heads(t * half + first_head + (middle + 1) * side, middle)
        bias[:, t * (main + HD) : t * (main + HD) + main] = whole
    joint = [bias_heads(t * half + first_head + middle, 1) for t in range(2)]
    front = lax.broadcasted_iota(jnp.int32, (1, HD), 1) // (HD // 2) == side
    bias[:, main : main + HD] = jnp.where(front, joint[0], pltpu.roll(joint[1], HD // 2, 1))

    sign = jnp.where(lane < HD // 2, -1.0, 1.0)
    token = lax.broadcasted_iota(jnp.int32, (STRETCH, HD), 0)
    for c in range(n):
        length = lengths_ref[streams_ref[first_slot + c]]
        angles = (length + token).astype(jnp.float32) * freq_ref[...]
        cos_table[c] = jnp.cos(angles)
        sin_table[c] = jnp.sin(angles) * sign

    @pl.loop(0, n + 2)
    def _(i):
        @pl.when(i < n)
        def _():
            forward(i, 1)
            relay(i)

        @pl.when(i == 1)
        def _():
            for p in range(2):
                weight_own(p).wait()
                weight_swap(p).wait()

        @pl.when((i >= 1) & (i < n + 1))
        def _():
            project(i - 1)

        @pl.when(i < n)
        def _():
            for s in range(2, chain):
                forward(i, s)

        @pl.when(i + 2 < n)
        def _():
            send_own(i + 2)

        @pl.when(i >= 2)
        def _():
            attention(i - 2)

    @pl.loop(0, n)
    def _(c):
        finish_sends(c)


def fused(tokens, qkv_weight, qkv_bias, cache, lengths, slot_stream):
    groups = lax.axis_size("grp")
    n = cache.shape[0]
    width, cols = qkv_weight.shape
    frequency = ROPE_THETA ** (-(np.arange(HD // 2) * 2.0) / HD)
    frequency = np.concatenate([frequency, frequency])[None, :].astype(np.float32)
    anywhere = pl.BlockSpec(memory_space=pl.ANY)
    vmem = pl.BlockSpec(memory_space=pltpu.VMEM)
    smem = pl.BlockSpec(memory_space=pltpu.SMEM)
    dma = pltpu.SemaphoreType.DMA
    rows = groups * STRETCH
    attention_ops = 4 * n * KVH * STRETCH * GROUP * CAP * HD
    return pl.pallas_call(
        functools.partial(fused_kernel, n, groups, cols),
        out_shape=jax.ShapeDtypeStruct((n * STRETCH, HQ * HD), jnp.bfloat16),
        in_specs=[anywhere, anywhere, vmem, anywhere, smem, smem, vmem],
        out_specs=vmem,
        scratch_shapes=[
            pltpu.VMEM((n, groups, STRETCH, width), jnp.bfloat16),
            pltpu.VMEM((2 * cols, width), jnp.bfloat16),
            pltpu.VMEM(cache.shape, jnp.bfloat16),
            pltpu.VMEM((1, 2 * cols), jnp.float32),
            pltpu.VMEM((n, groups, STRETCH, 2 * cols), jnp.bfloat16),
            pltpu.VMEM((n, groups, STRETCH, 2 * cols), jnp.bfloat16),
            pltpu.VMEM((n, STRETCH, HD), jnp.float32),
            pltpu.VMEM((n, STRETCH, HD), jnp.float32),
            dma((n,)),
            dma((n, groups, 3)),
            dma((n, groups)),
            dma((n, groups)),
            dma((n, groups)),
            dma((2, 3)),
            dma((n,)),
            dma((n, 2)),
        ],
        compiler_params=pltpu.CompilerParams(
            collective_id=0, has_side_effects=True, vmem_limit_bytes=56 * 2**20
        ),
        cost_estimate=pl.CostEstimate(
            flops=4 * n * rows * width * cols + attention_ops,
            bytes_accessed=2 * (cache.size + 2 * qkv_weight.size),
            transcendentals=n * KVH * STRETCH * GROUP * CAP,
        ),
    )(tokens, qkv_weight.T, qkv_bias[None, :], cache, lengths, slot_stream, jnp.asarray(frequency))


def solution(mesh):
    def program(tokens, qkv_weight, qkv_bias, cache, lengths, slot_stream):
        cols = qkv_weight.shape[1]
        groups = lax.axis_size("grp")
        fits = lax.axis_size("tp") == 2 and groups % 4 == 0 and cols % HD == HD // 2
        body = fused if fits else on_device
        return body(tokens, qkv_weight, qkv_bias, cache, lengths, slot_stream)

    in_specs = (
        P(("rep", "tp", "grp"), None),
        P(None, ("tp", "grp")),
        P(),
        P(("rep", "tp", "grp"), None, None),
        P("rep"),
        P("rep"),
    )
    out_specs = P(("rep", "tp", "grp"), None)
    return jax.shard_map(
        program, mesh=mesh, in_specs=in_specs, out_specs=out_specs, check_vma=False
    )
```

```python
import functools

import jax
import jax.numpy as jnp
import numpy as np
from jax import lax
from jax.experimental import pallas as pl
from jax.experimental.pallas import tpu as pltpu
from jax.sharding import PartitionSpec as P

HD = 128
HQ = 32
KVH = 4
STRETCH = 16
CAP = 1024
GROUP = 8


ROPE_THETA = 1000000.0


def rotate(vectors, positions):
    half_width = vectors.shape[-1] // 2
    frequency = ROPE_THETA ** (
        -(jnp.arange(half_width, dtype=jnp.float32) * 2.0) / vectors.shape[-1]
    )
    angles = positions.astype(jnp.float32)[:, None] * frequency[None, :]
    cosine = jnp.cos(angles)[:, None, :]
    sine_part = jnp.sin(angles)[:, None, :]
    front_half = vectors[..., :half_width]
    back_half = vectors[..., half_width:]
    return jnp.concatenate(
        [front_half * cosine - back_half * sine_part, back_half * cosine + front_half * sine_part],
        axis=-1,
    )


def attend(token_block, slot_cache, length):
    query_width = HQ * HD
    kv_width = KVH * HD
    positions = length + jnp.arange(STRETCH, dtype=jnp.int32)
    queries = rotate(
        token_block[:, :query_width].astype(jnp.float32).reshape(STRETCH, HQ, HD), positions
    ).astype(jnp.bfloat16)
    new_keys = rotate(
        token_block[:, query_width : query_width + kv_width]
        .astype(jnp.float32)
        .reshape(STRETCH, KVH, HD),
        positions,
    ).astype(jnp.bfloat16)
    new_values = token_block[:, query_width + kv_width :].reshape(STRETCH, KVH, HD)
    grouped = (
        queries.reshape(STRETCH, KVH, GROUP, HD)
        .transpose(1, 0, 2, 3)
        .reshape(KVH, STRETCH * GROUP, HD)
    )
    score_scale = HD ** (-0.5)
    query_token = jnp.arange(STRETCH * GROUP, dtype=jnp.int32) // GROUP
    scores = (
        jnp.einsum("krd,jkd->krj", grouped, new_keys, preferred_element_type=jnp.float32)
        * score_scale
    )
    causal = jnp.arange(STRETCH, dtype=jnp.int32)[None, :] <= query_token[:, None]
    scores = jnp.where(causal[None], scores, -jnp.inf)
    row_max = jnp.max(scores, axis=-1)
    exponent = jnp.exp(scores - row_max[..., None])
    row_total = jnp.sum(exponent, axis=-1)
    running = jnp.einsum(
        "krj,jkd->krd",
        exponent.astype(jnp.bfloat16),
        new_values,
        preferred_element_type=jnp.float32,
    )
    key_span = min(CAP, 256)
    key_part = slot_cache[:, :kv_width]
    value_part = slot_cache[:, kv_width:]

    def visit(block_index, running_state):
        old_max, old_total, old_sum = running_state
        offset = block_index * key_span
        key_block = lax.dynamic_slice_in_dim(key_part, offset, key_span, 0).reshape(
            key_span, KVH, HD
        )
        value_block = lax.dynamic_slice_in_dim(value_part, offset, key_span, 0).reshape(
            key_span, KVH, HD
        )
        block_scores = (
            jnp.einsum("krd,jkd->krj", grouped, key_block, preferred_element_type=jnp.float32)
            * score_scale
        )
        in_cache = offset + jnp.arange(key_span, dtype=jnp.int32) < length
        block_scores = jnp.where(in_cache[None, None, :], block_scores, -jnp.inf)
        new_max = jnp.maximum(old_max, jnp.max(block_scores, axis=-1))
        rescale = jnp.exp(old_max - new_max)
        block_exp = jnp.exp(block_scores - new_max[..., None])
        new_total = old_total * rescale + jnp.sum(block_exp, axis=-1)
        new_sum = old_sum * rescale[..., None] + jnp.einsum(
            "krj,jkd->krd",
            block_exp.astype(jnp.bfloat16),
            value_block,
            preferred_element_type=jnp.float32,
        )
        return (new_max, new_total, new_sum)

    block_count = CAP // key_span
    row_max, row_total, running = lax.fori_loop(
        0, block_count, visit, (row_max, row_total, running)
    )
    result = running / row_total[..., None]
    return (
        result.reshape(KVH, STRETCH, GROUP, HD)
        .transpose(1, 0, 2, 3)
        .reshape(STRETCH, HQ * HD)
        .astype(jnp.bfloat16)
    )


def on_device(tokens, qkv_weight, qkv_bias, cache, lengths, slot_stream):
    my_index = lax.axis_index(("tp", "grp"))
    grp_index = lax.axis_index("grp")
    tp_count = lax.axis_size("tp")
    grp_count = lax.axis_size("grp")
    per_device = cache.shape[0]
    local_rows = per_device * STRETCH
    shard_cols = qkv_weight.shape[1]
    weight_cols = lax.all_gather(qkv_weight, "tp", axis=1, tiled=True)
    bias_table = qkv_bias.reshape(tp_count, grp_count, shard_cols)
    bias_cols = (
        lax.dynamic_index_in_dim(bias_table, grp_index, 1, keepdims=False)
        .reshape(-1)
        .astype(jnp.float32)
    )
    partial_cols = jnp.dot(
        lax.all_gather(tokens, "grp", axis=0, tiled=True),
        weight_cols,
        preferred_element_type=jnp.float32,
    )
    rounded_cols = (partial_cols + bias_cols[None, :]).astype(jnp.bfloat16)
    received = lax.all_to_all(rounded_cols, "grp", split_axis=0, concat_axis=1, tiled=True)
    projected_qkv = (
        received.reshape(local_rows, grp_count, tp_count, shard_cols)
        .transpose(0, 2, 1, 3)
        .reshape(local_rows, -1)
    )
    my_slots = my_index * per_device + jnp.arange(per_device, dtype=jnp.int32)
    my_lengths = jnp.take(lengths, jnp.take(slot_stream, my_slots))
    attended = jnp.concatenate(
        [
            attend(
                projected_qkv[slot_index * STRETCH : (slot_index + 1) * STRETCH],
                cache[slot_index],
                my_lengths[slot_index],
            )
            for slot_index in range(per_device)
        ],
        axis=0,
    )
    return attended


MESH = pl.DeviceIdType.MESH
LOG2E = 1.4426950408889634


def fused_kernel(
    n,
    groups,
    cols,
    tokens_ref,
    weight_ref,
    bias_ref,
    cache_ref,
    lengths_ref,
    streams_ref,
    freq_ref,
    out_ref,
    tok,
    weights,
    slots,
    bias,
    outgoing,
    incoming,
    cos_table,
    sin_table,
    tok_local,
    tok_send,
    tok_recv,
    part_send,
    part_recv,
    weight_sems,
    cache_sems,
    relay_sems,
    bias_all,
    done,
    out_sems,
):
    tp = lax.axis_index("tp")
    me = lax.axis_index("grp")
    chain = groups // 2
    depth = me // 2
    side = me % 2
    across = depth * 2 + 1 - side
    paired = depth + 1 - 2 * (depth % 2)
    width = tok.shape[3]
    split = width * 11 // 32 // HD * HD
    main = cols - HD // 2
    first_slot = (tp * groups + me) * n

    def local_tokens(c):
        return pltpu.make_async_copy(
            tokens_ref.at[pl.ds(pl.multiple_of(c * STRETCH, STRETCH), STRETCH)],
            tok.at[c, me],
            tok_local.at[c],
        )

    def cache_copy(c):
        return pltpu.make_async_copy(cache_ref.at[c], slots.at[c], cache_sems.at[c])

    def out_copy(c):
        return pltpu.make_async_copy(
            done.at[c],
            out_ref.at[pl.ds(pl.multiple_of(c * STRETCH, STRETCH), STRETCH)],
            out_sems.at[c],
        )

    def tok_copy(c, block, direction, target):
        return pltpu.make_async_remote_copy(
            src_ref=tok.at[c, block],
            dst_ref=tok.at[c, block],
            send_sem=tok_send.at[c, block, direction],
            recv_sem=tok_recv.at[c, block],
            device_id={"grp": target},
            device_id_type=MESH,
        )

    def rest_copy(c, block):
        part = tok.at[c, block, :, pl.ds(split, width - split)]
        return pltpu.make_async_remote_copy(
            src_ref=part,
            dst_ref=part,
            send_sem=tok_send.at[c, block, 2],
            recv_sem=tok_recv.at[c, block],
            device_id={"grp": across},
            device_id_type=MESH,
        )

    def relay_copy(c, level):
        part = tok.at[c, level * 2 + 1 - side, :, pl.ds(0, split)]
        return pltpu.make_async_remote_copy(
            src_ref=part,
            dst_ref=part,
            send_sem=relay_sems.at[c, 0],
            recv_sem=relay_sems.at[c, 1],
            device_id={"grp": paired * 2 + side},
            device_id_type=MESH,
        )

    def part_copy(c, peer):
        return pltpu.make_async_remote_copy(
            src_ref=outgoing.at[c, peer],
            dst_ref=incoming.at[c, me],
            send_sem=part_send.at[c, peer],
            recv_sem=part_recv.at[c, me],
            device_id={"grp": peer},
            device_id_type=MESH,
        )

    def part_arrival(c, peer):
        return pltpu.make_async_remote_copy(
            src_ref=outgoing.at[c, peer],
            dst_ref=incoming.at[c, peer],
            send_sem=part_send.at[c, peer],
            recv_sem=part_recv.at[c, peer],
            device_id={"grp": peer},
            device_id_type=MESH,
        )

    pieces = (
        (HD // 2 * side, main, (main + HD) * tp),
        (main * (1 - side), HD // 2, main + HD // 2 * ((tp + side) % 2)),
    )

    def weight_own(p):
        start, size, at = pieces[p]
        return pltpu.make_async_copy(
            weight_ref.at[pl.ds(pl.multiple_of(start, HD // 2), size)],
            weights.at[pl.ds(pl.multiple_of(at, HD // 2), size)],
            weight_sems.at[p, 0],
        )

    def weight_swap(p):
        start, size, at = pieces[p]
        return pltpu.make_async_remote_copy(
            src_ref=weight_ref.at[pl.ds(pl.multiple_of(start, HD // 2), size)],
            dst_ref=weights.at[pl.ds(pl.multiple_of(at, HD // 2), size)],
            send_sem=weight_sems.at[p, 1],
            recv_sem=weight_sems.at[p, 2],
            device_id={"tp": 1 - tp},
            device_id_type=MESH,
        )

    for c in range(n):
        local_tokens(c).start()

    barrier = pltpu.get_barrier_semaphore()
    pl.semaphore_signal(barrier, inc=1, device_id={"tp": 1 - tp}, device_id_type=MESH)
    for d in range(1, groups):
        pl.semaphore_signal(
            barrier, inc=1, device_id={"grp": lax.rem(me + d, groups)}, device_id_type=MESH
        )
    pl.semaphore_wait(barrier, groups)

    def send_own(c):
        local_tokens(c).wait()
        tok_copy(c, me, 2, across).start()

        @pl.when(depth + 1 < chain)
        def _():
            tok_copy(c, me, 0, me + 2).start()

        @pl.when(depth >= 1)
        def _():
            tok_copy(c, me, 1, me - 2).start()

    def send_across(c, block, shared):
        @pl.when(shared)
        def _():
            rest_copy(c, block).start()

        @pl.when(jnp.logical_not(shared))
        def _():
            tok_copy(c, block, 2, across).start()

    def relay(c):
        tok_copy(c, across, 2, across).wait_recv()
        relay_copy(c, depth).start()

    def forward(c, s):
        @pl.when(depth >= s)
        def _():
            block = me - 2 * s
            tok_copy(c, block, 2, across).wait_recv()
            send_across(c, block, (s == 1) & (depth % 2 == 1))

            @pl.when(depth + 1 < chain)
            def _():
                tok_copy(c, block, 0, me + 2).start()

        @pl.when(depth + s < chain)
        def _():
            block = me + 2 * s
            tok_copy(c, block, 2, across).wait_recv()
            send_across(c, block, (s == 1) & (depth % 2 == 0))

            @pl.when(depth >= 1)
            def _():
                tok_copy(c, block, 1, me - 2).start()

    nt = (((1,), (1,)), ((), ()))

    def finish_sends(c):
        for level in range(chain):
            block = level * 2 + side

            @pl.when(level == paired)
            def _():
                rest_copy(c, block).wait_send()

            @pl.when(level != paired)
            def _():
                tok_copy(c, block, 2, across).wait_send()

            @pl.when((level <= depth) & (depth + 1 < chain))
            def _():
                tok_copy(c, block, 0, me + 2).wait_send()

            @pl.when((level >= depth) & (depth >= 1))
            def _():
                tok_copy(c, block, 1, me - 2).wait_send()

        relay_copy(c, depth).wait_send()
        for d in range(1, groups):
            part_copy(c, lax.rem(me + d, groups)).wait_send()

    def project(c):
        for level in range(chain):
            block = level * 2 + 1 - side

            @pl.when((level != paired) & (level != depth))
            def _():
                tok_copy(c, block, 2, across).wait_recv()

            @pl.when(level == paired)
            def _():
                rest_copy(c, block).wait_recv()
                relay_copy(c, level).wait_recv()

        rows = tok[c].reshape(groups * STRETCH, tok.shape[3])
        product = lax.dot_general(rows, weights[...], nt, preferred_element_type=jnp.float32)
        product = (product + bias[...]).astype(jnp.bfloat16)
        outgoing[c] = product.reshape(groups, STRETCH, 2 * cols)
        for d in range(1, groups):
            part_copy(c, lax.rem(me + d, groups)).start()
        incoming[c, me] = outgoing[c, me]

    lane = lax.broadcasted_iota(jnp.int32, (STRETCH, HD), 1)
    rows_all = STRETCH * GROUP
    pair_heads = 2 * cols // HD
    half = groups // 2 * pair_heads
    middle = pair_heads // 2

    def attention(c):
        for d in range(1, groups):
            part_arrival(c, lax.rem(me + d, groups)).wait_recv()
        cache_copy(c).wait()
        length = lengths_ref[streams_ref[first_slot + c]]
        cosine = cos_table[c]
        sine = sin_table[c]
        key_index = lax.broadcasted_iota(jnp.int32, (1, CAP), 1)
        in_cache = key_index < length
        new_index = lax.broadcasted_iota(jnp.int32, (rows_all, STRETCH), 1)
        new_token = lax.broadcasted_iota(jnp.int32, (rows_all, STRETCH), 0) % STRETCH
        causal = new_index <= new_token
        factor = HD ** (-0.5) * LOG2E

        def head(i):
            t, rest = divmod(i, half)
            pair, k = divmod(rest, pair_heads)
            if k != middle:
                block, at = (2 * pair, k) if k < middle else (2 * pair + 1, k - middle - 1)
                at = at * HD + t * (main + HD)
                return incoming[c, block, :, at : at + HD]
            left = incoming[c, 2 * pair, :, main : main + HD].astype(jnp.float32)
            right = incoming[c, 2 * pair + 1, :, main : main + HD].astype(jnp.float32)
            if t == 0:
                joined = jnp.where(lane < HD // 2, left, right)
            else:
                joined = pltpu.roll(jnp.where(lane < HD // 2, right, left), HD // 2, 1)
            return joined.astype(jnp.bfloat16)

        def rotated(i):
            u = head(i).astype(jnp.float32)
            return (u * cosine + pltpu.roll(u, HD // 2, 1) * sine).astype(jnp.bfloat16)

        for k in range(KVH):
            queries = jnp.concatenate([rotated(k * GROUP + g) for g in range(GROUP)], axis=0)
            new_keys = rotated(HQ + k)
            new_values = head(HQ + KVH + k)
            keys = slots[c, :, k * HD : (k + 1) * HD]
            values = slots[c, :, (KVH + k) * HD : (KVH + k + 1) * HD]
            scores = lax.dot_general(queries, keys, nt, preferred_element_type=jnp.float32)
            scores = jnp.where(in_cache, scores, -jnp.inf)
            new_scores = lax.dot_general(queries, new_keys, nt, preferred_element_type=jnp.float32)
            new_scores = jnp.where(causal, new_scores, -jnp.inf)
            top = jnp.maximum(
                jnp.max(scores, axis=-1, keepdims=True), jnp.max(new_scores, axis=-1, keepdims=True)
            )
            probs = jnp.exp2((scores - top) * factor)
            new_probs = jnp.exp2((new_scores - top) * factor)
            total = jnp.sum(probs, axis=-1, keepdims=True) + jnp.sum(
                new_probs, axis=-1, keepdims=True
            )
            summed = jnp.dot(
                probs.astype(jnp.bfloat16), values, preferred_element_type=jnp.float32
            ) + jnp.dot(
                new_probs.astype(jnp.bfloat16), new_values, preferred_element_type=jnp.float32
            )
            result = (summed / total).astype(jnp.bfloat16)
            for g in range(GROUP):
                h = k * GROUP + g
                done[c, :, h * HD : (h + 1) * HD] = result[g * STRETCH : (g + 1) * STRETCH]
        out_copy(c).start()

    send_own(0)
    for p in range(2):
        weight_own(p).start()
        weight_swap(p).start()
    for c in range(n):
        cache_copy(c).start()

    for start in range(0, bias_ref.shape[0], 2 * HD):
        piece = bias_ref[start : start + 2 * HD].astype(jnp.float32)
        bias_all[:, start : start + 2 * HD] = piece.reshape(1, 2 * HD)

    first_head = depth * pair_heads

    def bias_heads(start, count):
        at = pl.multiple_of(start * HD, HD)
        return bias_all[:, pl.ds(at, count * HD)]

    for t in range(2):
        whole = bias_heads(t * half + first_head + (middle + 1) * side, middle)
        bias[:, t * (main + HD) : t * (main + HD) + main] = whole
    joint = [bias_heads(t * half + first_head + middle, 1) for t in range(2)]
    front = lax.broadcasted_iota(jnp.int32, (1, HD), 1) // (HD // 2) == side
    bias[:, main : main + HD] = jnp.where(front, joint[0], pltpu.roll(joint[1], HD // 2, 1))

    sign = jnp.where(lane < HD // 2, -1.0, 1.0)
    token = lax.broadcasted_iota(jnp.int32, (STRETCH, HD), 0)
    for c in range(n):
        length = lengths_ref[streams_ref[first_slot + c]]
        angles = (length + token).astype(jnp.float32) * freq_ref[...]
        cos_table[c] = jnp.cos(angles)
        sin_table[c] = jnp.sin(angles) * sign

    @pl.loop(0, n + 3)
    def _(i):
        @pl.when(i < n)
        def _():
            forward(i, 1)

        @pl.when(i + 1 < n)
        def _():
            send_own(i + 1)

        @pl.when(((i >= 2) & (i < n)) | ((i > n) & (i >= 3)))
        def _():
            attention(jnp.where(i < n, i - 2, i - 3))

        @pl.when(i < n)
        def _():
            relay(i)
            for s in range(2, chain - 1):
                forward(i, s)

        @pl.when(i == 1)
        def _():
            for p in range(2):
                weight_own(p).wait()
                weight_swap(p).wait()

        @pl.when((i >= 1) & (i < n + 1))
        def _():
            project(i - 1)

        @pl.when(i < n)
        def _():
            forward(i, chain - 1)

    @pl.loop(0, n)
    def _(c):
        finish_sends(c)
        out_copy(c).wait()


def fused(tokens, qkv_weight, qkv_bias, cache, lengths, slot_stream):
    groups = lax.axis_size("grp")
    n = cache.shape[0]
    width, cols = qkv_weight.shape
    frequency = ROPE_THETA ** (-(np.arange(HD // 2) * 2.0) / HD)
    frequency = np.concatenate([frequency, frequency])[None, :].astype(np.float32)
    anywhere = pl.BlockSpec(memory_space=pl.ANY)
    vmem = pl.BlockSpec(memory_space=pltpu.VMEM)
    smem = pl.BlockSpec(memory_space=pltpu.SMEM)
    dma = pltpu.SemaphoreType.DMA
    rows = groups * STRETCH
    attention_ops = 4 * n * KVH * STRETCH * GROUP * CAP * HD
    return pl.pallas_call(
        functools.partial(fused_kernel, n, groups, cols),
        out_shape=jax.ShapeDtypeStruct((n * STRETCH, HQ * HD), jnp.bfloat16),
        in_specs=[anywhere, anywhere, vmem, anywhere, smem, smem, vmem],
        out_specs=anywhere,
        scratch_shapes=[
            pltpu.VMEM((n, groups, STRETCH, width), jnp.bfloat16),
            pltpu.VMEM((2 * cols, width), jnp.bfloat16),
            pltpu.VMEM(cache.shape, jnp.bfloat16),
            pltpu.VMEM((1, 2 * cols), jnp.float32),
            pltpu.VMEM((n, groups, STRETCH, 2 * cols), jnp.bfloat16),
            pltpu.VMEM((n, groups, STRETCH, 2 * cols), jnp.bfloat16),
            pltpu.VMEM((n, STRETCH, HD), jnp.float32),
            pltpu.VMEM((n, STRETCH, HD), jnp.float32),
            dma((n,)),
            dma((n, groups, 3)),
            dma((n, groups)),
            dma((n, groups)),
            dma((n, groups)),
            dma((2, 3)),
            dma((n,)),
            dma((n, 2)),
            pltpu.VMEM((1, qkv_bias.shape[0]), jnp.float32),
            pltpu.VMEM((n, STRETCH, HQ * HD), jnp.bfloat16),
            dma((n,)),
        ],
        compiler_params=pltpu.CompilerParams(
            collective_id=0, has_side_effects=True, vmem_limit_bytes=56 * 2**20
        ),
        cost_estimate=pl.CostEstimate(
            flops=4 * n * rows * width * cols + attention_ops,
            bytes_accessed=2 * (cache.size + 2 * qkv_weight.size),
            transcendentals=n * KVH * STRETCH * GROUP * CAP,
        ),
    )(tokens, qkv_weight.T, qkv_bias, cache, lengths, slot_stream, jnp.asarray(frequency))


def solution(mesh):
    def program(tokens, qkv_weight, qkv_bias, cache, lengths, slot_stream):
        cols = qkv_weight.shape[1]
        groups = lax.axis_size("grp")
        fits = lax.axis_size("tp") == 2 and groups % 4 == 0 and cols % HD == HD // 2
        body = fused if fits else on_device
        return body(tokens, qkv_weight, qkv_bias, cache, lengths, slot_stream)

    in_specs = (
        P(("rep", "tp", "grp"), None),
        P(None, ("tp", "grp")),
        P(),
        P(("rep", "tp", "grp"), None, None),
        P("rep"),
        P("rep"),
    )
    out_specs = P(("rep", "tp", "grp"), None)
    return jax.shard_map(
        program, mesh=mesh, in_specs=in_specs, out_specs=out_specs, check_vma=False
    )
```

```python
import functools

import jax
import jax.numpy as jnp
import numpy as np
from jax import lax
from jax.experimental import pallas as pl
from jax.experimental.pallas import tpu as pltpu
from jax.sharding import PartitionSpec as P

HD = 128
HQ = 32
KVH = 4
STRETCH = 16
CAP = 1024
GROUP = 8


ROPE_THETA = 1000000.0


def rotate(vectors, positions):
    half_width = vectors.shape[-1] // 2
    frequency = ROPE_THETA ** (
        -(jnp.arange(half_width, dtype=jnp.float32) * 2.0) / vectors.shape[-1]
    )
    angles = positions.astype(jnp.float32)[:, None] * frequency[None, :]
    cosine = jnp.cos(angles)[:, None, :]
    sine_part = jnp.sin(angles)[:, None, :]
    front_half = vectors[..., :half_width]
    back_half = vectors[..., half_width:]
    return jnp.concatenate(
        [front_half * cosine - back_half * sine_part, back_half * cosine + front_half * sine_part],
        axis=-1,
    )


def attend(token_block, slot_cache, length):
    query_width = HQ * HD
    kv_width = KVH * HD
    positions = length + jnp.arange(STRETCH, dtype=jnp.int32)
    queries = rotate(
        token_block[:, :query_width].astype(jnp.float32).reshape(STRETCH, HQ, HD), positions
    ).astype(jnp.bfloat16)
    new_keys = rotate(
        token_block[:, query_width : query_width + kv_width]
        .astype(jnp.float32)
        .reshape(STRETCH, KVH, HD),
        positions,
    ).astype(jnp.bfloat16)
    new_values = token_block[:, query_width + kv_width :].reshape(STRETCH, KVH, HD)
    grouped = (
        queries.reshape(STRETCH, KVH, GROUP, HD)
        .transpose(1, 0, 2, 3)
        .reshape(KVH, STRETCH * GROUP, HD)
    )
    score_scale = HD ** (-0.5)
    query_token = jnp.arange(STRETCH * GROUP, dtype=jnp.int32) // GROUP
    scores = (
        jnp.einsum("krd,jkd->krj", grouped, new_keys, preferred_element_type=jnp.float32)
        * score_scale
    )
    causal = jnp.arange(STRETCH, dtype=jnp.int32)[None, :] <= query_token[:, None]
    scores = jnp.where(causal[None], scores, -jnp.inf)
    row_max = jnp.max(scores, axis=-1)
    exponent = jnp.exp(scores - row_max[..., None])
    row_total = jnp.sum(exponent, axis=-1)
    running = jnp.einsum(
        "krj,jkd->krd",
        exponent.astype(jnp.bfloat16),
        new_values,
        preferred_element_type=jnp.float32,
    )
    key_span = min(CAP, 256)
    key_part = slot_cache[:, :kv_width]
    value_part = slot_cache[:, kv_width:]

    def visit(block_index, running_state):
        old_max, old_total, old_sum = running_state
        offset = block_index * key_span
        key_block = lax.dynamic_slice_in_dim(key_part, offset, key_span, 0).reshape(
            key_span, KVH, HD
        )
        value_block = lax.dynamic_slice_in_dim(value_part, offset, key_span, 0).reshape(
            key_span, KVH, HD
        )
        block_scores = (
            jnp.einsum("krd,jkd->krj", grouped, key_block, preferred_element_type=jnp.float32)
            * score_scale
        )
        in_cache = offset + jnp.arange(key_span, dtype=jnp.int32) < length
        block_scores = jnp.where(in_cache[None, None, :], block_scores, -jnp.inf)
        new_max = jnp.maximum(old_max, jnp.max(block_scores, axis=-1))
        rescale = jnp.exp(old_max - new_max)
        block_exp = jnp.exp(block_scores - new_max[..., None])
        new_total = old_total * rescale + jnp.sum(block_exp, axis=-1)
        new_sum = old_sum * rescale[..., None] + jnp.einsum(
            "krj,jkd->krd",
            block_exp.astype(jnp.bfloat16),
            value_block,
            preferred_element_type=jnp.float32,
        )
        return (new_max, new_total, new_sum)

    block_count = CAP // key_span
    row_max, row_total, running = lax.fori_loop(
        0, block_count, visit, (row_max, row_total, running)
    )
    result = running / row_total[..., None]
    return (
        result.reshape(KVH, STRETCH, GROUP, HD)
        .transpose(1, 0, 2, 3)
        .reshape(STRETCH, HQ * HD)
        .astype(jnp.bfloat16)
    )


def on_device(tokens, qkv_weight, qkv_bias, cache, lengths, slot_stream):
    my_index = lax.axis_index(("tp", "grp"))
    grp_index = lax.axis_index("grp")
    tp_count = lax.axis_size("tp")
    grp_count = lax.axis_size("grp")
    per_device = cache.shape[0]
    local_rows = per_device * STRETCH
    shard_cols = qkv_weight.shape[1]
    weight_cols = lax.all_gather(qkv_weight, "tp", axis=1, tiled=True)
    bias_table = qkv_bias.reshape(tp_count, grp_count, shard_cols)
    bias_cols = (
        lax.dynamic_index_in_dim(bias_table, grp_index, 1, keepdims=False)
        .reshape(-1)
        .astype(jnp.float32)
    )
    partial_cols = jnp.dot(
        lax.all_gather(tokens, "grp", axis=0, tiled=True),
        weight_cols,
        preferred_element_type=jnp.float32,
    )
    rounded_cols = (partial_cols + bias_cols[None, :]).astype(jnp.bfloat16)
    received = lax.all_to_all(rounded_cols, "grp", split_axis=0, concat_axis=1, tiled=True)
    projected_qkv = (
        received.reshape(local_rows, grp_count, tp_count, shard_cols)
        .transpose(0, 2, 1, 3)
        .reshape(local_rows, -1)
    )
    my_slots = my_index * per_device + jnp.arange(per_device, dtype=jnp.int32)
    my_lengths = jnp.take(lengths, jnp.take(slot_stream, my_slots))
    attended = jnp.concatenate(
        [
            attend(
                projected_qkv[slot_index * STRETCH : (slot_index + 1) * STRETCH],
                cache[slot_index],
                my_lengths[slot_index],
            )
            for slot_index in range(per_device)
        ],
        axis=0,
    )
    return attended


MESH = pl.DeviceIdType.MESH
LOG2E = 1.4426950408889634


def fused_kernel(
    n,
    groups,
    cols,
    tokens_ref,
    weight_ref,
    bias_ref,
    cache_ref,
    lengths_ref,
    streams_ref,
    freq_ref,
    out_ref,
    tok,
    weights,
    slots,
    bias,
    outgoing,
    incoming,
    cos_table,
    sin_table,
    tok_local,
    tok_send,
    tok_recv,
    part_send,
    part_recv,
    weight_sems,
    cache_sems,
    relay_sems,
    bias_all,
    partner_in,
):
    tp = lax.axis_index("tp")
    me = lax.axis_index("grp")
    chain = groups // 2
    depth = me // 2
    side = me % 2
    across = depth * 2 + 1 - side
    paired = depth + 1 - 2 * (depth % 2)
    width = tok.shape[3]
    split = width * 11 // 32 // HD * HD
    main = cols - HD // 2
    first_slot = (tp * groups + me) * n

    def local_tokens(c):
        return pltpu.make_async_copy(
            tokens_ref.at[pl.ds(pl.multiple_of(c * STRETCH, STRETCH), STRETCH)],
            tok.at[c, me],
            tok_local.at[c],
        )

    def cache_copy(c):
        return pltpu.make_async_copy(cache_ref.at[c], slots.at[c], cache_sems.at[c])

    def tok_copy(c, block, direction, target):
        return pltpu.make_async_remote_copy(
            src_ref=tok.at[c, block],
            dst_ref=tok.at[c, block],
            send_sem=tok_send.at[c, block, direction],
            recv_sem=tok_recv.at[c, block],
            device_id={"grp": target},
            device_id_type=MESH,
        )

    def rest_copy(c, block):
        part = tok.at[c, block, :, pl.ds(split, width - split)]
        return pltpu.make_async_remote_copy(
            src_ref=part,
            dst_ref=part,
            send_sem=tok_send.at[c, block, 2],
            recv_sem=tok_recv.at[c, block],
            device_id={"grp": across},
            device_id_type=MESH,
        )

    def relay_copy(c, level):
        part = tok.at[c, level * 2 + 1 - side, :, pl.ds(0, split)]
        return pltpu.make_async_remote_copy(
            src_ref=part,
            dst_ref=part,
            send_sem=relay_sems.at[c, 0],
            recv_sem=relay_sems.at[c, 1],
            device_id={"grp": paired * 2 + side},
            device_id_type=MESH,
        )

    def part_copy(c, peer):
        return pltpu.make_async_remote_copy(
            src_ref=outgoing.at[c, peer],
            dst_ref=incoming.at[c, me],
            send_sem=part_send.at[c, peer],
            recv_sem=part_recv.at[c, me],
            device_id={"grp": peer},
            device_id_type=MESH,
        )

    def part_arrival(c, peer):
        return pltpu.make_async_remote_copy(
            src_ref=outgoing.at[c, peer],
            dst_ref=incoming.at[c, peer],
            send_sem=part_send.at[c, peer],
            recv_sem=part_recv.at[c, peer],
            device_id={"grp": peer},
            device_id_type=MESH,
        )

    pieces = (
        (HD // 2 * side, main, (main + HD) * tp),
        (main * (1 - side), HD // 2, main + HD // 2 * ((tp + side) % 2)),
    )

    def weight_own(p):
        start, size, at = pieces[p]
        return pltpu.make_async_copy(
            weight_ref.at[pl.ds(pl.multiple_of(start, HD // 2), size)],
            weights.at[pl.ds(pl.multiple_of(at, HD // 2), size)],
            weight_sems.at[p, 0],
        )

    def weight_swap(p):
        start, size, at = pieces[p]
        return pltpu.make_async_remote_copy(
            src_ref=weight_ref.at[pl.ds(pl.multiple_of(start, HD // 2), size)],
            dst_ref=weights.at[pl.ds(pl.multiple_of(at, HD // 2), size)],
            send_sem=weight_sems.at[p, 1],
            recv_sem=weight_sems.at[p, 2],
            device_id={"tp": 1 - tp},
            device_id_type=MESH,
        )

    for c in range(n):
        local_tokens(c).start()

    for p in range(2):
        weight_own(p).start()
    for c in range(n):
        cache_copy(c).start()

    barrier = pltpu.get_barrier_semaphore()

    @pl.when(tp == 0)
    def _():
        pl.semaphore_signal(barrier, inc=1, device_id={"tp": 1 - tp}, device_id_type=MESH)

    for d in range(1, groups):
        pl.semaphore_signal(
            barrier, inc=1, device_id={"grp": lax.rem(me + d, groups)}, device_id_type=MESH
        )
    pl.semaphore_wait(barrier, groups - 1 + tp)

    @pl.when(tp == 1)
    def _():
        pl.semaphore_signal(partner_in, inc=1, device_id={"tp": 1 - tp}, device_id_type=MESH)

    def send_own(c):
        local_tokens(c).wait()
        tok_copy(c, me, 2, across).start()

        @pl.when(depth + 1 < chain)
        def _():
            tok_copy(c, me, 0, me + 2).start()

        @pl.when(depth >= 1)
        def _():
            tok_copy(c, me, 1, me - 2).start()

    def send_across(c, block, shared):
        @pl.when(shared)
        def _():
            rest_copy(c, block).start()

        @pl.when(jnp.logical_not(shared))
        def _():
            tok_copy(c, block, 2, across).start()

    def relay(c):
        tok_copy(c, across, 2, across).wait_recv()
        relay_copy(c, depth).start()

    def forward(c, s):
        @pl.when(depth >= s)
        def _():
            block = me - 2 * s
            tok_copy(c, block, 2, across).wait_recv()
            send_across(c, block, (s == 1) & (depth % 2 == 1))

            @pl.when(depth + 1 < chain)
            def _():
                tok_copy(c, block, 0, me + 2).start()

        @pl.when(depth + s < chain)
        def _():
            block = me + 2 * s
            tok_copy(c, block, 2, across).wait_recv()
            send_across(c, block, (s == 1) & (depth % 2 == 0))

            @pl.when(depth >= 1)
            def _():
                tok_copy(c, block, 1, me - 2).start()

    nt = (((1,), (1,)), ((), ()))

    def finish_sends(c):
        for level in range(chain):
            block = level * 2 + side

            @pl.when(level == paired)
            def _():
                rest_copy(c, block).wait_send()

            @pl.when(level != paired)
            def _():
                tok_copy(c, block, 2, across).wait_send()

            @pl.when((level <= depth) & (depth + 1 < chain))
            def _():
                tok_copy(c, block, 0, me + 2).wait_send()

            @pl.when((level >= depth) & (depth >= 1))
            def _():
                tok_copy(c, block, 1, me - 2).wait_send()

        relay_copy(c, depth).wait_send()
        for d in range(1, groups):
            part_copy(c, lax.rem(me + d, groups)).wait_send()

    def project(c):
        for level in range(chain):
            block = level * 2 + 1 - side

            @pl.when((level != paired) & (level != depth))
            def _():
                tok_copy(c, block, 2, across).wait_recv()

            @pl.when(level == paired)
            def _():
                rest_copy(c, block).wait_recv()
                relay_copy(c, level).wait_recv()

        rows = tok[c].reshape(groups * STRETCH, tok.shape[3])
        product = lax.dot_general(rows, weights[...], nt, preferred_element_type=jnp.float32)
        product = (product + bias[...]).astype(jnp.bfloat16)
        outgoing[c] = product.reshape(groups, STRETCH, 2 * cols)
        for d in range(1, groups):
            part_copy(c, lax.rem(me + d, groups)).start()
        incoming[c, me] = outgoing[c, me]

    lane = lax.broadcasted_iota(jnp.int32, (STRETCH, HD), 1)
    rows_all = STRETCH * GROUP
    pair_heads = 2 * cols // HD
    half = groups // 2 * pair_heads
    middle = pair_heads // 2

    def attention(c):
        for d in range(1, groups):
            part_arrival(c, lax.rem(me + d, groups)).wait_recv()
        cache_copy(c).wait()
        length = lengths_ref[streams_ref[first_slot + c]]
        cosine = cos_table[c]
        sine = sin_table[c]
        key_index = lax.broadcasted_iota(jnp.int32, (1, CAP), 1)
        in_cache = key_index < length
        new_index = lax.broadcasted_iota(jnp.int32, (rows_all, STRETCH), 1)
        new_token = lax.broadcasted_iota(jnp.int32, (rows_all, STRETCH), 0) % STRETCH
        causal = new_index <= new_token
        factor = HD ** (-0.5) * LOG2E

        def head(i):
            t, rest = divmod(i, half)
            pair, k = divmod(rest, pair_heads)
            if k != middle:
                block, at = (2 * pair, k) if k < middle else (2 * pair + 1, k - middle - 1)
                at = at * HD + t * (main + HD)
                return incoming[c, block, :, at : at + HD]
            left = incoming[c, 2 * pair, :, main : main + HD].astype(jnp.float32)
            right = incoming[c, 2 * pair + 1, :, main : main + HD].astype(jnp.float32)
            if t == 0:
                joined = jnp.where(lane < HD // 2, left, right)
            else:
                joined = pltpu.roll(jnp.where(lane < HD // 2, right, left), HD // 2, 1)
            return joined.astype(jnp.bfloat16)

        def rotated(i):
            u = head(i).astype(jnp.float32)
            return (u * cosine + pltpu.roll(u, HD // 2, 1) * sine).astype(jnp.bfloat16)

        for k in range(KVH):
            queries = jnp.concatenate([rotated(k * GROUP + g) for g in range(GROUP)], axis=0)
            new_keys = rotated(HQ + k)
            new_values = head(HQ + KVH + k)
            keys = slots[c, :, k * HD : (k + 1) * HD]
            values = slots[c, :, (KVH + k) * HD : (KVH + k + 1) * HD]
            scores = lax.dot_general(queries, keys, nt, preferred_element_type=jnp.float32)
            scores = jnp.where(in_cache, scores, -jnp.inf)
            new_scores = lax.dot_general(queries, new_keys, nt, preferred_element_type=jnp.float32)
            new_scores = jnp.where(causal, new_scores, -jnp.inf)
            top = jnp.maximum(
                jnp.max(scores, axis=-1, keepdims=True), jnp.max(new_scores, axis=-1, keepdims=True)
            )
            probs = jnp.exp2((scores - top) * factor)
            new_probs = jnp.exp2((new_scores - top) * factor)
            total = jnp.sum(probs, axis=-1, keepdims=True) + jnp.sum(
                new_probs, axis=-1, keepdims=True
            )
            summed = jnp.dot(
                probs.astype(jnp.bfloat16), values, preferred_element_type=jnp.float32
            ) + jnp.dot(
                new_probs.astype(jnp.bfloat16), new_values, preferred_element_type=jnp.float32
            )
            result = (summed / total).astype(jnp.bfloat16)
            for g in range(GROUP):
                h = k * GROUP + g
                out_ref[
                    pl.ds(pl.multiple_of(c * STRETCH, STRETCH), STRETCH), h * HD : (h + 1) * HD
                ] = result[g * STRETCH : (g + 1) * STRETCH]

    send_own(0)

    @pl.when(tp == 1)
    def _():
        for p in range(2):
            weight_swap(p).start()

    for start in range(0, bias_ref.shape[0], 2 * HD):
        piece = bias_ref[start : start + 2 * HD].astype(jnp.float32)
        bias_all[:, start : start + 2 * HD] = piece.reshape(1, 2 * HD)

    first_head = depth * pair_heads

    def bias_heads(start, count):
        at = pl.multiple_of(start * HD, HD)
        return bias_all[:, pl.ds(at, count * HD)]

    for t in range(2):
        whole = bias_heads(t * half + first_head + (middle + 1) * side, middle)
        bias[:, t * (main + HD) : t * (main + HD) + main] = whole
    joint = [bias_heads(t * half + first_head + middle, 1) for t in range(2)]
    front = lax.broadcasted_iota(jnp.int32, (1, HD), 1) // (HD // 2) == side
    bias[:, main : main + HD] = jnp.where(front, joint[0], pltpu.roll(joint[1], HD // 2, 1))

    sign = jnp.where(lane < HD // 2, -1.0, 1.0)
    token = lax.broadcasted_iota(jnp.int32, (STRETCH, HD), 0)
    for c in range(n):
        length = lengths_ref[streams_ref[first_slot + c]]
        angles = (length + token).astype(jnp.float32) * freq_ref[...]
        cos_table[c] = jnp.cos(angles)
        sin_table[c] = jnp.sin(angles) * sign

    @pl.loop(0, n + 3)
    def _(i):
        @pl.when(i < n)
        def _():
            forward(i, 1)

        @pl.when(i + 1 < n)
        def _():
            send_own(i + 1)

        @pl.when((i == 0) & (tp == 0))
        def _():
            pl.semaphore_wait(partner_in, 1)
            for p in range(2):
                weight_swap(p).start()

        @pl.when(((i >= 2) & (i < n)) | ((i > n) & (i >= 3)))
        def _():
            attention(jnp.where(i < n, i - 2, i - 3))

        @pl.when(i < n)
        def _():
            relay(i)
            for s in range(2, chain - 1):
                forward(i, s)

        @pl.when(i == 1)
        def _():
            for p in range(2):
                weight_own(p).wait()
                weight_swap(p).wait()

        @pl.when((i >= 1) & (i < n + 1))
        def _():
            project(i - 1)

        @pl.when(i < n)
        def _():
            forward(i, chain - 1)

    @pl.loop(0, n)
    def _(c):
        finish_sends(c)


def fused(tokens, qkv_weight, qkv_bias, cache, lengths, slot_stream):
    groups = lax.axis_size("grp")
    n = cache.shape[0]
    width, cols = qkv_weight.shape
    frequency = ROPE_THETA ** (-(np.arange(HD // 2) * 2.0) / HD)
    frequency = np.concatenate([frequency, frequency])[None, :].astype(np.float32)
    anywhere = pl.BlockSpec(memory_space=pl.ANY)
    vmem = pl.BlockSpec(memory_space=pltpu.VMEM)
    smem = pl.BlockSpec(memory_space=pltpu.SMEM)
    dma = pltpu.SemaphoreType.DMA
    rows = groups * STRETCH
    attention_ops = 4 * n * KVH * STRETCH * GROUP * CAP * HD
    return pl.pallas_call(
        functools.partial(fused_kernel, n, groups, cols),
        out_shape=pltpu.VMEM((n * STRETCH, HQ * HD), jnp.bfloat16),
        in_specs=[anywhere, anywhere, vmem, anywhere, smem, smem, vmem],
        out_specs=vmem,
        scratch_shapes=[
            pltpu.VMEM((n, groups, STRETCH, width), jnp.bfloat16),
            pltpu.VMEM((2 * cols, width), jnp.bfloat16),
            pltpu.VMEM(cache.shape, jnp.bfloat16),
            pltpu.VMEM((1, 2 * cols), jnp.float32),
            pltpu.VMEM((n, groups, STRETCH, 2 * cols), jnp.bfloat16),
            pltpu.VMEM((n, groups, STRETCH, 2 * cols), jnp.bfloat16),
            pltpu.VMEM((n, STRETCH, HD), jnp.float32),
            pltpu.VMEM((n, STRETCH, HD), jnp.float32),
            dma((n,)),
            dma((n, groups, 3)),
            dma((n, groups)),
            dma((n, groups)),
            dma((n, groups)),
            dma((2, 3)),
            dma((n,)),
            dma((n, 2)),
            pltpu.VMEM((1, qkv_bias.shape[0]), jnp.float32),
            pltpu.SemaphoreType.REGULAR,
        ],
        compiler_params=pltpu.CompilerParams(
            collective_id=0, has_side_effects=True, vmem_limit_bytes=56 * 2**20
        ),
        cost_estimate=pl.CostEstimate(
            flops=4 * n * rows * width * cols + attention_ops,
            bytes_accessed=2 * (cache.size + 2 * qkv_weight.size),
            transcendentals=n * KVH * STRETCH * GROUP * CAP,
        ),
    )(tokens, qkv_weight.T, qkv_bias, cache, lengths, slot_stream, jnp.asarray(frequency))


def solution(mesh):
    def program(tokens, qkv_weight, qkv_bias, cache, lengths, slot_stream):
        cols = qkv_weight.shape[1]
        groups = lax.axis_size("grp")
        fits = lax.axis_size("tp") == 2 and groups % 4 == 0 and cols % HD == HD // 2
        body = fused if fits else on_device
        return body(tokens, qkv_weight, qkv_bias, cache, lengths, slot_stream)

    in_specs = (
        P(("rep", "tp", "grp"), None),
        P(None, ("tp", "grp")),
        P(),
        P(("rep", "tp", "grp"), None, None),
        P("rep"),
        P("rep"),
    )
    out_specs = P(("rep", "tp", "grp"), None)
    return jax.shard_map(
        program, mesh=mesh, in_specs=in_specs, out_specs=out_specs, check_vma=False
    )
```

```python
import functools

import jax
import jax.numpy as jnp
import numpy as np
from jax import lax
from jax.experimental import pallas as pl
from jax.experimental.pallas import tpu as pltpu
from jax.sharding import PartitionSpec as P

HD = 128
HQ = 32
KVH = 4
STRETCH = 16
CAP = 1024
GROUP = 8


ROPE_THETA = 1000000.0


def rotate(vectors, positions):
    half_width = vectors.shape[-1] // 2
    frequency = ROPE_THETA ** (
        -(jnp.arange(half_width, dtype=jnp.float32) * 2.0) / vectors.shape[-1]
    )
    angles = positions.astype(jnp.float32)[:, None] * frequency[None, :]
    cosine = jnp.cos(angles)[:, None, :]
    sine_part = jnp.sin(angles)[:, None, :]
    front_half = vectors[..., :half_width]
    back_half = vectors[..., half_width:]
    return jnp.concatenate(
        [front_half * cosine - back_half * sine_part, back_half * cosine + front_half * sine_part],
        axis=-1,
    )


def attend(token_block, slot_cache, length):
    query_width = HQ * HD
    kv_width = KVH * HD
    positions = length + jnp.arange(STRETCH, dtype=jnp.int32)
    queries = rotate(
        token_block[:, :query_width].astype(jnp.float32).reshape(STRETCH, HQ, HD), positions
    ).astype(jnp.bfloat16)
    new_keys = rotate(
        token_block[:, query_width : query_width + kv_width]
        .astype(jnp.float32)
        .reshape(STRETCH, KVH, HD),
        positions,
    ).astype(jnp.bfloat16)
    new_values = token_block[:, query_width + kv_width :].reshape(STRETCH, KVH, HD)
    grouped = (
        queries.reshape(STRETCH, KVH, GROUP, HD)
        .transpose(1, 0, 2, 3)
        .reshape(KVH, STRETCH * GROUP, HD)
    )
    score_scale = HD ** (-0.5)
    query_token = jnp.arange(STRETCH * GROUP, dtype=jnp.int32) // GROUP
    scores = (
        jnp.einsum("krd,jkd->krj", grouped, new_keys, preferred_element_type=jnp.float32)
        * score_scale
    )
    causal = jnp.arange(STRETCH, dtype=jnp.int32)[None, :] <= query_token[:, None]
    scores = jnp.where(causal[None], scores, -jnp.inf)
    row_max = jnp.max(scores, axis=-1)
    exponent = jnp.exp(scores - row_max[..., None])
    row_total = jnp.sum(exponent, axis=-1)
    running = jnp.einsum(
        "krj,jkd->krd",
        exponent.astype(jnp.bfloat16),
        new_values,
        preferred_element_type=jnp.float32,
    )
    key_span = min(CAP, 256)
    key_part = slot_cache[:, :kv_width]
    value_part = slot_cache[:, kv_width:]

    def visit(block_index, running_state):
        old_max, old_total, old_sum = running_state
        offset = block_index * key_span
        key_block = lax.dynamic_slice_in_dim(key_part, offset, key_span, 0).reshape(
            key_span, KVH, HD
        )
        value_block = lax.dynamic_slice_in_dim(value_part, offset, key_span, 0).reshape(
            key_span, KVH, HD
        )
        block_scores = (
            jnp.einsum("krd,jkd->krj", grouped, key_block, preferred_element_type=jnp.float32)
            * score_scale
        )
        in_cache = offset + jnp.arange(key_span, dtype=jnp.int32) < length
        block_scores = jnp.where(in_cache[None, None, :], block_scores, -jnp.inf)
        new_max = jnp.maximum(old_max, jnp.max(block_scores, axis=-1))
        rescale = jnp.exp(old_max - new_max)
        block_exp = jnp.exp(block_scores - new_max[..., None])
        new_total = old_total * rescale + jnp.sum(block_exp, axis=-1)
        new_sum = old_sum * rescale[..., None] + jnp.einsum(
            "krj,jkd->krd",
            block_exp.astype(jnp.bfloat16),
            value_block,
            preferred_element_type=jnp.float32,
        )
        return (new_max, new_total, new_sum)

    block_count = CAP // key_span
    row_max, row_total, running = lax.fori_loop(
        0, block_count, visit, (row_max, row_total, running)
    )
    result = running / row_total[..., None]
    return (
        result.reshape(KVH, STRETCH, GROUP, HD)
        .transpose(1, 0, 2, 3)
        .reshape(STRETCH, HQ * HD)
        .astype(jnp.bfloat16)
    )


def on_device(tokens, qkv_weight, qkv_bias, cache, lengths, slot_stream):
    my_index = lax.axis_index(("tp", "grp"))
    grp_index = lax.axis_index("grp")
    tp_count = lax.axis_size("tp")
    grp_count = lax.axis_size("grp")
    per_device = cache.shape[0]
    local_rows = per_device * STRETCH
    shard_cols = qkv_weight.shape[1]
    weight_cols = lax.all_gather(qkv_weight, "tp", axis=1, tiled=True)
    bias_table = qkv_bias.reshape(tp_count, grp_count, shard_cols)
    bias_cols = (
        lax.dynamic_index_in_dim(bias_table, grp_index, 1, keepdims=False)
        .reshape(-1)
        .astype(jnp.float32)
    )
    partial_cols = jnp.dot(
        lax.all_gather(tokens, "grp", axis=0, tiled=True),
        weight_cols,
        preferred_element_type=jnp.float32,
    )
    rounded_cols = (partial_cols + bias_cols[None, :]).astype(jnp.bfloat16)
    received = lax.all_to_all(rounded_cols, "grp", split_axis=0, concat_axis=1, tiled=True)
    projected_qkv = (
        received.reshape(local_rows, grp_count, tp_count, shard_cols)
        .transpose(0, 2, 1, 3)
        .reshape(local_rows, -1)
    )
    my_slots = my_index * per_device + jnp.arange(per_device, dtype=jnp.int32)
    my_lengths = jnp.take(lengths, jnp.take(slot_stream, my_slots))
    attended = jnp.concatenate(
        [
            attend(
                projected_qkv[slot_index * STRETCH : (slot_index + 1) * STRETCH],
                cache[slot_index],
                my_lengths[slot_index],
            )
            for slot_index in range(per_device)
        ],
        axis=0,
    )
    return attended


MESH = pl.DeviceIdType.MESH
LOG2E = 1.4426950408889634
AHEAD = 2


def fused_kernel(
    n,
    groups,
    cols,
    tokens_ref,
    weight_ref,
    bias_ref,
    cache_ref,
    lengths_ref,
    streams_ref,
    freq_ref,
    out_ref,
    tok,
    weights,
    slots,
    bias,
    outgoing,
    incoming,
    cos_table,
    sin_table,
    tok_local,
    tok_send,
    tok_recv,
    part_send,
    part_recv,
    weight_sems,
    cache_sems,
    relay_sems,
    bias_all,
    partner_in,
    partial,
):
    tp = lax.axis_index("tp")
    me = lax.axis_index("grp")
    chain = groups // 2
    depth = me // 2
    side = me % 2
    across = depth * 2 + 1 - side
    paired = depth + 1 - 2 * (depth % 2)
    width = tok.shape[3]
    split = width * 11 // 32 // HD * HD
    main = cols - HD // 2
    first_slot = (tp * groups + me) * n

    def local_tokens(c):
        return pltpu.make_async_copy(
            tokens_ref.at[
                pl.ds(pl.multiple_of(c // 2 * STRETCH, STRETCH), STRETCH),
                pl.ds(pl.multiple_of(c % 2 * width, HD), width),
            ],
            tok.at[c, me],
            tok_local.at[c],
        )

    def cache_copy(c):
        return pltpu.make_async_copy(cache_ref.at[c], slots.at[c], cache_sems.at[c])

    def tok_copy(c, block, direction, target):
        return pltpu.make_async_remote_copy(
            src_ref=tok.at[c, block],
            dst_ref=tok.at[c, block],
            send_sem=tok_send.at[c, block, direction],
            recv_sem=tok_recv.at[c, block],
            device_id={"grp": target},
            device_id_type=MESH,
        )

    def rest_copy(c, block):
        part = tok.at[c, block, :, pl.ds(split, width - split)]
        return pltpu.make_async_remote_copy(
            src_ref=part,
            dst_ref=part,
            send_sem=tok_send.at[c, block, 2],
            recv_sem=tok_recv.at[c, block],
            device_id={"grp": across},
            device_id_type=MESH,
        )

    def relay_copy(c, level):
        part = tok.at[c, level * 2 + 1 - side, :, pl.ds(0, split)]
        return pltpu.make_async_remote_copy(
            src_ref=part,
            dst_ref=part,
            send_sem=relay_sems.at[c, 0],
            recv_sem=relay_sems.at[c, 1],
            device_id={"grp": paired * 2 + side},
            device_id_type=MESH,
        )

    def part_copy(c, peer):
        return pltpu.make_async_remote_copy(
            src_ref=outgoing.at[c, peer],
            dst_ref=incoming.at[c, me],
            send_sem=part_send.at[c, peer],
            recv_sem=part_recv.at[c, me],
            device_id={"grp": peer},
            device_id_type=MESH,
        )

    def part_arrival(c, peer):
        return pltpu.make_async_remote_copy(
            src_ref=outgoing.at[c, peer],
            dst_ref=incoming.at[c, peer],
            send_sem=part_send.at[c, peer],
            recv_sem=part_recv.at[c, peer],
            device_id={"grp": peer},
            device_id_type=MESH,
        )

    pieces = (
        (HD // 2 * side, main, (main + HD) * tp),
        (main * (1 - side), HD // 2, main + HD // 2 * ((tp + side) % 2)),
    )

    def weight_own(q):
        p, h = divmod(q, 2)
        start, size, at = pieces[p]
        return pltpu.make_async_copy(
            weight_ref.at[pl.ds(pl.multiple_of(start, HD // 2), size), pl.ds(h * width, width)],
            weights.at[h, pl.ds(pl.multiple_of(at, HD // 2), size)],
            weight_sems.at[q, 0],
        )

    def weight_swap(q):
        p, h = divmod(q, 2)
        start, size, at = pieces[p]
        return pltpu.make_async_remote_copy(
            src_ref=weight_ref.at[pl.ds(pl.multiple_of(start, HD // 2), size), pl.ds(h * width, width)],
            dst_ref=weights.at[h, pl.ds(pl.multiple_of(at, HD // 2), size)],
            send_sem=weight_sems.at[q, 1],
            recv_sem=weight_sems.at[q, 2],
            device_id={"tp": 1 - tp},
            device_id_type=MESH,
        )

    for c in range(2 * n):
        local_tokens(c).start()

    for p in range(4):
        weight_own(p).start()
    for c in range(n):
        cache_copy(c).start()

    barrier = pltpu.get_barrier_semaphore()

    @pl.when(tp == 0)
    def _():
        pl.semaphore_signal(barrier, inc=1, device_id={"tp": 1 - tp}, device_id_type=MESH)

    for d in range(1, groups):
        pl.semaphore_signal(
            barrier, inc=1, device_id={"grp": lax.rem(me + d, groups)}, device_id_type=MESH
        )
    pl.semaphore_wait(barrier, groups - 1 + tp)

    @pl.when(tp == 1)
    def _():
        pl.semaphore_signal(partner_in, inc=1, device_id={"tp": 1 - tp}, device_id_type=MESH)

    def send_own(c):
        local_tokens(c).wait()
        tok_copy(c, me, 2, across).start()

        @pl.when(depth + 1 < chain)
        def _():
            tok_copy(c, me, 0, me + 2).start()

        @pl.when(depth >= 1)
        def _():
            tok_copy(c, me, 1, me - 2).start()

    def send_across(c, block, shared):
        @pl.when(shared)
        def _():
            rest_copy(c, block).start()

        @pl.when(jnp.logical_not(shared))
        def _():
            tok_copy(c, block, 2, across).start()

    def relay(c):
        tok_copy(c, across, 2, across).wait_recv()
        relay_copy(c, depth).start()

    def forward(c, s):
        @pl.when(depth >= s)
        def _():
            block = me - 2 * s
            tok_copy(c, block, 2, across).wait_recv()
            send_across(c, block, (s == 1) & (depth % 2 == 1))

            @pl.when(depth + 1 < chain)
            def _():
                tok_copy(c, block, 0, me + 2).start()

        @pl.when(depth + s < chain)
        def _():
            block = me + 2 * s
            tok_copy(c, block, 2, across).wait_recv()
            send_across(c, block, (s == 1) & (depth % 2 == 0))

            @pl.when(depth >= 1)
            def _():
                tok_copy(c, block, 1, me - 2).start()

    nt = (((1,), (1,)), ((), ()))

    def finish_sends(c):
        for level in range(chain):
            block = level * 2 + side

            @pl.when(level == paired)
            def _():
                rest_copy(c, block).wait_send()

            @pl.when(level != paired)
            def _():
                tok_copy(c, block, 2, across).wait_send()

            @pl.when((level <= depth) & (depth + 1 < chain))
            def _():
                tok_copy(c, block, 0, me + 2).wait_send()

            @pl.when((level >= depth) & (depth >= 1))
            def _():
                tok_copy(c, block, 1, me - 2).wait_send()

        relay_copy(c, depth).wait_send()

    def project(c):
        for level in range(chain):
            block = level * 2 + 1 - side

            @pl.when((level != paired) & (level != depth))
            def _():
                tok_copy(c, block, 2, across).wait_recv()

            @pl.when(level == paired)
            def _():
                rest_copy(c, block).wait_recv()
                relay_copy(c, level).wait_recv()

        rows = tok[c].reshape(groups * STRETCH, width)
        product = lax.dot_general(rows, weights[c % 2], nt, preferred_element_type=jnp.float32)

        @pl.when(c % 2 == 0)
        def _():
            partial[...] = product + bias[...]

        @pl.when(c % 2 == 1)
        def _():
            slot = c // 2
            full = (partial[...] + product).astype(jnp.bfloat16)
            outgoing[slot] = full.reshape(groups, STRETCH, 2 * cols)
            for d in range(1, groups):
                part_copy(slot, lax.rem(me + d, groups)).start()
            incoming[slot, me] = outgoing[slot, me]

    lane = lax.broadcasted_iota(jnp.int32, (STRETCH, HD), 1)
    rows_all = STRETCH * GROUP
    pair_heads = 2 * cols // HD
    half = groups // 2 * pair_heads
    middle = pair_heads // 2

    def arrive(c):
        for d in range(1, groups):
            part_arrival(c, lax.rem(me + d, groups)).wait_recv()
        cache_copy(c).wait()

    def attention(c, key_heads):
        length = lengths_ref[streams_ref[first_slot + c]]
        cosine = cos_table[c]
        sine = sin_table[c]
        key_index = lax.broadcasted_iota(jnp.int32, (1, CAP), 1)
        in_cache = key_index < length
        new_index = lax.broadcasted_iota(jnp.int32, (rows_all, STRETCH), 1)
        new_token = lax.broadcasted_iota(jnp.int32, (rows_all, STRETCH), 0) % STRETCH
        causal = new_index <= new_token
        factor = HD ** (-0.5) * LOG2E

        def head(i):
            t, rest = divmod(i, half)
            pair, k = divmod(rest, pair_heads)
            if k != middle:
                block, at = (2 * pair, k) if k < middle else (2 * pair + 1, k - middle - 1)
                at = at * HD + t * (main + HD)
                return incoming[c, block, :, at : at + HD]
            left = incoming[c, 2 * pair, :, main : main + HD].astype(jnp.float32)
            right = incoming[c, 2 * pair + 1, :, main : main + HD].astype(jnp.float32)
            if t == 0:
                joined = jnp.where(lane < HD // 2, left, right)
            else:
                joined = pltpu.roll(jnp.where(lane < HD // 2, right, left), HD // 2, 1)
            return joined.astype(jnp.bfloat16)

        def rotated(i):
            u = head(i).astype(jnp.float32)
            return (u * cosine + pltpu.roll(u, HD // 2, 1) * sine).astype(jnp.bfloat16)

        for k in key_heads:
            queries = jnp.concatenate([rotated(k * GROUP + g) for g in range(GROUP)], axis=0)
            new_keys = rotated(HQ + k)
            new_values = head(HQ + KVH + k)
            keys = slots[c, :, k * HD : (k + 1) * HD]
            values = slots[c, :, (KVH + k) * HD : (KVH + k + 1) * HD]
            scores = lax.dot_general(queries, keys, nt, preferred_element_type=jnp.float32)
            scores = jnp.where(in_cache, scores, -jnp.inf)
            new_scores = lax.dot_general(queries, new_keys, nt, preferred_element_type=jnp.float32)
            new_scores = jnp.where(causal, new_scores, -jnp.inf)
            top = jnp.maximum(
                jnp.max(scores, axis=-1, keepdims=True), jnp.max(new_scores, axis=-1, keepdims=True)
            )
            probs = jnp.exp2((scores - top) * factor)
            new_probs = jnp.exp2((new_scores - top) * factor)
            total = jnp.sum(probs, axis=-1, keepdims=True) + jnp.sum(
                new_probs, axis=-1, keepdims=True
            )
            summed = jnp.dot(
                probs.astype(jnp.bfloat16), values, preferred_element_type=jnp.float32
            ) + jnp.dot(
                new_probs.astype(jnp.bfloat16), new_values, preferred_element_type=jnp.float32
            )
            result = (summed / total).astype(jnp.bfloat16)
            for g in range(GROUP):
                h = k * GROUP + g
                out_ref[
                    pl.ds(pl.multiple_of(c * STRETCH, STRETCH), STRETCH), h * HD : (h + 1) * HD
                ] = result[g * STRETCH : (g + 1) * STRETCH]

    for c in range(AHEAD):
        send_own(c)

    @pl.when(tp == 1)
    def _():
        for p in range(4):
            weight_swap(p).start()

    for start in range(0, bias_ref.shape[0], 2 * HD):
        piece = bias_ref[start : start + 2 * HD].astype(jnp.float32)
        bias_all[:, start : start + 2 * HD] = piece.reshape(1, 2 * HD)

    first_head = depth * pair_heads

    def bias_heads(start, count):
        at = pl.multiple_of(start * HD, HD)
        return bias_all[:, pl.ds(at, count * HD)]

    for t in range(2):
        whole = bias_heads(t * half + first_head + (middle + 1) * side, middle)
        bias[:, t * (main + HD) : t * (main + HD) + main] = whole
    joint = [bias_heads(t * half + first_head + middle, 1) for t in range(2)]
    front = lax.broadcasted_iota(jnp.int32, (1, HD), 1) // (HD // 2) == side
    bias[:, main : main + HD] = jnp.where(front, joint[0], pltpu.roll(joint[1], HD // 2, 1))

    sign = jnp.where(lane < HD // 2, -1.0, 1.0)
    token = lax.broadcasted_iota(jnp.int32, (STRETCH, HD), 0)
    for c in range(n):
        length = lengths_ref[streams_ref[first_slot + c]]
        angles = (length + token).astype(jnp.float32) * freq_ref[...]
        cos_table[c] = jnp.cos(angles)
        sin_table[c] = jnp.sin(angles) * sign

    def stage(i, low, body):
        pl.when((i >= low) & (i < 2 * n + low))(lambda: body(i - low))

    @pl.loop(0, 2 * n + chain + 1)
    def _(i):
        for s in range(1, chain):
            stage(i, s - 1, functools.partial(forward, s=s))
        stage(i, 1, relay)

        @pl.when(i + AHEAD < 2 * n)
        def _():
            send_own(i + AHEAD)

        @pl.when((i == 0) & (tp == 0))
        def _():
            pl.semaphore_wait(partner_in, 1)
            for p in range(4):
                weight_swap(p).start()

        @pl.when(i == chain - 1)
        def _():
            for p in range(4):
                weight_own(p).wait()
                weight_swap(p).wait()

        stage(i, chain - 1, project)

        def first_heads(c):
            @pl.when(c % 2 == 0)
            def _():
                arrive(c // 2)
                attention(c // 2, range(KVH // 2))

        def other_heads(c):
            @pl.when(c % 2 == 1)
            def _():
                attention(c // 2, range(KVH // 2, KVH))

        stage(i, chain + 1, lambda c: (first_heads(c), other_heads(c)) and None)

    @pl.loop(0, 2 * n)
    def _(c):
        finish_sends(c)

    @pl.loop(0, n)
    def _(c):
        for d in range(1, groups):
            part_copy(c, lax.rem(me + d, groups)).wait_send()


def fused(tokens, qkv_weight, qkv_bias, cache, lengths, slot_stream):
    groups = lax.axis_size("grp")
    n = cache.shape[0]
    width, cols = qkv_weight.shape
    frequency = ROPE_THETA ** (-(np.arange(HD // 2) * 2.0) / HD)
    frequency = np.concatenate([frequency, frequency])[None, :].astype(np.float32)
    anywhere = pl.BlockSpec(memory_space=pl.ANY)
    vmem = pl.BlockSpec(memory_space=pltpu.VMEM)
    smem = pl.BlockSpec(memory_space=pltpu.SMEM)
    dma = pltpu.SemaphoreType.DMA
    rows = groups * STRETCH
    attention_ops = 4 * n * KVH * STRETCH * GROUP * CAP * HD
    return pl.pallas_call(
        functools.partial(fused_kernel, n, groups, cols),
        out_shape=pltpu.VMEM((n * STRETCH, HQ * HD), jnp.bfloat16),
        in_specs=[anywhere, anywhere, vmem, anywhere, smem, smem, vmem],
        out_specs=vmem,
        scratch_shapes=[
            pltpu.VMEM((2 * n, groups, STRETCH, width // 2), jnp.bfloat16),
            pltpu.VMEM((2, 2 * cols, width // 2), jnp.bfloat16),
            pltpu.VMEM(cache.shape, jnp.bfloat16),
            pltpu.VMEM((1, 2 * cols), jnp.float32),
            pltpu.VMEM((n, groups, STRETCH, 2 * cols), jnp.bfloat16),
            pltpu.VMEM((n, groups, STRETCH, 2 * cols), jnp.bfloat16),
            pltpu.VMEM((n, STRETCH, HD), jnp.float32),
            pltpu.VMEM((n, STRETCH, HD), jnp.float32),
            dma((2 * n,)),
            dma((2 * n, groups, 3)),
            dma((2 * n, groups)),
            dma((n, groups)),
            dma((n, groups)),
            dma((4, 3)),
            dma((n,)),
            dma((2 * n, 2)),
            pltpu.VMEM((1, qkv_bias.shape[0]), jnp.float32),
            pltpu.SemaphoreType.REGULAR,
            pltpu.VMEM((rows, 2 * cols), jnp.float32),
        ],
        compiler_params=pltpu.CompilerParams(
            collective_id=0, has_side_effects=True, vmem_limit_bytes=56 * 2**20
        ),
        cost_estimate=pl.CostEstimate(
            flops=4 * n * rows * width * cols + attention_ops,
            bytes_accessed=2 * (cache.size + 2 * qkv_weight.size),
            transcendentals=n * KVH * STRETCH * GROUP * CAP,
        ),
    )(tokens, qkv_weight.T, qkv_bias, cache, lengths, slot_stream, jnp.asarray(frequency))


def solution(mesh):
    def program(tokens, qkv_weight, qkv_bias, cache, lengths, slot_stream):
        cols = qkv_weight.shape[1]
        groups = lax.axis_size("grp")
        fits = lax.axis_size("tp") == 2 and groups % 4 == 0 and cols % HD == HD // 2
        body = fused if fits else on_device
        return body(tokens, qkv_weight, qkv_bias, cache, lengths, slot_stream)

    in_specs = (
        P(("rep", "tp", "grp"), None),
        P(None, ("tp", "grp")),
        P(),
        P(("rep", "tp", "grp"), None, None),
        P("rep"),
        P("rep"),
    )
    out_specs = P(("rep", "tp", "grp"), None)
    return jax.shard_map(
        program, mesh=mesh, in_specs=in_specs, out_specs=out_specs, check_vma=False
    )
```

```python
import functools

import jax
import jax.numpy as jnp
import numpy as np
from jax import lax
from jax.experimental import pallas as pl
from jax.experimental.pallas import tpu as pltpu
from jax.sharding import PartitionSpec as P

HD = 128
HQ = 32
KVH = 4
STRETCH = 16
CAP = 1024
GROUP = 8


ROPE_THETA = 1000000.0


def rotate(vectors, positions):
    half_width = vectors.shape[-1] // 2
    frequency = ROPE_THETA ** (
        -(jnp.arange(half_width, dtype=jnp.float32) * 2.0) / vectors.shape[-1]
    )
    angles = positions.astype(jnp.float32)[:, None] * frequency[None, :]
    cosine = jnp.cos(angles)[:, None, :]
    sine_part = jnp.sin(angles)[:, None, :]
    front_half = vectors[..., :half_width]
    back_half = vectors[..., half_width:]
    return jnp.concatenate(
        [front_half * cosine - back_half * sine_part, back_half * cosine + front_half * sine_part],
        axis=-1,
    )


def attend(token_block, slot_cache, length):
    query_width = HQ * HD
    kv_width = KVH * HD
    positions = length + jnp.arange(STRETCH, dtype=jnp.int32)
    queries = rotate(
        token_block[:, :query_width].astype(jnp.float32).reshape(STRETCH, HQ, HD), positions
    ).astype(jnp.bfloat16)
    new_keys = rotate(
        token_block[:, query_width : query_width + kv_width]
        .astype(jnp.float32)
        .reshape(STRETCH, KVH, HD),
        positions,
    ).astype(jnp.bfloat16)
    new_values = token_block[:, query_width + kv_width :].reshape(STRETCH, KVH, HD)
    grouped = (
        queries.reshape(STRETCH, KVH, GROUP, HD)
        .transpose(1, 0, 2, 3)
        .reshape(KVH, STRETCH * GROUP, HD)
    )
    score_scale = HD ** (-0.5)
    query_token = jnp.arange(STRETCH * GROUP, dtype=jnp.int32) // GROUP
    scores = (
        jnp.einsum("krd,jkd->krj", grouped, new_keys, preferred_element_type=jnp.float32)
        * score_scale
    )
    causal = jnp.arange(STRETCH, dtype=jnp.int32)[None, :] <= query_token[:, None]
    scores = jnp.where(causal[None], scores, -jnp.inf)
    row_max = jnp.max(scores, axis=-1)
    exponent = jnp.exp(scores - row_max[..., None])
    row_total = jnp.sum(exponent, axis=-1)
    running = jnp.einsum(
        "krj,jkd->krd",
        exponent.astype(jnp.bfloat16),
        new_values,
        preferred_element_type=jnp.float32,
    )
    key_span = min(CAP, 256)
    key_part = slot_cache[:, :kv_width]
    value_part = slot_cache[:, kv_width:]

    def visit(block_index, running_state):
        old_max, old_total, old_sum = running_state
        offset = block_index * key_span
        key_block = lax.dynamic_slice_in_dim(key_part, offset, key_span, 0).reshape(
            key_span, KVH, HD
        )
        value_block = lax.dynamic_slice_in_dim(value_part, offset, key_span, 0).reshape(
            key_span, KVH, HD
        )
        block_scores = (
            jnp.einsum("krd,jkd->krj", grouped, key_block, preferred_element_type=jnp.float32)
            * score_scale
        )
        in_cache = offset + jnp.arange(key_span, dtype=jnp.int32) < length
        block_scores = jnp.where(in_cache[None, None, :], block_scores, -jnp.inf)
        new_max = jnp.maximum(old_max, jnp.max(block_scores, axis=-1))
        rescale = jnp.exp(old_max - new_max)
        block_exp = jnp.exp(block_scores - new_max[..., None])
        new_total = old_total * rescale + jnp.sum(block_exp, axis=-1)
        new_sum = old_sum * rescale[..., None] + jnp.einsum(
            "krj,jkd->krd",
            block_exp.astype(jnp.bfloat16),
            value_block,
            preferred_element_type=jnp.float32,
        )
        return (new_max, new_total, new_sum)

    block_count = CAP // key_span
    row_max, row_total, running = lax.fori_loop(
        0, block_count, visit, (row_max, row_total, running)
    )
    result = running / row_total[..., None]
    return (
        result.reshape(KVH, STRETCH, GROUP, HD)
        .transpose(1, 0, 2, 3)
        .reshape(STRETCH, HQ * HD)
        .astype(jnp.bfloat16)
    )


def on_device(tokens, qkv_weight, qkv_bias, cache, lengths, slot_stream):
    my_index = lax.axis_index(("tp", "grp"))
    grp_index = lax.axis_index("grp")
    tp_count = lax.axis_size("tp")
    grp_count = lax.axis_size("grp")
    per_device = cache.shape[0]
    local_rows = per_device * STRETCH
    shard_cols = qkv_weight.shape[1]
    weight_cols = lax.all_gather(qkv_weight, "tp", axis=1, tiled=True)
    bias_table = qkv_bias.reshape(tp_count, grp_count, shard_cols)
    bias_cols = (
        lax.dynamic_index_in_dim(bias_table, grp_index, 1, keepdims=False)
        .reshape(-1)
        .astype(jnp.float32)
    )
    partial_cols = jnp.dot(
        lax.all_gather(tokens, "grp", axis=0, tiled=True),
        weight_cols,
        preferred_element_type=jnp.float32,
    )
    rounded_cols = (partial_cols + bias_cols[None, :]).astype(jnp.bfloat16)
    received = lax.all_to_all(rounded_cols, "grp", split_axis=0, concat_axis=1, tiled=True)
    projected_qkv = (
        received.reshape(local_rows, grp_count, tp_count, shard_cols)
        .transpose(0, 2, 1, 3)
        .reshape(local_rows, -1)
    )
    my_slots = my_index * per_device + jnp.arange(per_device, dtype=jnp.int32)
    my_lengths = jnp.take(lengths, jnp.take(slot_stream, my_slots))
    attended = jnp.concatenate(
        [
            attend(
                projected_qkv[slot_index * STRETCH : (slot_index + 1) * STRETCH],
                cache[slot_index],
                my_lengths[slot_index],
            )
            for slot_index in range(per_device)
        ],
        axis=0,
    )
    return attended


MESH = pl.DeviceIdType.MESH
LOG2E = 1.4426950408889634


def fused_kernel(
    n,
    groups,
    cols,
    tokens_ref,
    weight_ref,
    bias_ref,
    cache_ref,
    lengths_ref,
    streams_ref,
    freq_ref,
    out_ref,
    tok,
    weights,
    slots,
    bias,
    outgoing,
    incoming,
    cos_table,
    sin_table,
    tok_local,
    tok_send,
    tok_recv,
    part_send,
    part_recv,
    weight_sems,
    cache_sems,
    relay_sems,
    bias_all,
    partner_in,
):
    tp = lax.axis_index("tp")
    me = lax.axis_index("grp")
    chain = groups // 2
    depth = me // 2
    side = me % 2
    across = depth * 2 + 1 - side
    paired = depth + 1 - 2 * (depth % 2)
    at_end = (depth == 0) | (depth == chain - 1)
    paired_at_end = (paired == 0) | (paired == chain - 1)
    width = tok.shape[3]
    split = width * 11 // 32 // HD * HD
    main = cols - HD // 2
    first_slot = (tp * groups + me) * n

    def local_tokens(c):
        return pltpu.make_async_copy(
            tokens_ref.at[pl.ds(pl.multiple_of(c * STRETCH, STRETCH), STRETCH)],
            tok.at[c, me],
            tok_local.at[c],
        )

    def cache_copy(c):
        return pltpu.make_async_copy(cache_ref.at[c], slots.at[c], cache_sems.at[c])

    def tok_copy(c, block, direction, target):
        return pltpu.make_async_remote_copy(
            src_ref=tok.at[c, block],
            dst_ref=tok.at[c, block],
            send_sem=tok_send.at[c, block, direction],
            recv_sem=tok_recv.at[c, block],
            device_id={"grp": target},
            device_id_type=MESH,
        )

    def rest_copy(c, block):
        part = tok.at[c, block, :, pl.ds(split, width - split)]
        return pltpu.make_async_remote_copy(
            src_ref=part,
            dst_ref=part,
            send_sem=tok_send.at[c, block, 2],
            recv_sem=tok_recv.at[c, block],
            device_id={"grp": across},
            device_id_type=MESH,
        )

    def relay_copy(c, level, size):
        part = tok.at[c, level * 2 + 1 - side, :, pl.ds(0, size)]
        return pltpu.make_async_remote_copy(
            src_ref=part,
            dst_ref=part,
            send_sem=relay_sems.at[c, 0],
            recv_sem=relay_sems.at[c, 1],
            device_id={"grp": paired * 2 + side},
            device_id_type=MESH,
        )

    def part_copy(c, peer):
        return pltpu.make_async_remote_copy(
            src_ref=outgoing.at[c, peer],
            dst_ref=incoming.at[c, me],
            send_sem=part_send.at[c, peer],
            recv_sem=part_recv.at[c, me],
            device_id={"grp": peer},
            device_id_type=MESH,
        )

    def part_arrival(c, peer):
        return pltpu.make_async_remote_copy(
            src_ref=outgoing.at[c, peer],
            dst_ref=incoming.at[c, peer],
            send_sem=part_send.at[c, peer],
            recv_sem=part_recv.at[c, peer],
            device_id={"grp": peer},
            device_id_type=MESH,
        )

    pieces = (
        (HD // 2 * side, main, (main + HD) * tp),
        (main * (1 - side), HD // 2, main + HD // 2 * ((tp + side) % 2)),
    )

    def weight_own(p):
        start, size, at = pieces[p]
        return pltpu.make_async_copy(
            weight_ref.at[pl.ds(pl.multiple_of(start, HD // 2), size)],
            weights.at[pl.ds(pl.multiple_of(at, HD // 2), size)],
            weight_sems.at[p, 0],
        )

    def weight_swap(p):
        start, size, at = pieces[p]
        return pltpu.make_async_remote_copy(
            src_ref=weight_ref.at[pl.ds(pl.multiple_of(start, HD // 2), size)],
            dst_ref=weights.at[pl.ds(pl.multiple_of(at, HD // 2), size)],
            send_sem=weight_sems.at[p, 1],
            recv_sem=weight_sems.at[p, 2],
            device_id={"tp": 1 - tp},
            device_id_type=MESH,
        )

    for c in range(n):
        local_tokens(c).start()

    for p in range(2):
        weight_own(p).start()
    for c in range(n):
        cache_copy(c).start()

    barrier = pltpu.get_barrier_semaphore()

    @pl.when(tp == 0)
    def _():
        pl.semaphore_signal(barrier, inc=1, device_id={"tp": 1 - tp}, device_id_type=MESH)

    for d in range(1, groups):
        pl.semaphore_signal(
            barrier, inc=1, device_id={"grp": lax.rem(me + d, groups)}, device_id_type=MESH
        )
    pl.semaphore_wait(barrier, groups - 1 + tp)

    @pl.when(tp == 1)
    def _():
        pl.semaphore_signal(partner_in, inc=1, device_id={"tp": 1 - tp}, device_id_type=MESH)

    def send_own(c):
        local_tokens(c).wait()
        tok_copy(c, me, 2, across).start()

        @pl.when(depth + 1 < chain)
        def _():
            tok_copy(c, me, 0, me + 2).start()

        @pl.when(depth >= 1)
        def _():
            tok_copy(c, me, 1, me - 2).start()

    def send_across(c, block, shared):
        @pl.when(shared & jnp.logical_not(paired_at_end))
        def _():
            rest_copy(c, block).start()

        @pl.when(jnp.logical_not(shared))
        def _():
            tok_copy(c, block, 2, across).start()

    def relay(c):
        tok_copy(c, across, 2, across).wait_recv()

        @pl.when(at_end)
        def _():
            relay_copy(c, depth, width).start()

        @pl.when(jnp.logical_not(at_end))
        def _():
            relay_copy(c, depth, split).start()

    def forward(c, s):
        @pl.when(depth >= s)
        def _():
            block = me - 2 * s
            tok_copy(c, block, 2, across).wait_recv()
            send_across(c, block, (s == 1) & (depth % 2 == 1))

            @pl.when(depth + 1 < chain)
            def _():
                tok_copy(c, block, 0, me + 2).start()

        @pl.when(depth + s < chain)
        def _():
            block = me + 2 * s
            tok_copy(c, block, 2, across).wait_recv()
            send_across(c, block, (s == 1) & (depth % 2 == 0))

            @pl.when(depth >= 1)
            def _():
                tok_copy(c, block, 1, me - 2).start()

    nt = (((1,), (1,)), ((), ()))

    def finish_sends(c):
        for level in range(chain):
            block = level * 2 + side

            @pl.when((level == paired) & jnp.logical_not(paired_at_end))
            def _():
                rest_copy(c, block).wait_send()

            @pl.when(level != paired)
            def _():
                tok_copy(c, block, 2, across).wait_send()

            @pl.when((level <= depth) & (depth + 1 < chain))
            def _():
                tok_copy(c, block, 0, me + 2).wait_send()

            @pl.when((level >= depth) & (depth >= 1))
            def _():
                tok_copy(c, block, 1, me - 2).wait_send()

        @pl.when(at_end)
        def _():
            relay_copy(c, depth, width).wait_send()

        @pl.when(jnp.logical_not(at_end))
        def _():
            relay_copy(c, depth, split).wait_send()

        for d in range(1, groups):
            part_copy(c, lax.rem(me + d, groups)).wait_send()

    def project(c):
        for level in range(chain):
            block = level * 2 + 1 - side

            @pl.when((level != paired) & (level != depth))
            def _():
                tok_copy(c, block, 2, across).wait_recv()

            @pl.when((level == paired) & paired_at_end)
            def _():
                relay_copy(c, level, width).wait_recv()

            @pl.when((level == paired) & jnp.logical_not(paired_at_end))
            def _():
                rest_copy(c, block).wait_recv()
                relay_copy(c, level, split).wait_recv()

        rows = tok[c].reshape(groups * STRETCH, tok.shape[3])
        product = lax.dot_general(rows, weights[...], nt, preferred_element_type=jnp.float32)
        product = (product + bias[...]).astype(jnp.bfloat16)
        outgoing[c] = product.reshape(groups, STRETCH, 2 * cols)
        for d in range(1, groups):
            part_copy(c, lax.rem(me + d, groups)).start()
        incoming[c, me] = outgoing[c, me]

    lane = lax.broadcasted_iota(jnp.int32, (STRETCH, HD), 1)
    rows_all = STRETCH * GROUP
    pair_heads = 2 * cols // HD
    half = groups // 2 * pair_heads
    middle = pair_heads // 2

    def attention(c):
        for d in range(1, groups):
            part_arrival(c, lax.rem(me + d, groups)).wait_recv()
        cache_copy(c).wait()
        length = lengths_ref[streams_ref[first_slot + c]]
        cosine = cos_table[c]
        sine = sin_table[c]
        key_index = lax.broadcasted_iota(jnp.int32, (1, CAP), 1)
        in_cache = key_index < length
        new_index = lax.broadcasted_iota(jnp.int32, (rows_all, STRETCH), 1)
        new_token = lax.broadcasted_iota(jnp.int32, (rows_all, STRETCH), 0) % STRETCH
        causal = new_index <= new_token
        factor = HD ** (-0.5) * LOG2E

        def head(i):
            t, rest = divmod(i, half)
            pair, k = divmod(rest, pair_heads)
            if k != middle:
                block, at = (2 * pair, k) if k < middle else (2 * pair + 1, k - middle - 1)
                at = at * HD + t * (main + HD)
                return incoming[c, block, :, at : at + HD]
            left = incoming[c, 2 * pair, :, main : main + HD].astype(jnp.float32)
            right = incoming[c, 2 * pair + 1, :, main : main + HD].astype(jnp.float32)
            if t == 0:
                joined = jnp.where(lane < HD // 2, left, right)
            else:
                joined = pltpu.roll(jnp.where(lane < HD // 2, right, left), HD // 2, 1)
            return joined.astype(jnp.bfloat16)

        def rotated(i):
            u = head(i).astype(jnp.float32)
            return (u * cosine + pltpu.roll(u, HD // 2, 1) * sine).astype(jnp.bfloat16)

        for k in range(KVH):
            queries = jnp.concatenate([rotated(k * GROUP + g) for g in range(GROUP)], axis=0)
            new_keys = rotated(HQ + k)
            new_values = head(HQ + KVH + k)
            keys = slots[c, :, k * HD : (k + 1) * HD]
            values = slots[c, :, (KVH + k) * HD : (KVH + k + 1) * HD]
            scores = lax.dot_general(queries, keys, nt, preferred_element_type=jnp.float32)
            scores = jnp.where(in_cache, scores, -jnp.inf)
            new_scores = lax.dot_general(queries, new_keys, nt, preferred_element_type=jnp.float32)
            new_scores = jnp.where(causal, new_scores, -jnp.inf)
            top = jnp.maximum(
                jnp.max(scores, axis=-1, keepdims=True), jnp.max(new_scores, axis=-1, keepdims=True)
            )
            probs = jnp.exp2((scores - top) * factor)
            new_probs = jnp.exp2((new_scores - top) * factor)
            total = jnp.sum(probs, axis=-1, keepdims=True) + jnp.sum(
                new_probs, axis=-1, keepdims=True
            )
            summed = jnp.dot(
                probs.astype(jnp.bfloat16), values, preferred_element_type=jnp.float32
            ) + jnp.dot(
                new_probs.astype(jnp.bfloat16), new_values, preferred_element_type=jnp.float32
            )
            result = (summed / total).astype(jnp.bfloat16)
            for g in range(GROUP):
                h = k * GROUP + g
                out_ref[
                    pl.ds(pl.multiple_of(c * STRETCH, STRETCH), STRETCH), h * HD : (h + 1) * HD
                ] = result[g * STRETCH : (g + 1) * STRETCH]

    send_own(0)

    @pl.when(tp == 1)
    def _():
        for p in range(2):
            weight_swap(p).start()

    for start in range(0, bias_ref.shape[0], 2 * HD):
        piece = bias_ref[start : start + 2 * HD].astype(jnp.float32)
        bias_all[:, start : start + 2 * HD] = piece.reshape(1, 2 * HD)

    first_head = depth * pair_heads

    def bias_heads(start, count):
        at = pl.multiple_of(start * HD, HD)
        return bias_all[:, pl.ds(at, count * HD)]

    for t in range(2):
        whole = bias_heads(t * half + first_head + (middle + 1) * side, middle)
        bias[:, t * (main + HD) : t * (main + HD) + main] = whole
    joint = [bias_heads(t * half + first_head + middle, 1) for t in range(2)]
    front = lax.broadcasted_iota(jnp.int32, (1, HD), 1) // (HD // 2) == side
    bias[:, main : main + HD] = jnp.where(front, joint[0], pltpu.roll(joint[1], HD // 2, 1))

    sign = jnp.where(lane < HD // 2, -1.0, 1.0)
    token = lax.broadcasted_iota(jnp.int32, (STRETCH, HD), 0)
    for c in range(n):
        length = lengths_ref[streams_ref[first_slot + c]]
        angles = (length + token).astype(jnp.float32) * freq_ref[...]
        cos_table[c] = jnp.cos(angles)
        sin_table[c] = jnp.sin(angles) * sign

    @pl.loop(0, n + 3)
    def _(i):
        @pl.when(i < n)
        def _():
            forward(i, 1)

        @pl.when(i + 1 < n)
        def _():
            send_own(i + 1)

        @pl.when((i == 0) & (tp == 0))
        def _():
            pl.semaphore_wait(partner_in, 1)
            for p in range(2):
                weight_swap(p).start()

        @pl.when(((i >= 2) & (i < n)) | ((i > n) & (i >= 3)))
        def _():
            attention(jnp.where(i < n, i - 2, i - 3))

        @pl.when(i < n)
        def _():
            relay(i)
            for s in range(2, chain - 1):
                forward(i, s)

        @pl.when(i == 1)
        def _():
            for p in range(2):
                weight_own(p).wait()
                weight_swap(p).wait()

        @pl.when((i >= 1) & (i < n + 1))
        def _():
            project(i - 1)

        @pl.when(i < n)
        def _():
            forward(i, chain - 1)

    @pl.loop(0, n)
    def _(c):
        finish_sends(c)


def fused(tokens, qkv_weight, qkv_bias, cache, lengths, slot_stream):
    groups = lax.axis_size("grp")
    n = cache.shape[0]
    width, cols = qkv_weight.shape
    frequency = ROPE_THETA ** (-(np.arange(HD // 2) * 2.0) / HD)
    frequency = np.concatenate([frequency, frequency])[None, :].astype(np.float32)
    anywhere = pl.BlockSpec(memory_space=pl.ANY)
    vmem = pl.BlockSpec(memory_space=pltpu.VMEM)
    smem = pl.BlockSpec(memory_space=pltpu.SMEM)
    dma = pltpu.SemaphoreType.DMA
    rows = groups * STRETCH
    attention_ops = 4 * n * KVH * STRETCH * GROUP * CAP * HD
    return pl.pallas_call(
        functools.partial(fused_kernel, n, groups, cols),
        out_shape=pltpu.VMEM((n * STRETCH, HQ * HD), jnp.bfloat16),
        in_specs=[anywhere, anywhere, vmem, anywhere, smem, smem, vmem],
        out_specs=vmem,
        scratch_shapes=[
            pltpu.VMEM((n, groups, STRETCH, width), jnp.bfloat16),
            pltpu.VMEM((2 * cols, width), jnp.bfloat16),
            pltpu.VMEM(cache.shape, jnp.bfloat16),
            pltpu.VMEM((1, 2 * cols), jnp.float32),
            pltpu.VMEM((n, groups, STRETCH, 2 * cols), jnp.bfloat16),
            pltpu.VMEM((n, groups, STRETCH, 2 * cols), jnp.bfloat16),
            pltpu.VMEM((n, STRETCH, HD), jnp.float32),
            pltpu.VMEM((n, STRETCH, HD), jnp.float32),
            dma((n,)),
            dma((n, groups, 3)),
            dma((n, groups)),
            dma((n, groups)),
            dma((n, groups)),
            dma((2, 3)),
            dma((n,)),
            dma((n, 2)),
            pltpu.VMEM((1, qkv_bias.shape[0]), jnp.float32),
            pltpu.SemaphoreType.REGULAR,
        ],
        compiler_params=pltpu.CompilerParams(
            collective_id=0, has_side_effects=True, vmem_limit_bytes=56 * 2**20
        ),
        cost_estimate=pl.CostEstimate(
            flops=4 * n * rows * width * cols + attention_ops,
            bytes_accessed=2 * (cache.size + 2 * qkv_weight.size),
            transcendentals=n * KVH * STRETCH * GROUP * CAP,
        ),
    )(tokens, qkv_weight.T, qkv_bias, cache, lengths, slot_stream, jnp.asarray(frequency))


def solution(mesh):
    def program(tokens, qkv_weight, qkv_bias, cache, lengths, slot_stream):
        cols = qkv_weight.shape[1]
        groups = lax.axis_size("grp")
        fits = lax.axis_size("tp") == 2 and groups % 4 == 0 and cols % HD == HD // 2
        body = fused if fits else on_device
        return body(tokens, qkv_weight, qkv_bias, cache, lengths, slot_stream)

    in_specs = (
        P(("rep", "tp", "grp"), None),
        P(None, ("tp", "grp")),
        P(),
        P(("rep", "tp", "grp"), None, None),
        P("rep"),
        P("rep"),
    )
    out_specs = P(("rep", "tp", "grp"), None)
    return jax.shard_map(
        program, mesh=mesh, in_specs=in_specs, out_specs=out_specs, check_vma=False
    )
```

```python
import functools

import jax
import jax.numpy as jnp
import numpy as np
from jax import lax
from jax.experimental import pallas as pl
from jax.experimental.pallas import tpu as pltpu
from jax.sharding import PartitionSpec as P

HD = 128
HQ = 32
KVH = 4
STRETCH = 16
CAP = 1024
GROUP = 8


ROPE_THETA = 1000000.0


def rotate(vectors, positions):
    half_width = vectors.shape[-1] // 2
    frequency = ROPE_THETA ** (
        -(jnp.arange(half_width, dtype=jnp.float32) * 2.0) / vectors.shape[-1]
    )
    angles = positions.astype(jnp.float32)[:, None] * frequency[None, :]
    cosine = jnp.cos(angles)[:, None, :]
    sine_part = jnp.sin(angles)[:, None, :]
    front_half = vectors[..., :half_width]
    back_half = vectors[..., half_width:]
    return jnp.concatenate(
        [front_half * cosine - back_half * sine_part, back_half * cosine + front_half * sine_part],
        axis=-1,
    )


def attend(token_block, slot_cache, length):
    query_width = HQ * HD
    kv_width = KVH * HD
    positions = length + jnp.arange(STRETCH, dtype=jnp.int32)
    queries = rotate(
        token_block[:, :query_width].astype(jnp.float32).reshape(STRETCH, HQ, HD), positions
    ).astype(jnp.bfloat16)
    new_keys = rotate(
        token_block[:, query_width : query_width + kv_width]
        .astype(jnp.float32)
        .reshape(STRETCH, KVH, HD),
        positions,
    ).astype(jnp.bfloat16)
    new_values = token_block[:, query_width + kv_width :].reshape(STRETCH, KVH, HD)
    grouped = (
        queries.reshape(STRETCH, KVH, GROUP, HD)
        .transpose(1, 0, 2, 3)
        .reshape(KVH, STRETCH * GROUP, HD)
    )
    score_scale = HD ** (-0.5)
    query_token = jnp.arange(STRETCH * GROUP, dtype=jnp.int32) // GROUP
    scores = (
        jnp.einsum("krd,jkd->krj", grouped, new_keys, preferred_element_type=jnp.float32)
        * score_scale
    )
    causal = jnp.arange(STRETCH, dtype=jnp.int32)[None, :] <= query_token[:, None]
    scores = jnp.where(causal[None], scores, -jnp.inf)
    row_max = jnp.max(scores, axis=-1)
    exponent = jnp.exp(scores - row_max[..., None])
    row_total = jnp.sum(exponent, axis=-1)
    running = jnp.einsum(
        "krj,jkd->krd",
        exponent.astype(jnp.bfloat16),
        new_values,
        preferred_element_type=jnp.float32,
    )
    key_span = min(CAP, 256)
    key_part = slot_cache[:, :kv_width]
    value_part = slot_cache[:, kv_width:]

    def visit(block_index, running_state):
        old_max, old_total, old_sum = running_state
        offset = block_index * key_span
        key_block = lax.dynamic_slice_in_dim(key_part, offset, key_span, 0).reshape(
            key_span, KVH, HD
        )
        value_block = lax.dynamic_slice_in_dim(value_part, offset, key_span, 0).reshape(
            key_span, KVH, HD
        )
        block_scores = (
            jnp.einsum("krd,jkd->krj", grouped, key_block, preferred_element_type=jnp.float32)
            * score_scale
        )
        in_cache = offset + jnp.arange(key_span, dtype=jnp.int32) < length
        block_scores = jnp.where(in_cache[None, None, :], block_scores, -jnp.inf)
        new_max = jnp.maximum(old_max, jnp.max(block_scores, axis=-1))
        rescale = jnp.exp(old_max - new_max)
        block_exp = jnp.exp(block_scores - new_max[..., None])
        new_total = old_total * rescale + jnp.sum(block_exp, axis=-1)
        new_sum = old_sum * rescale[..., None] + jnp.einsum(
            "krj,jkd->krd",
            block_exp.astype(jnp.bfloat16),
            value_block,
            preferred_element_type=jnp.float32,
        )
        return (new_max, new_total, new_sum)

    block_count = CAP // key_span
    row_max, row_total, running = lax.fori_loop(
        0, block_count, visit, (row_max, row_total, running)
    )
    result = running / row_total[..., None]
    return (
        result.reshape(KVH, STRETCH, GROUP, HD)
        .transpose(1, 0, 2, 3)
        .reshape(STRETCH, HQ * HD)
        .astype(jnp.bfloat16)
    )


def on_device(tokens, qkv_weight, qkv_bias, cache, lengths, slot_stream):
    my_index = lax.axis_index(("tp", "grp"))
    grp_index = lax.axis_index("grp")
    tp_count = lax.axis_size("tp")
    grp_count = lax.axis_size("grp")
    per_device = cache.shape[0]
    local_rows = per_device * STRETCH
    shard_cols = qkv_weight.shape[1]
    weight_cols = lax.all_gather(qkv_weight, "tp", axis=1, tiled=True)
    bias_table = qkv_bias.reshape(tp_count, grp_count, shard_cols)
    bias_cols = (
        lax.dynamic_index_in_dim(bias_table, grp_index, 1, keepdims=False)
        .reshape(-1)
        .astype(jnp.float32)
    )
    partial_cols = jnp.dot(
        lax.all_gather(tokens, "grp", axis=0, tiled=True),
        weight_cols,
        preferred_element_type=jnp.float32,
    )
    rounded_cols = (partial_cols + bias_cols[None, :]).astype(jnp.bfloat16)
    received = lax.all_to_all(rounded_cols, "grp", split_axis=0, concat_axis=1, tiled=True)
    projected_qkv = (
        received.reshape(local_rows, grp_count, tp_count, shard_cols)
        .transpose(0, 2, 1, 3)
        .reshape(local_rows, -1)
    )
    my_slots = my_index * per_device + jnp.arange(per_device, dtype=jnp.int32)
    my_lengths = jnp.take(lengths, jnp.take(slot_stream, my_slots))
    attended = jnp.concatenate(
        [
            attend(
                projected_qkv[slot_index * STRETCH : (slot_index + 1) * STRETCH],
                cache[slot_index],
                my_lengths[slot_index],
            )
            for slot_index in range(per_device)
        ],
        axis=0,
    )
    return attended


MESH = pl.DeviceIdType.MESH
LOG2E = 1.4426950408889634


def fused_kernel(
    n,
    groups,
    cols,
    tokens_ref,
    weight_ref,
    bias_ref,
    cache_ref,
    lengths_ref,
    streams_ref,
    freq_ref,
    out_ref,
    tok,
    weights,
    slots,
    bias,
    outgoing,
    incoming,
    cos_table,
    sin_table,
    tok_local,
    tok_send,
    tok_recv,
    part_send,
    part_recv,
    weight_sems,
    cache_sems,
    relay_sems,
    bias_all,
    partner_in,
):
    tp = lax.axis_index("tp")
    me = lax.axis_index("grp")
    chain = groups // 2
    depth = me // 2
    side = me % 2
    across = depth * 2 + 1 - side
    paired = depth + 1 - 2 * (depth % 2)
    at_end = (depth == 0) | (depth == chain - 1)
    paired_at_end = (paired == 0) | (paired == chain - 1)
    width = tok.shape[3]
    split = width * 11 // 32 // HD * HD
    main = cols - HD // 2
    first_slot = (tp * groups + me) * n

    def local_tokens(c):
        return pltpu.make_async_copy(
            tokens_ref.at[pl.ds(pl.multiple_of(c * STRETCH, STRETCH), STRETCH)],
            tok.at[c, me],
            tok_local.at[c],
        )

    def cache_copy(c):
        return pltpu.make_async_copy(cache_ref.at[c], slots.at[c], cache_sems.at[c])

    def tok_copy(c, block, direction, target):
        return pltpu.make_async_remote_copy(
            src_ref=tok.at[c, block],
            dst_ref=tok.at[c, block],
            send_sem=tok_send.at[c, block, direction],
            recv_sem=tok_recv.at[c, block],
            device_id={"grp": target},
            device_id_type=MESH,
        )

    def rest_copy(c, block):
        part = tok.at[c, block, :, pl.ds(split, width - split)]
        return pltpu.make_async_remote_copy(
            src_ref=part,
            dst_ref=part,
            send_sem=tok_send.at[c, block, 2],
            recv_sem=tok_recv.at[c, block],
            device_id={"grp": across},
            device_id_type=MESH,
        )

    def relay_copy(c, level, size):
        part = tok.at[c, level * 2 + 1 - side, :, pl.ds(0, size)]
        return pltpu.make_async_remote_copy(
            src_ref=part,
            dst_ref=part,
            send_sem=relay_sems.at[c, 0],
            recv_sem=relay_sems.at[c, 1],
            device_id={"grp": paired * 2 + side},
            device_id_type=MESH,
        )

    def part_copy(c, peer):
        return pltpu.make_async_remote_copy(
            src_ref=outgoing.at[c, peer],
            dst_ref=incoming.at[c, me],
            send_sem=part_send.at[c, peer],
            recv_sem=part_recv.at[c, me],
            device_id={"grp": peer},
            device_id_type=MESH,
        )

    def part_arrival(c, peer):
        return pltpu.make_async_remote_copy(
            src_ref=outgoing.at[c, peer],
            dst_ref=incoming.at[c, peer],
            send_sem=part_send.at[c, peer],
            recv_sem=part_recv.at[c, peer],
            device_id={"grp": peer},
            device_id_type=MESH,
        )

    pieces = (
        (HD // 2 * side, main, (main + HD) * tp),
        (main * (1 - side), HD // 2, main + HD // 2 * ((tp + side) % 2)),
    )

    def weight_own(p):
        start, size, at = pieces[p]
        return pltpu.make_async_copy(
            weight_ref.at[pl.ds(pl.multiple_of(start, HD // 2), size)],
            weights.at[pl.ds(pl.multiple_of(at, HD // 2), size)],
            weight_sems.at[p, 0],
        )

    def weight_swap(p):
        start, size, at = pieces[p]
        return pltpu.make_async_remote_copy(
            src_ref=weight_ref.at[pl.ds(pl.multiple_of(start, HD // 2), size)],
            dst_ref=weights.at[pl.ds(pl.multiple_of(at, HD // 2), size)],
            send_sem=weight_sems.at[p, 1],
            recv_sem=weight_sems.at[p, 2],
            device_id={"tp": 1 - tp},
            device_id_type=MESH,
        )

    for c in range(n):
        local_tokens(c).start()

    for p in range(2):
        weight_own(p).start()
    for c in range(n):
        cache_copy(c).start()

    barrier = pltpu.get_barrier_semaphore()

    @pl.when(tp == 0)
    def _():
        pl.semaphore_signal(barrier, inc=1, device_id={"tp": 1 - tp}, device_id_type=MESH)

    for d in range(1, groups):
        pl.semaphore_signal(
            barrier, inc=1, device_id={"grp": lax.rem(me + d, groups)}, device_id_type=MESH
        )
    pl.semaphore_wait(barrier, groups - 1 + tp)

    @pl.when(tp == 1)
    def _():
        pl.semaphore_signal(partner_in, inc=1, device_id={"tp": 1 - tp}, device_id_type=MESH)

    def send_own(c):
        local_tokens(c).wait()
        tok_copy(c, me, 2, across).start()

        @pl.when(depth + 1 < chain)
        def _():
            tok_copy(c, me, 0, me + 2).start()

        @pl.when(depth >= 1)
        def _():
            tok_copy(c, me, 1, me - 2).start()

    def send_across(c, block, shared):
        @pl.when(shared & jnp.logical_not(paired_at_end))
        def _():
            rest_copy(c, block).start()

        @pl.when(jnp.logical_not(shared))
        def _():
            tok_copy(c, block, 2, across).start()

    def relay(c):
        tok_copy(c, across, 2, across).wait_recv()

        @pl.when(at_end)
        def _():
            relay_copy(c, depth, width).start()

        @pl.when(jnp.logical_not(at_end))
        def _():
            relay_copy(c, depth, split).start()

    def forward(c, s):
        @pl.when(depth >= s)
        def _():
            block = me - 2 * s
            tok_copy(c, block, 2, across).wait_recv()
            send_across(c, block, (s == 1) & (depth % 2 == 1))

            @pl.when(depth + 1 < chain)
            def _():
                tok_copy(c, block, 0, me + 2).start()

        @pl.when(depth + s < chain)
        def _():
            block = me + 2 * s
            tok_copy(c, block, 2, across).wait_recv()
            send_across(c, block, (s == 1) & (depth % 2 == 0))

            @pl.when(depth >= 1)
            def _():
                tok_copy(c, block, 1, me - 2).start()

    nt = (((1,), (1,)), ((), ()))

    def finish_sends(c):
        for level in range(chain):
            block = level * 2 + side

            @pl.when((level == paired) & jnp.logical_not(paired_at_end))
            def _():
                rest_copy(c, block).wait_send()

            @pl.when(level != paired)
            def _():
                tok_copy(c, block, 2, across).wait_send()

            @pl.when((level <= depth) & (depth + 1 < chain))
            def _():
                tok_copy(c, block, 0, me + 2).wait_send()

            @pl.when((level >= depth) & (depth >= 1))
            def _():
                tok_copy(c, block, 1, me - 2).wait_send()

        @pl.when(at_end)
        def _():
            relay_copy(c, depth, width).wait_send()

        @pl.when(jnp.logical_not(at_end))
        def _():
            relay_copy(c, depth, split).wait_send()

        for d in range(1, groups):
            part_copy(c, lax.rem(me + d, groups)).wait_send()

    def project(c):
        for level in range(chain):
            block = level * 2 + 1 - side

            @pl.when((level != paired) & (level != depth))
            def _():
                tok_copy(c, block, 2, across).wait_recv()

            @pl.when((level == paired) & paired_at_end)
            def _():
                relay_copy(c, level, width).wait_recv()

            @pl.when((level == paired) & jnp.logical_not(paired_at_end))
            def _():
                rest_copy(c, block).wait_recv()
                relay_copy(c, level, split).wait_recv()

        rows = tok[c].reshape(groups * STRETCH, tok.shape[3])
        product = lax.dot_general(rows, weights[...], nt, preferred_element_type=jnp.float32)
        product = (product + bias[...]).astype(jnp.bfloat16)
        outgoing[c] = product.reshape(groups, STRETCH, 2 * cols)
        for d in range(1, groups):
            part_copy(c, lax.rem(me + d, groups)).start()
        incoming[c, me] = outgoing[c, me]

    lane = lax.broadcasted_iota(jnp.int32, (STRETCH, HD), 1)
    rows_all = STRETCH * GROUP
    pair_heads = 2 * cols // HD
    half = groups // 2 * pair_heads
    middle = pair_heads // 2

    def arrive(c):
        for d in range(1, groups):
            part_arrival(c, lax.rem(me + d, groups)).wait_recv()
        cache_copy(c).wait()

    def attention(c, key_heads):
        length = lengths_ref[streams_ref[first_slot + c]]
        cosine = cos_table[c]
        sine = sin_table[c]
        key_index = lax.broadcasted_iota(jnp.int32, (1, CAP), 1)
        in_cache = key_index < length
        new_index = lax.broadcasted_iota(jnp.int32, (rows_all, STRETCH), 1)
        new_token = lax.broadcasted_iota(jnp.int32, (rows_all, STRETCH), 0) % STRETCH
        causal = new_index <= new_token
        factor = HD ** (-0.5) * LOG2E

        def head(i):
            t, rest = divmod(i, half)
            pair, k = divmod(rest, pair_heads)
            if k != middle:
                block, at = (2 * pair, k) if k < middle else (2 * pair + 1, k - middle - 1)
                at = at * HD + t * (main + HD)
                return incoming[c, block, :, at : at + HD]
            left = incoming[c, 2 * pair, :, main : main + HD].astype(jnp.float32)
            right = incoming[c, 2 * pair + 1, :, main : main + HD].astype(jnp.float32)
            if t == 0:
                joined = jnp.where(lane < HD // 2, left, right)
            else:
                joined = pltpu.roll(jnp.where(lane < HD // 2, right, left), HD // 2, 1)
            return joined.astype(jnp.bfloat16)

        def rotated(i):
            u = head(i).astype(jnp.float32)
            return (u * cosine + pltpu.roll(u, HD // 2, 1) * sine).astype(jnp.bfloat16)

        for k in key_heads:
            queries = jnp.concatenate([rotated(k * GROUP + g) for g in range(GROUP)], axis=0)
            new_keys = rotated(HQ + k)
            new_values = head(HQ + KVH + k)
            keys = slots[c, :, k * HD : (k + 1) * HD]
            values = slots[c, :, (KVH + k) * HD : (KVH + k + 1) * HD]
            scores = lax.dot_general(queries, keys, nt, preferred_element_type=jnp.float32)
            scores = jnp.where(in_cache, scores, -jnp.inf)
            new_scores = lax.dot_general(queries, new_keys, nt, preferred_element_type=jnp.float32)
            new_scores = jnp.where(causal, new_scores, -jnp.inf)
            top = jnp.maximum(
                jnp.max(scores, axis=-1, keepdims=True), jnp.max(new_scores, axis=-1, keepdims=True)
            )
            probs = jnp.exp2((scores - top) * factor)
            new_probs = jnp.exp2((new_scores - top) * factor)
            total = jnp.sum(probs, axis=-1, keepdims=True) + jnp.sum(
                new_probs, axis=-1, keepdims=True
            )
            summed = jnp.dot(
                probs.astype(jnp.bfloat16), values, preferred_element_type=jnp.float32
            ) + jnp.dot(
                new_probs.astype(jnp.bfloat16), new_values, preferred_element_type=jnp.float32
            )
            result = (summed / total).astype(jnp.bfloat16)
            for g in range(GROUP):
                h = k * GROUP + g
                out_ref[
                    pl.ds(pl.multiple_of(c * STRETCH, STRETCH), STRETCH), h * HD : (h + 1) * HD
                ] = result[g * STRETCH : (g + 1) * STRETCH]

    send_own(0)

    @pl.when(tp == 1)
    def _():
        for p in range(2):
            weight_swap(p).start()

    for start in range(0, bias_ref.shape[0], 2 * HD):
        piece = bias_ref[start : start + 2 * HD].astype(jnp.float32)
        bias_all[:, start : start + 2 * HD] = piece.reshape(1, 2 * HD)

    first_head = depth * pair_heads

    def bias_heads(start, count):
        at = pl.multiple_of(start * HD, HD)
        return bias_all[:, pl.ds(at, count * HD)]

    for t in range(2):
        whole = bias_heads(t * half + first_head + (middle + 1) * side, middle)
        bias[:, t * (main + HD) : t * (main + HD) + main] = whole
    joint = [bias_heads(t * half + first_head + middle, 1) for t in range(2)]
    front = lax.broadcasted_iota(jnp.int32, (1, HD), 1) // (HD // 2) == side
    bias[:, main : main + HD] = jnp.where(front, joint[0], pltpu.roll(joint[1], HD // 2, 1))

    sign = jnp.where(lane < HD // 2, -1.0, 1.0)
    token = lax.broadcasted_iota(jnp.int32, (STRETCH, HD), 0)
    for c in range(n):
        length = lengths_ref[streams_ref[first_slot + c]]
        angles = (length + token).astype(jnp.float32) * freq_ref[...]
        cos_table[c] = jnp.cos(angles)
        sin_table[c] = jnp.sin(angles) * sign

    @pl.loop(0, n + 2)
    def _(i):
        @pl.when(i < n)
        def _():
            forward(i, 1)

        @pl.when(i + 1 < n)
        def _():
            send_own(i + 1)

        @pl.when((i == 0) & (tp == 0))
        def _():
            pl.semaphore_wait(partner_in, 1)
            for p in range(2):
                weight_swap(p).start()

        @pl.when(i >= 2)
        def _():
            arrive(i - 2)
            attention(i - 2, range(KVH // 2))

        @pl.when(i < n)
        def _():
            relay(i)
            for s in range(2, chain - 1):
                forward(i, s)

        @pl.when(i == 1)
        def _():
            for p in range(2):
                weight_own(p).wait()
                weight_swap(p).wait()

        @pl.when((i >= 1) & (i < n + 1))
        def _():
            project(i - 1)

        @pl.when(i < n)
        def _():
            forward(i, chain - 1)

        @pl.when(i >= 2)
        def _():
            attention(i - 2, range(KVH // 2, KVH))

    @pl.loop(0, n)
    def _(c):
        finish_sends(c)


def fused(tokens, qkv_weight, qkv_bias, cache, lengths, slot_stream):
    groups = lax.axis_size("grp")
    n = cache.shape[0]
    width, cols = qkv_weight.shape
    frequency = ROPE_THETA ** (-(np.arange(HD // 2) * 2.0) / HD)
    frequency = np.concatenate([frequency, frequency])[None, :].astype(np.float32)
    anywhere = pl.BlockSpec(memory_space=pl.ANY)
    vmem = pl.BlockSpec(memory_space=pltpu.VMEM)
    smem = pl.BlockSpec(memory_space=pltpu.SMEM)
    dma = pltpu.SemaphoreType.DMA
    rows = groups * STRETCH
    attention_ops = 4 * n * KVH * STRETCH * GROUP * CAP * HD
    return pl.pallas_call(
        functools.partial(fused_kernel, n, groups, cols),
        out_shape=pltpu.VMEM((n * STRETCH, HQ * HD), jnp.bfloat16),
        in_specs=[anywhere, anywhere, vmem, anywhere, smem, smem, vmem],
        out_specs=vmem,
        scratch_shapes=[
            pltpu.VMEM((n, groups, STRETCH, width), jnp.bfloat16),
            pltpu.VMEM((2 * cols, width), jnp.bfloat16),
            pltpu.VMEM(cache.shape, jnp.bfloat16),
            pltpu.VMEM((1, 2 * cols), jnp.float32),
            pltpu.VMEM((n, groups, STRETCH, 2 * cols), jnp.bfloat16),
            pltpu.VMEM((n, groups, STRETCH, 2 * cols), jnp.bfloat16),
            pltpu.VMEM((n, STRETCH, HD), jnp.float32),
            pltpu.VMEM((n, STRETCH, HD), jnp.float32),
            dma((n,)),
            dma((n, groups, 3)),
            dma((n, groups)),
            dma((n, groups)),
            dma((n, groups)),
            dma((2, 3)),
            dma((n,)),
            dma((n, 2)),
            pltpu.VMEM((1, qkv_bias.shape[0]), jnp.float32),
            pltpu.SemaphoreType.REGULAR,
        ],
        compiler_params=pltpu.CompilerParams(
            collective_id=0, has_side_effects=True, vmem_limit_bytes=56 * 2**20
        ),
        cost_estimate=pl.CostEstimate(
            flops=4 * n * rows * width * cols + attention_ops,
            bytes_accessed=2 * (cache.size + 2 * qkv_weight.size),
            transcendentals=n * KVH * STRETCH * GROUP * CAP,
        ),
    )(tokens, qkv_weight.T, qkv_bias, cache, lengths, slot_stream, jnp.asarray(frequency))


def solution(mesh):
    def program(tokens, qkv_weight, qkv_bias, cache, lengths, slot_stream):
        cols = qkv_weight.shape[1]
        groups = lax.axis_size("grp")
        fits = lax.axis_size("tp") == 2 and groups % 4 == 0 and cols % HD == HD // 2
        body = fused if fits else on_device
        return body(tokens, qkv_weight, qkv_bias, cache, lengths, slot_stream)

    in_specs = (
        P(("rep", "tp", "grp"), None),
        P(None, ("tp", "grp")),
        P(),
        P(("rep", "tp", "grp"), None, None),
        P("rep"),
        P("rep"),
    )
    out_specs = P(("rep", "tp", "grp"), None)
    return jax.shard_map(
        program, mesh=mesh, in_specs=in_specs, out_specs=out_specs, check_vma=False
    )
```

```python
import functools

import jax
import jax.numpy as jnp
import numpy as np
from jax import lax
from jax.experimental import pallas as pl
from jax.experimental.pallas import tpu as pltpu
from jax.sharding import PartitionSpec as P

HD = 128
HQ = 32
KVH = 4
STRETCH = 16
CAP = 1024
GROUP = 8


ROPE_THETA = 1000000.0


def rotate(vectors, positions):
    half_width = vectors.shape[-1] // 2
    frequency = ROPE_THETA ** (
        -(jnp.arange(half_width, dtype=jnp.float32) * 2.0) / vectors.shape[-1]
    )
    angles = positions.astype(jnp.float32)[:, None] * frequency[None, :]
    cosine = jnp.cos(angles)[:, None, :]
    sine_part = jnp.sin(angles)[:, None, :]
    front_half = vectors[..., :half_width]
    back_half = vectors[..., half_width:]
    return jnp.concatenate(
        [front_half * cosine - back_half * sine_part, back_half * cosine + front_half * sine_part],
        axis=-1,
    )


def attend(token_block, slot_cache, length):
    query_width = HQ * HD
    kv_width = KVH * HD
    positions = length + jnp.arange(STRETCH, dtype=jnp.int32)
    queries = rotate(
        token_block[:, :query_width].astype(jnp.float32).reshape(STRETCH, HQ, HD), positions
    ).astype(jnp.bfloat16)
    new_keys = rotate(
        token_block[:, query_width : query_width + kv_width]
        .astype(jnp.float32)
        .reshape(STRETCH, KVH, HD),
        positions,
    ).astype(jnp.bfloat16)
    new_values = token_block[:, query_width + kv_width :].reshape(STRETCH, KVH, HD)
    grouped = (
        queries.reshape(STRETCH, KVH, GROUP, HD)
        .transpose(1, 0, 2, 3)
        .reshape(KVH, STRETCH * GROUP, HD)
    )
    score_scale = HD ** (-0.5)
    query_token = jnp.arange(STRETCH * GROUP, dtype=jnp.int32) // GROUP
    scores = (
        jnp.einsum("krd,jkd->krj", grouped, new_keys, preferred_element_type=jnp.float32)
        * score_scale
    )
    causal = jnp.arange(STRETCH, dtype=jnp.int32)[None, :] <= query_token[:, None]
    scores = jnp.where(causal[None], scores, -jnp.inf)
    row_max = jnp.max(scores, axis=-1)
    exponent = jnp.exp(scores - row_max[..., None])
    row_total = jnp.sum(exponent, axis=-1)
    running = jnp.einsum(
        "krj,jkd->krd",
        exponent.astype(jnp.bfloat16),
        new_values,
        preferred_element_type=jnp.float32,
    )
    key_span = min(CAP, 256)
    key_part = slot_cache[:, :kv_width]
    value_part = slot_cache[:, kv_width:]

    def visit(block_index, running_state):
        old_max, old_total, old_sum = running_state
        offset = block_index * key_span
        key_block = lax.dynamic_slice_in_dim(key_part, offset, key_span, 0).reshape(
            key_span, KVH, HD
        )
        value_block = lax.dynamic_slice_in_dim(value_part, offset, key_span, 0).reshape(
            key_span, KVH, HD
        )
        block_scores = (
            jnp.einsum("krd,jkd->krj", grouped, key_block, preferred_element_type=jnp.float32)
            * score_scale
        )
        in_cache = offset + jnp.arange(key_span, dtype=jnp.int32) < length
        block_scores = jnp.where(in_cache[None, None, :], block_scores, -jnp.inf)
        new_max = jnp.maximum(old_max, jnp.max(block_scores, axis=-1))
        rescale = jnp.exp(old_max - new_max)
        block_exp = jnp.exp(block_scores - new_max[..., None])
        new_total = old_total * rescale + jnp.sum(block_exp, axis=-1)
        new_sum = old_sum * rescale[..., None] + jnp.einsum(
            "krj,jkd->krd",
            block_exp.astype(jnp.bfloat16),
            value_block,
            preferred_element_type=jnp.float32,
        )
        return (new_max, new_total, new_sum)

    block_count = CAP // key_span
    row_max, row_total, running = lax.fori_loop(
        0, block_count, visit, (row_max, row_total, running)
    )
    result = running / row_total[..., None]
    return (
        result.reshape(KVH, STRETCH, GROUP, HD)
        .transpose(1, 0, 2, 3)
        .reshape(STRETCH, HQ * HD)
        .astype(jnp.bfloat16)
    )


def on_device(tokens, qkv_weight, qkv_bias, cache, lengths, slot_stream):
    my_index = lax.axis_index(("tp", "grp"))
    grp_index = lax.axis_index("grp")
    tp_count = lax.axis_size("tp")
    grp_count = lax.axis_size("grp")
    per_device = cache.shape[0]
    local_rows = per_device * STRETCH
    shard_cols = qkv_weight.shape[1]
    weight_cols = lax.all_gather(qkv_weight, "tp", axis=1, tiled=True)
    bias_table = qkv_bias.reshape(tp_count, grp_count, shard_cols)
    bias_cols = (
        lax.dynamic_index_in_dim(bias_table, grp_index, 1, keepdims=False)
        .reshape(-1)
        .astype(jnp.float32)
    )
    partial_cols = jnp.dot(
        lax.all_gather(tokens, "grp", axis=0, tiled=True),
        weight_cols,
        preferred_element_type=jnp.float32,
    )
    rounded_cols = (partial_cols + bias_cols[None, :]).astype(jnp.bfloat16)
    received = lax.all_to_all(rounded_cols, "grp", split_axis=0, concat_axis=1, tiled=True)
    projected_qkv = (
        received.reshape(local_rows, grp_count, tp_count, shard_cols)
        .transpose(0, 2, 1, 3)
        .reshape(local_rows, -1)
    )
    my_slots = my_index * per_device + jnp.arange(per_device, dtype=jnp.int32)
    my_lengths = jnp.take(lengths, jnp.take(slot_stream, my_slots))
    attended = jnp.concatenate(
        [
            attend(
                projected_qkv[slot_index * STRETCH : (slot_index + 1) * STRETCH],
                cache[slot_index],
                my_lengths[slot_index],
            )
            for slot_index in range(per_device)
        ],
        axis=0,
    )
    return attended


MESH = pl.DeviceIdType.MESH
LOG2E = 1.4426950408889634


def fused_kernel(
    n,
    groups,
    cols,
    tokens_ref,
    weight_ref,
    bias_ref,
    cache_ref,
    lengths_ref,
    streams_ref,
    freq_ref,
    out_ref,
    tok,
    weights,
    slots,
    bias,
    outgoing,
    incoming,
    cos_table,
    sin_table,
    tok_local,
    tok_send,
    tok_recv,
    part_send,
    part_recv,
    weight_sems,
    cache_sems,
    relay_sems,
    bias_all,
    partner_in,
):
    tp = lax.axis_index("tp")
    me = lax.axis_index("grp")
    chain = groups // 2
    depth = me // 2
    side = me % 2
    across = depth * 2 + 1 - side
    paired = depth + 1 - 2 * (depth % 2)
    at_end = (depth == 0) | (depth == chain - 1)
    paired_at_end = (paired == 0) | (paired == chain - 1)
    width = tok.shape[3]
    split = width * 11 // 32 // HD * HD
    main = cols - HD // 2
    first_slot = (tp * groups + me) * n

    def local_tokens(c):
        return pltpu.make_async_copy(
            tokens_ref.at[pl.ds(pl.multiple_of(c * STRETCH, STRETCH), STRETCH)],
            tok.at[c, me],
            tok_local.at[c],
        )

    def cache_copy(c):
        return pltpu.make_async_copy(cache_ref.at[c], slots.at[c], cache_sems.at[c])

    def tok_copy(c, block, direction, target):
        return pltpu.make_async_remote_copy(
            src_ref=tok.at[c, block],
            dst_ref=tok.at[c, block],
            send_sem=tok_send.at[c, block, direction],
            recv_sem=tok_recv.at[c, block],
            device_id={"grp": target},
            device_id_type=MESH,
        )

    def rest_copy(c, block):
        part = tok.at[c, block, :, pl.ds(split, width - split)]
        return pltpu.make_async_remote_copy(
            src_ref=part,
            dst_ref=part,
            send_sem=tok_send.at[c, block, 2],
            recv_sem=tok_recv.at[c, block],
            device_id={"grp": across},
            device_id_type=MESH,
        )

    def relay_copy(c, level, size):
        part = tok.at[c, level * 2 + 1 - side, :, pl.ds(0, size)]
        return pltpu.make_async_remote_copy(
            src_ref=part,
            dst_ref=part,
            send_sem=relay_sems.at[c, 0],
            recv_sem=relay_sems.at[c, 1],
            device_id={"grp": paired * 2 + side},
            device_id_type=MESH,
        )

    def part_copy(c, peer):
        return pltpu.make_async_remote_copy(
            src_ref=outgoing.at[c, peer],
            dst_ref=incoming.at[c, me],
            send_sem=part_send.at[c, peer],
            recv_sem=part_recv.at[c, me],
            device_id={"grp": peer},
            device_id_type=MESH,
        )

    def part_arrival(c, peer):
        return pltpu.make_async_remote_copy(
            src_ref=outgoing.at[c, peer],
            dst_ref=incoming.at[c, peer],
            send_sem=part_send.at[c, peer],
            recv_sem=part_recv.at[c, peer],
            device_id={"grp": peer},
            device_id_type=MESH,
        )

    pieces = (
        (HD // 2 * side, main, (main + HD) * tp),
        (main * (1 - side), HD // 2, main + HD // 2 * ((tp + side) % 2)),
    )

    def weight_own(p):
        start, size, at = pieces[p]
        return pltpu.make_async_copy(
            weight_ref.at[pl.ds(pl.multiple_of(start, HD // 2), size)],
            weights.at[pl.ds(pl.multiple_of(at, HD // 2), size)],
            weight_sems.at[p, 0],
        )

    def weight_swap(p):
        start, size, at = pieces[p]
        return pltpu.make_async_remote_copy(
            src_ref=weight_ref.at[pl.ds(pl.multiple_of(start, HD // 2), size)],
            dst_ref=weights.at[pl.ds(pl.multiple_of(at, HD // 2), size)],
            send_sem=weight_sems.at[p, 1],
            recv_sem=weight_sems.at[p, 2],
            device_id={"tp": 1 - tp},
            device_id_type=MESH,
        )

    for c in range(n):
        local_tokens(c).start()

    for p in range(2):
        weight_own(p).start()
    for c in range(n):
        cache_copy(c).start()

    barrier = pltpu.get_barrier_semaphore()

    @pl.when(tp == 0)
    def _():
        pl.semaphore_signal(barrier, inc=1, device_id={"tp": 1 - tp}, device_id_type=MESH)

    for d in range(1, groups):
        pl.semaphore_signal(
            barrier, inc=1, device_id={"grp": lax.rem(me + d, groups)}, device_id_type=MESH
        )
    pl.semaphore_wait(barrier, groups - 1 + tp)

    @pl.when(tp == 1)
    def _():
        pl.semaphore_signal(partner_in, inc=1, device_id={"tp": 1 - tp}, device_id_type=MESH)

    def send_own(c):
        local_tokens(c).wait()
        tok_copy(c, me, 2, across).start()

        @pl.when(depth + 1 < chain)
        def _():
            tok_copy(c, me, 0, me + 2).start()

        @pl.when(depth >= 1)
        def _():
            tok_copy(c, me, 1, me - 2).start()

    def send_across(c, block, shared):
        @pl.when(shared & jnp.logical_not(paired_at_end))
        def _():
            rest_copy(c, block).start()

        @pl.when(jnp.logical_not(shared))
        def _():
            tok_copy(c, block, 2, across).start()

    def relay(c):
        tok_copy(c, across, 2, across).wait_recv()

        @pl.when(at_end)
        def _():
            relay_copy(c, depth, width).start()

        @pl.when(jnp.logical_not(at_end))
        def _():
            relay_copy(c, depth, split).start()

    def forward(c, s):
        @pl.when(depth >= s)
        def _():
            block = me - 2 * s
            tok_copy(c, block, 2, across).wait_recv()
            send_across(c, block, (s == 1) & (depth % 2 == 1))

            @pl.when(depth + 1 < chain)
            def _():
                tok_copy(c, block, 0, me + 2).start()

        @pl.when(depth + s < chain)
        def _():
            block = me + 2 * s
            tok_copy(c, block, 2, across).wait_recv()
            send_across(c, block, (s == 1) & (depth % 2 == 0))

            @pl.when(depth >= 1)
            def _():
                tok_copy(c, block, 1, me - 2).start()

    nt = (((1,), (1,)), ((), ()))

    def finish_sends(c):
        for level in range(chain):
            block = level * 2 + side

            @pl.when((level == paired) & jnp.logical_not(paired_at_end))
            def _():
                rest_copy(c, block).wait_send()

            @pl.when(level != paired)
            def _():
                tok_copy(c, block, 2, across).wait_send()

            @pl.when((level <= depth) & (depth + 1 < chain))
            def _():
                tok_copy(c, block, 0, me + 2).wait_send()

            @pl.when((level >= depth) & (depth >= 1))
            def _():
                tok_copy(c, block, 1, me - 2).wait_send()

        @pl.when(at_end)
        def _():
            relay_copy(c, depth, width).wait_send()

        @pl.when(jnp.logical_not(at_end))
        def _():
            relay_copy(c, depth, split).wait_send()

        for d in range(1, groups):
            part_copy(c, lax.rem(me + d, groups)).wait_send()

    def project(c):
        for level in range(chain):
            block = level * 2 + 1 - side

            @pl.when((level != paired) & (level != depth))
            def _():
                tok_copy(c, block, 2, across).wait_recv()

            @pl.when((level == paired) & paired_at_end)
            def _():
                relay_copy(c, level, width).wait_recv()

            @pl.when((level == paired) & jnp.logical_not(paired_at_end))
            def _():
                rest_copy(c, block).wait_recv()
                relay_copy(c, level, split).wait_recv()

        rows = tok[c].reshape(groups * STRETCH, tok.shape[3])
        product = lax.dot_general(rows, weights[...], nt, preferred_element_type=jnp.float32)
        product = (product + bias[...]).astype(jnp.bfloat16)
        outgoing[c] = product.reshape(groups, STRETCH, 2 * cols)
        for d in range(1, groups):
            part_copy(c, lax.rem(me + d, groups)).start()
        incoming[c, me] = outgoing[c, me]

    lane = lax.broadcasted_iota(jnp.int32, (STRETCH, HD), 1)
    rows_all = STRETCH * GROUP
    pair_heads = 2 * cols // HD
    half = groups // 2 * pair_heads
    middle = pair_heads // 2

    def attention(c):
        for d in range(1, groups):
            part_arrival(c, lax.rem(me + d, groups)).wait_recv()
        cache_copy(c).wait()
        length = lengths_ref[streams_ref[first_slot + c]]
        cosine = cos_table[c]
        sine = sin_table[c]
        key_index = lax.broadcasted_iota(jnp.int32, (1, CAP), 1)
        in_cache = key_index < length
        new_index = lax.broadcasted_iota(jnp.int32, (rows_all, STRETCH), 1)
        new_token = lax.broadcasted_iota(jnp.int32, (rows_all, STRETCH), 0) % STRETCH
        causal = new_index <= new_token
        factor = HD ** (-0.5) * LOG2E

        def head(i):
            t, rest = divmod(i, half)
            pair, k = divmod(rest, pair_heads)
            if k != middle:
                block, at = (2 * pair, k) if k < middle else (2 * pair + 1, k - middle - 1)
                at = at * HD + t * (main + HD)
                return incoming[c, block, :, at : at + HD]
            left = incoming[c, 2 * pair, :, main : main + HD].astype(jnp.float32)
            right = incoming[c, 2 * pair + 1, :, main : main + HD].astype(jnp.float32)
            if t == 0:
                joined = jnp.where(lane < HD // 2, left, right)
            else:
                joined = pltpu.roll(jnp.where(lane < HD // 2, right, left), HD // 2, 1)
            return joined.astype(jnp.bfloat16)

        def rotated(i):
            u = head(i).astype(jnp.float32)
            return (u * cosine + pltpu.roll(u, HD // 2, 1) * sine).astype(jnp.bfloat16)

        for k in range(KVH):
            queries = jnp.concatenate([rotated(k * GROUP + g) for g in range(GROUP)], axis=0)
            new_keys = rotated(HQ + k)
            new_values = head(HQ + KVH + k)
            keys = slots[c, :, k * HD : (k + 1) * HD]
            values = slots[c, :, (KVH + k) * HD : (KVH + k + 1) * HD]
            scores = lax.dot_general(queries, keys, nt, preferred_element_type=jnp.float32)
            scores = jnp.where(in_cache, scores, -jnp.inf)
            new_scores = lax.dot_general(queries, new_keys, nt, preferred_element_type=jnp.float32)
            new_scores = jnp.where(causal, new_scores, -jnp.inf)
            top = jnp.maximum(
                jnp.max(scores, axis=-1, keepdims=True), jnp.max(new_scores, axis=-1, keepdims=True)
            )
            probs = jnp.exp2((scores - top) * factor)
            new_probs = jnp.exp2((new_scores - top) * factor)
            total = jnp.sum(probs, axis=-1, keepdims=True) + jnp.sum(
                new_probs, axis=-1, keepdims=True
            )
            summed = jnp.dot(
                probs.astype(jnp.bfloat16), values, preferred_element_type=jnp.float32
            ) + jnp.dot(
                new_probs.astype(jnp.bfloat16), new_values, preferred_element_type=jnp.float32
            )
            result = (summed / total).astype(jnp.bfloat16)
            for g in range(GROUP):
                h = k * GROUP + g
                out_ref[
                    pl.ds(pl.multiple_of(c * STRETCH, STRETCH), STRETCH), h * HD : (h + 1) * HD
                ] = result[g * STRETCH : (g + 1) * STRETCH]

    ahead = 2 - tp
    send_own(0)
    if n > 1:

        @pl.when(tp == 0)
        def _():
            send_own(1)


    @pl.when(tp == 1)
    def _():
        for p in range(2):
            weight_swap(p).start()

    for start in range(0, bias_ref.shape[0], 2 * HD):
        piece = bias_ref[start : start + 2 * HD].astype(jnp.float32)
        bias_all[:, start : start + 2 * HD] = piece.reshape(1, 2 * HD)

    first_head = depth * pair_heads

    def bias_heads(start, count):
        at = pl.multiple_of(start * HD, HD)
        return bias_all[:, pl.ds(at, count * HD)]

    for t in range(2):
        whole = bias_heads(t * half + first_head + (middle + 1) * side, middle)
        bias[:, t * (main + HD) : t * (main + HD) + main] = whole
    joint = [bias_heads(t * half + first_head + middle, 1) for t in range(2)]
    front = lax.broadcasted_iota(jnp.int32, (1, HD), 1) // (HD // 2) == side
    bias[:, main : main + HD] = jnp.where(front, joint[0], pltpu.roll(joint[1], HD // 2, 1))

    sign = jnp.where(lane < HD // 2, -1.0, 1.0)
    token = lax.broadcasted_iota(jnp.int32, (STRETCH, HD), 0)
    for c in range(n):
        length = lengths_ref[streams_ref[first_slot + c]]
        angles = (length + token).astype(jnp.float32) * freq_ref[...]
        cos_table[c] = jnp.cos(angles)
        sin_table[c] = jnp.sin(angles) * sign

    @pl.loop(0, n + 3)
    def _(i):
        @pl.when(i < n)
        def _():
            forward(i, 1)

        @pl.when(i + ahead < n)
        def _():
            send_own(i + ahead)

        @pl.when((i == 0) & (tp == 0))
        def _():
            pl.semaphore_wait(partner_in, 1)
            for p in range(2):
                weight_swap(p).start()

        @pl.when(((i >= 2) & (i < n)) | ((i > n) & (i >= 3)))
        def _():
            attention(jnp.where(i < n, i - 2, i - 3))

        @pl.when(i < n)
        def _():
            relay(i)
            for s in range(2, chain - 1):
                forward(i, s)

        @pl.when(i == 1)
        def _():
            for p in range(2):
                weight_own(p).wait()
                weight_swap(p).wait()

        @pl.when((i >= 1) & (i < n + 1))
        def _():
            project(i - 1)

        @pl.when(i < n)
        def _():
            forward(i, chain - 1)

    @pl.loop(0, n)
    def _(c):
        finish_sends(c)


def fused(tokens, qkv_weight, qkv_bias, cache, lengths, slot_stream):
    groups = lax.axis_size("grp")
    n = cache.shape[0]
    width, cols = qkv_weight.shape
    frequency = ROPE_THETA ** (-(np.arange(HD // 2) * 2.0) / HD)
    frequency = np.concatenate([frequency, frequency])[None, :].astype(np.float32)
    anywhere = pl.BlockSpec(memory_space=pl.ANY)
    vmem = pl.BlockSpec(memory_space=pltpu.VMEM)
    smem = pl.BlockSpec(memory_space=pltpu.SMEM)
    dma = pltpu.SemaphoreType.DMA
    rows = groups * STRETCH
    attention_ops = 4 * n * KVH * STRETCH * GROUP * CAP * HD
    return pl.pallas_call(
        functools.partial(fused_kernel, n, groups, cols),
        out_shape=pltpu.VMEM((n * STRETCH, HQ * HD), jnp.bfloat16),
        in_specs=[anywhere, anywhere, vmem, anywhere, smem, smem, vmem],
        out_specs=vmem,
        scratch_shapes=[
            pltpu.VMEM((n, groups, STRETCH, width), jnp.bfloat16),
            pltpu.VMEM((2 * cols, width), jnp.bfloat16),
            pltpu.VMEM(cache.shape, jnp.bfloat16),
            pltpu.VMEM((1, 2 * cols), jnp.float32),
            pltpu.VMEM((n, groups, STRETCH, 2 * cols), jnp.bfloat16),
            pltpu.VMEM((n, groups, STRETCH, 2 * cols), jnp.bfloat16),
            pltpu.VMEM((n, STRETCH, HD), jnp.float32),
            pltpu.VMEM((n, STRETCH, HD), jnp.float32),
            dma((n,)),
            dma((n, groups, 3)),
            dma((n, groups)),
            dma((n, groups)),
            dma((n, groups)),
            dma((2, 3)),
            dma((n,)),
            dma((n, 2)),
            pltpu.VMEM((1, qkv_bias.shape[0]), jnp.float32),
            pltpu.SemaphoreType.REGULAR,
        ],
        compiler_params=pltpu.CompilerParams(
            collective_id=0, has_side_effects=True, vmem_limit_bytes=56 * 2**20
        ),
        cost_estimate=pl.CostEstimate(
            flops=4 * n * rows * width * cols + attention_ops,
            bytes_accessed=2 * (cache.size + 2 * qkv_weight.size),
            transcendentals=n * KVH * STRETCH * GROUP * CAP,
        ),
    )(tokens, qkv_weight.T, qkv_bias, cache, lengths, slot_stream, jnp.asarray(frequency))


def solution(mesh):
    def program(tokens, qkv_weight, qkv_bias, cache, lengths, slot_stream):
        cols = qkv_weight.shape[1]
        groups = lax.axis_size("grp")
        fits = lax.axis_size("tp") == 2 and groups % 4 == 0 and cols % HD == HD // 2
        body = fused if fits else on_device
        return body(tokens, qkv_weight, qkv_bias, cache, lengths, slot_stream)

    in_specs = (
        P(("rep", "tp", "grp"), None),
        P(None, ("tp", "grp")),
        P(),
        P(("rep", "tp", "grp"), None, None),
        P("rep"),
        P("rep"),
    )
    out_specs = P(("rep", "tp", "grp"), None)
    return jax.shard_map(
        program, mesh=mesh, in_specs=in_specs, out_specs=out_specs, check_vma=False
    )
```
